32 devices in a mesh: dp: 4 (over y, x), seq: 8 (over z, core).
Axes of the slice: x: 2, y: 2, z: 4, core: 2. Of those that a mesh axis runs over, the one named last changes fastest.
Arguments:
- tokens: bfloat16 [2, 4096, 1088], P(None, ('dp', 'seq')), may hold values from -6 to 6
- cotangent: bfloat16 [2, 4096, 1088], P(None, ('dp', 'seq')), may hold values from -6 to 6
- w_qkv: bfloat16 [1088, 3264], P('dp', 'seq'), may hold values from -0.1875 to 0.1875
- w_out: bfloat16 [1088, 1088], P('dp', 'seq'), may hold values from -1.5 to 1.5
- w_up: bfloat16 [1088, 4352], P('dp', 'seq'), may hold values from -0.1875 to 0.1875
- w_down: bfloat16 [4352, 1088], P('dp', 'seq'), may hold values from -0.09375 to 0.09375
- gain_one: bfloat16 [1088], P('dp'), may hold values from 0.25 to 1.75
- bias_one: bfloat16 [1088], P('dp'), may hold values from -3 to 3
- gain_two: bfloat16 [1088], P('dp'), may hold values from 0.25 to 1.75
- bias_two: bfloat16 [1088], P('dp'), may hold values from -3 to 3
- lengths: int32 [2, 4, 8], P(None, 'dp'), may hold values from 1 to 896, 1024 in all within a row
- slot_order: int32 [2, 4, 8], P(None, 'dp'), may hold values from 0 to 7, each once within a row
Outputs:
- block_out: bfloat16 [2, 4096, 1088], P(None, ('dp', 'seq'))
- grad_input: bfloat16 [2, 4096, 1088], P(None, ('dp', 'seq'))
- grad_qkv: float32 [1088, 3264], P('dp', 'seq')
- grad_proj: float32 [1088, 1088], P('dp', 'seq')
- grad_up: float32 [1088, 4352], P('dp', 'seq')
- grad_down: float32 [4352, 1088], P('dp', 'seq')
- grad_gain_one: float32 [1088], P('dp')
- grad_bias_one: float32 [1088], P('dp')
- grad_gain_two: float32 [1088], P('dp')
- grad_bias_two: float32 [1088], P('dp')
The draws below stay inside these ranges and needn't reach their ends.
Inputs may be any that keep to these rules, and one draw needn't show every extreme that they name: For each micro-batch and group the 8 lengths sum to 1024; the largest is exactly 896. `slot_order`: each row over the last dimension holds every number below 8 once.
All inputs are finite; a program needn't handle non-finite values.
Results may differ from the reference program's by a relative error of at most 0.02.
Values may be sent and summed in bfloat16 or wider, within the bound.
A program may use at most 192 MiB of HBM per device.

```python
import math
import jax
import jax.numpy as jnp
import numpy as np
from jax import lax

D = 1088
HEADS = 17
HEAD_DIM = 64
FF = 4352
TOK_DEV = 128
MICRO = 2
DOCS = 8
TOK_GROUP = 1024
TOKENS = 4096
MOST = 896
N_DP = 4
N_SEQ = 8


def block_scale(own_key, extent, shards, least, largest):
    level = 1.0
    for axis_at, shards_of in shards:
        steps = jax.random.uniform(jax.random.fold_in(jax.random.fold_in(own_key, 6), axis_at), (shards_of,), jnp.float32, least / len(shards), largest / len(shards))
        level = level * jnp.repeat(jnp.exp(steps), extent[axis_at] // shards_of).reshape((-1,) + (1,) * (len(extent) - 1 - axis_at))
    return level


def split_up(number_of, total, bound, lean):
    weights = [(1 << 20) // math.isqrt(grade ** lean) + 1 for grade in range(2, number_of + 1)]
    surplus, given = total - bound - (number_of - 1), [1] * (number_of - 1)
    while surplus > 0:
        movable = [i for i in range(number_of - 1) if given[i] < bound]
        whole, left = sum([weights[i] for i in movable]), surplus
        for i in movable:
            more = min(bound - given[i], max(1, left * weights[i] // whole), surplus)
            given[i] = given[i] + more
            surplus = surplus - more
    return np.array([bound] + given)


def uneven(key, number_of, total, limit, skew):
    if number_of == 2:
        one = jax.random.randint(key, (), max(1, total - limit), min(limit, total - 1) + 1)
        return jnp.stack([one, total - one])
    tallies = jnp.asarray(split_up(number_of, total, limit, skew), jnp.int32)
    couples = (number_of - 1) // 2
    source_of, taker = tallies[1:1 + 2 * couples:2], tallies[2:2 + 2 * couples:2]
    slack = jnp.minimum(source_of - 1, limit - taker)
    passed = jax.random.randint(jax.random.fold_in(key, 1), (couples,), 0, 1 << 20) % (slack + 1)
    tallies = tallies.at[1:1 + 2 * couples:2].set(source_of - passed).at[2:2 + 2 * couples:2].set(taker + passed)
    return tallies[jax.random.permutation(jax.random.fold_in(key, 2), number_of)]


def normal_values(rng, extent, width, reach, cuts=(), kind=jnp.bfloat16):
    level = block_scale(rng, extent, cuts, -0.22, 0.18) if cuts else 1.0
    values = jax.random.normal(rng, extent, jnp.float32) * width * level
    return jnp.minimum(jnp.maximum(values, -reach), reach).astype(kind)


def setup_inputs(seed: int = 0) -> dict:
    key_list = jax.random.split(jax.random.key(seed), 13)
    return {
        "tokens": normal_values(key_list[0], (MICRO, TOKENS, D), 1.0, 6.0, ((1, 32),)),
        "cotangent": normal_values(key_list[1], (MICRO, TOKENS, D), 1.0, 6.0, ((1, 32),)),
        "w_qkv": normal_values(key_list[2], (D, 3 * D), D ** -0.5, 0.1875, ((0, 4), (1, 8))),
        "w_out": normal_values(key_list[3], (D, D), (max(D // 64, 1)) ** -0.5, 1.5, ((0, 4), (1, 8))),
        "w_up": normal_values(key_list[4], (D, FF), D ** -0.5, 0.1875, ((0, 4), (1, 8))),
        "w_down": normal_values(key_list[5], (FF, D), FF ** -0.5, 0.09375, ((0, 4), (1, 8))),
        "gain_one": jnp.clip(1.0 + 0.15 * jax.random.normal(key_list[6], (D,), jnp.float32), 0.25, 1.75).astype(jnp.bfloat16),
        "bias_one": normal_values(key_list[7], (D,), 0.5, 3.0, ((0, 4),)),
        "gain_two": jnp.clip(1.0 + 0.15 * jax.random.normal(key_list[8], (D,), jnp.float32), 0.25, 1.75).astype(jnp.bfloat16),
        "bias_two": normal_values(key_list[9], (D,), 0.5, 3.0, ((0, 4),)),
        "lengths": jax.vmap(lambda own: uneven(own, DOCS, TOK_GROUP, MOST, 2))(jax.random.split(key_list[10], MICRO * N_DP)).reshape((MICRO, N_DP, DOCS)).astype(jnp.int32),
        "slot_order": jax.vmap(lambda own: jax.random.permutation(own, N_SEQ))(jax.random.split(key_list[11], MICRO * N_DP)).reshape((MICRO, N_DP, N_SEQ)).astype(jnp.int32),
    }


@jax.custom_vjp
def low(v):
    return lax.optimization_barrier(v.astype(jnp.bfloat16)).astype(jnp.float32)

@jax.custom_vjp
def low_back(v):
    return v

def low_keep(v):
    return (low(v), None)

def low_pass(kept, grad):
    return (grad,)

def back_keep(v):
    return (v, None)

def back_low(kept, grad):
    return (low(grad),)
low.defvjp(low_keep, low_pass)
low_back.defvjp(back_keep, back_low)
EPS = 1e-05
NEG = -1e+30
GELU_C = 0.7978845608028654

def matmul_high(left_side, right_side):
    return jnp.dot(left_side, right_side, precision=lax.Precision.HIGHEST, preferred_element_type=jnp.float32)

def layer_norm(residual, gain_row, offset):
    row_mean = lax.optimization_barrier(jnp.mean(residual, -1, keepdims=True))
    centered = residual - row_mean
    variance = lax.optimization_barrier(jnp.mean(centered * centered, -1, keepdims=True))
    return centered * lax.rsqrt(variance + EPS) * gain_row + offset

def gelu_tanh(values):
    return 0.5 * values * (1.0 + jnp.tanh(GELU_C * (values + 0.044715 * values * values * values)))

def attend_block(queries, q_place, q_segment, key_all, value_all, k_place, k_segment):
    scores = jnp.einsum('qhd,khd->hqk', queries, key_all, precision=lax.Precision.HIGHEST) * HEAD_DIM ** (-0.5)
    allowed = (q_segment[:, None] == k_segment[None, :]) & (k_place[None, :] <= q_place[:, None])
    scores = low_back(jnp.where(allowed[None], scores, NEG))
    probabilities = jax.nn.softmax(scores, axis=-1)
    return jnp.einsum('hqk,khd->qhd', low(probabilities), value_all, precision=lax.Precision.HIGHEST)

def group_layer(residual, places, segments, params):
    w_qkv, w_out, w_up, w_down, gain_one, bias_one, gain_two, bias_two = params
    normed = low(layer_norm(residual, gain_one, bias_one))
    qkv_all = low(low_back(matmul_high(normed, w_qkv)))
    queries = qkv_all[:, :D].reshape(TOK_GROUP, HEADS, HEAD_DIM)
    key_all = qkv_all[:, D:2 * D].reshape(TOK_GROUP, HEADS, HEAD_DIM)
    value_all = qkv_all[:, 2 * D:].reshape(TOK_GROUP, HEADS, HEAD_DIM)
    checked = jax.checkpoint(attend_block)

    def per_block(block_item):
        return checked(block_item[0], block_item[1], block_item[2], key_all, value_all, places, segments)
    attended = lax.map(per_block, (queries.reshape(N_SEQ, TOK_DEV, HEADS, HEAD_DIM), places.reshape(N_SEQ, TOK_DEV), segments.reshape(N_SEQ, TOK_DEV)))
    attended = low(low_back(attended.reshape(TOK_GROUP, D)))
    middle = residual + low_back(matmul_high(attended, w_out))
    normed_two = low(layer_norm(middle, gain_two, bias_two))
    hidden = low_back(matmul_high(normed_two, w_up))
    activated = low(gelu_tanh(hidden))
    return middle + matmul_high(activated, w_down)

def reference(tokens, cotangent, w_qkv, w_out, w_up, w_down, gain_one, bias_one, gain_two, bias_two, lengths, slot_order):
    groups = MICRO * N_DP
    resid_all = tokens.astype(jnp.float32).reshape(groups, TOK_GROUP, D)
    order_rows = slot_order.reshape(groups, N_SEQ).astype(jnp.int32)
    places = order_rows[:, :, None] * TOK_DEV + jnp.arange(TOK_DEV, dtype=jnp.int32)[None, None, :]
    places = places.reshape(groups, TOK_GROUP).astype(jnp.int32)
    doc_ends = jnp.cumsum(lengths.reshape(groups, DOCS), axis=-1).astype(jnp.int32)
    segments = lax.optimization_barrier(jnp.sum((places[:, :, None] >= doc_ends[:, None, :]).astype(jnp.int32), axis=-1)).astype(jnp.int32)
    params = (w_qkv.astype(jnp.float32), w_out.astype(jnp.float32), w_up.astype(jnp.float32), w_down.astype(jnp.float32), gain_one.astype(jnp.float32), bias_one.astype(jnp.float32), gain_two.astype(jnp.float32), bias_two.astype(jnp.float32))

    def forward(resid_all, params):

        def per_group(group_item):
            return group_layer(group_item[0], group_item[1], group_item[2], params)
        return lax.map(per_group, (resid_all, places, segments))
    outputs, pullback = jax.vjp(forward, resid_all, params)
    grad_resid, grad_params = pullback(cotangent.astype(jnp.float32).reshape(groups, TOK_GROUP, D))
    return (outputs.astype(jnp.bfloat16).reshape(MICRO, TOKENS, D), grad_resid.astype(jnp.bfloat16).reshape(MICRO, TOKENS, D), grad_params[0], grad_params[1], grad_params[2], grad_params[3], grad_params[4], grad_params[5], grad_params[6], grad_params[7])
```

```python
import functools

import jax
import jax.numpy as jnp
from jax import lax
from jax.experimental import pallas as pl
from jax.experimental.pallas import tpu as pltpu
from jax.sharding import PartitionSpec as P

HEADS = 17


EPS = 1e-05
GELU_C = 0.7978845608028654


def gelu_tanh(values):
    return 0.5 * values * (1.0 + jnp.tanh(GELU_C * (values + 0.044715 * values * values * values)))


def normalize(residual):
    row_mean = jnp.mean(residual, -1, keepdims=True)
    centered = residual - row_mean
    inv_std = lax.rsqrt(jnp.mean(centered * centered, -1, keepdims=True) + EPS)
    return (centered * inv_std, inv_std)


def norm_back(grad_normed, scaled, inv_std, gain_row):
    grad_scaled = grad_normed * gain_row
    return inv_std * (
        grad_scaled
        - jnp.mean(grad_scaled, -1, keepdims=True)
        - scaled * jnp.mean(grad_scaled * scaled, -1, keepdims=True)
    )


def running_total(counts):
    index = jnp.arange(counts.shape[0], dtype=jnp.int32)
    return jnp.sum(jnp.where(index[None, :] <= index[:, None], counts[None, :], 0), 1)


def segment_of(places, doc_ends):
    return jnp.sum((places[:, None] >= doc_ends[None, :]).astype(jnp.int32), 1)


def pair_swap(block):
    route = [(i, i ^ 1) for i in range(lax.axis_size("seq"))]
    return lax.ppermute(block, "seq", route)


def same_core():
    n_seq = lax.axis_size("seq")
    return [list(range(core, n_seq, 2)) for core in range(2)]


def gather_stack(shard):
    chips = lax.all_gather(shard, "seq", axis_index_groups=same_core())
    held = lax.all_gather(chips, "dp")
    other = pair_swap(held)
    first = lax.axis_index("seq") % 2 == 0
    both = jnp.stack([jnp.where(first, held, other), jnp.where(first, other, held)], 2)
    dp, chip_count = held.shape[:2]
    return both.transpose(1, 2, 0, 3, 4).reshape(2 * chip_count, dp, *shard.shape)


def pair_sum(parts):
    pairs = parts.reshape(parts.shape[0] // 2, 2, *parts.shape[1:])
    first = lax.axis_index("seq") % 2 == 0
    mine = jnp.where(first, pairs[:, 0], pairs[:, 1])
    other = jnp.where(first, pairs[:, 1], pairs[:, 0])
    got = pair_swap(other)
    return (mine.astype(jnp.float32) + got.astype(jnp.float32)).astype(jnp.bfloat16)


def scatter_stack(parts, after):
    held = pair_sum(parts).transpose(1, 0, 2, 3).reshape(-1, parts.shape[3])
    if after is not None:
        held, after = lax.optimization_barrier((held, after))
    held = lax.psum_scatter(held, "dp", scatter_dimension=0, tiled=True)
    held = lax.psum_scatter(
        held, "seq", scatter_dimension=0, axis_index_groups=same_core(), tiled=True
    )
    return held, after


def dot(left, right):
    return jnp.dot(left, right, preferred_element_type=jnp.float32)


def dot_right_t(left, right):
    return lax.dot_general(left, right, (((1,), (1,)), ((), ())), preferred_element_type=jnp.float32)


def dot_left_t(left, right):
    return lax.dot_general(left, right, (((0,), (0,)), ((), ())), preferred_element_type=jnp.float32)


def cols_of(rows, count):
    return rows.reshape(rows.shape[0], count, -1).transpose(1, 0, 2)


def apply_cols(rows, cols):
    lifted = jnp.broadcast_to(rows[None], (cols.shape[0],) + rows.shape)
    made = lax.dot_general(
        lifted, cols, (((2,), (1,)), ((0,), (0,))), preferred_element_type=jnp.float32
    )
    return made.transpose(1, 0, 2).reshape(rows.shape[0], -1)


def apply_cols_t(rows, cols):
    lifted = cols_of(rows, cols.shape[0])
    return lax.dot_general(
        lifted, cols, (((0, 2), (0, 2)), ((), ())), preferred_element_type=jnp.float32
    )


def grad_cols(left, right, count):
    lifted = jnp.broadcast_to(left[None], (count,) + left.shape)
    return lax.dot_general(
        lifted, cols_of(right, count), (((1,), (1,)), ((0,), (0,))),
        preferred_element_type=jnp.float32,
    )


def heads_of(rows, micro_count, head_dim):
    return rows.reshape(micro_count, -1, HEADS, head_dim).transpose(0, 2, 1, 3)


def rows_of(heads):
    micro_count, _, slots, head_dim = heads.shape
    return heads.transpose(0, 2, 1, 3).reshape(micro_count * slots, HEADS * head_dim)


def batched(left, right, left_dim, right_dim):
    return lax.dot_general(
        left,
        right,
        (((left_dim,), (right_dim,)), ((0, 1), (0, 1))),
        preferred_element_type=jnp.float32,
    )


def shards_plain(
    tokens,
    cotangent,
    w_qkv,
    w_out,
    w_up,
    w_down,
    gain_one,
    bias_one,
    gain_two,
    bias_two,
    lengths,
    slot_order,
):
    micro_count, tok_dev, width = tokens.shape
    rows = micro_count * tok_dev
    head_dim = width // HEADS
    score_scale = head_dim ** (-0.5)
    n_seq = lax.axis_size("seq")
    my_slot = lax.axis_index("seq")
    bf16 = jnp.bfloat16

    norms = lax.all_gather(
        jnp.stack([gain_one, bias_one, gain_two, bias_two]), "dp", axis=1, tiled=True
    ).astype(jnp.float32)
    g_one, b_one, g_two, b_two = norms[0], norms[1], norms[2], norms[3]
    n_dp = lax.axis_size("dp")
    part, qkv_cols = w_qkv.shape
    out_cols = w_out.shape[1]
    up_cols = w_up.shape[1]
    fold = w_down.shape[0] // up_cols
    attn_stack = gather_stack(jnp.concatenate([w_qkv, w_out], 1))
    down_t = w_down.T
    ffn_stack = gather_stack(
        jnp.concatenate([w_up, *jnp.split(down_t, fold, 1)], 0)
    )
    cols_qkv = attn_stack[..., :qkv_cols].reshape(n_seq, width, qkv_cols)
    full_out = (
        attn_stack[..., qkv_cols:].reshape(n_seq, width, out_cols).transpose(1, 0, 2)
    ).reshape(width, width)
    cols_up = ffn_stack[:, :, :part].reshape(n_seq, width, up_cols)
    full_down_t = (
        ffn_stack[:, :, part:]
        .reshape(n_seq, n_dp, fold, out_cols, up_cols)
        .transpose(0, 3, 1, 2, 4)
        .reshape(width, fold * n_dp * up_cols)
    )

    doc_ends = jax.vmap(running_total)(lengths[:, 0])
    k_place = (
        slot_order[:, 0, :, None] * tok_dev + jnp.arange(tok_dev, dtype=jnp.int32)
    ).reshape(micro_count, n_seq * tok_dev)
    k_segment = jax.vmap(segment_of)(k_place, doc_ends)
    base_slot = lax.dynamic_slice_in_dim(slot_order[:, 0], my_slot, 1, 1)
    q_place = base_slot * tok_dev + jnp.arange(tok_dev, dtype=jnp.int32)
    q_segment = jax.vmap(segment_of)(q_place, doc_ends)
    allowed = (q_segment[:, :, None] == k_segment[:, None, :]) & (
        k_place[:, None, :] <= q_place[:, :, None]
    )

    residual = tokens.astype(jnp.float32).reshape(rows, width)
    scaled_one, inv_one = normalize(residual)
    normed_one = (scaled_one * g_one + b_one).astype(bf16)
    qkv_all = apply_cols(normed_one, cols_qkv).astype(bf16)
    queries = heads_of(qkv_all[:, :width], micro_count, head_dim)
    local_kv = qkv_all[:, width:].reshape(micro_count, tok_dev, 2 * width)
    group_kv = lax.all_gather(local_kv, "seq", axis=1, tiled=True)
    keys = heads_of(group_kv[..., :width], micro_count, head_dim)
    values = heads_of(group_kv[..., width:], micro_count, head_dim)

    scores = batched(queries, keys, 3, 3) * score_scale
    scores = jnp.where(allowed[:, None], scores, -jnp.inf)
    weights = jnp.exp(scores - jnp.max(scores, -1, keepdims=True))
    probs = weights * (1.0 / jnp.sum(weights, -1, keepdims=True))
    probs_low = probs.astype(bf16)
    attended = batched(probs_low, values, 3, 2)
    attn_flat = rows_of(attended.astype(bf16))
    middle = residual + dot(attn_flat, full_out)
    scaled_two, inv_two = normalize(middle)
    normed_two = (scaled_two * g_two + b_two).astype(bf16)
    hidden = apply_cols(normed_two, cols_up)
    activated_full, gelu_back = jax.vjp(gelu_tanh, hidden)
    activated = activated_full.astype(bf16)

    grad_rows = cotangent.reshape(rows, width)
    block_out = (middle + dot_right_t(activated, full_down_t)).astype(bf16)
    grad_hidden = gelu_back(dot(grad_rows, full_down_t))[0].astype(bf16)
    sum_down_t = dot_left_t(grad_rows, activated).astype(bf16)
    sum_down_t = (
        sum_down_t.reshape(n_seq, out_cols, n_dp, fold, up_cols)
        .transpose(0, 2, 3, 1, 4)
        .reshape(n_seq, n_dp, fold * out_cols, up_cols)
    )
    sum_up = grad_cols(normed_two, grad_hidden, n_seq).astype(bf16)
    sum_ffn, _ = scatter_stack(
        jnp.concatenate([sum_up.reshape(n_seq, n_dp, part, up_cols), sum_down_t], 2), None
    )
    grad_normed_two = apply_cols_t(grad_hidden, cols_up)
    grad_middle = grad_rows.astype(jnp.float32) + norm_back(
        grad_normed_two, scaled_two, inv_two, g_two
    )
    grad_branch = grad_middle.astype(bf16)
    sum_proj = grad_cols(attn_flat, grad_branch, n_seq).astype(bf16)
    grad_heads = heads_of(
        dot_right_t(grad_branch, full_out).astype(bf16), micro_count, head_dim
    )

    grad_probs = batched(grad_heads, values, 3, 3)
    row_dot = jnp.sum(probs * grad_probs, -1, keepdims=True)
    grad_scores = (probs * (grad_probs - row_dot)).astype(bf16)
    grad_query = rows_of(batched(grad_scores, keys, 3, 2) * score_scale)
    grad_keys = rows_of(batched(grad_scores, queries, 2, 2) * score_scale)
    grad_values = rows_of(batched(probs_low, grad_heads, 2, 2))
    grad_kv = jnp.concatenate([grad_keys.astype(bf16), grad_values.astype(bf16)], 1)
    grad_kv = grad_kv.reshape(micro_count, n_seq, tok_dev, 2 * width).transpose(1, 0, 2, 3)
    grad_kv = lax.psum_scatter(
        pair_sum(grad_kv), "seq", scatter_dimension=0, axis_index_groups=same_core()
    ).reshape(rows, 2 * width)
    grad_qkv_rows = jnp.concatenate([grad_query.astype(bf16), grad_kv], 1)
    sum_qkv = grad_cols(normed_one, grad_qkv_rows, n_seq).astype(bf16)
    sum_attn, sum_ffn = scatter_stack(
        jnp.concatenate([sum_qkv, sum_proj], 2).reshape(n_seq, n_dp, part, qkv_cols + out_cols),
        sum_ffn,
    )
    sum_attn = sum_attn.astype(jnp.float32)
    sum_ffn = sum_ffn.astype(jnp.float32)
    out_up = sum_ffn[:part]
    out_down = jnp.concatenate(jnp.split(sum_ffn[part:], fold, 0), 1).T
    out_qkv = sum_attn[:, :qkv_cols]
    out_proj = sum_attn[:, qkv_cols:]
    grad_normed_one = apply_cols_t(grad_qkv_rows, cols_qkv)
    grad_input = (
        grad_middle + norm_back(grad_normed_one, scaled_one, inv_one, g_one)
    ).astype(bf16)

    norm_sums = jnp.stack(
        [
            jnp.sum(grad_normed_one * scaled_one, 0),
            jnp.sum(grad_normed_one, 0),
            jnp.sum(grad_normed_two * scaled_two, 0),
            jnp.sum(grad_normed_two, 0),
        ]
    )
    norm_totals = lax.psum(norm_sums, ("dp", "seq"))
    norm_mine = lax.dynamic_slice_in_dim(norm_totals, lax.axis_index("dp") * part, part, 1)
    return (
        block_out.reshape(tokens.shape),
        grad_input.reshape(tokens.shape),
        out_qkv,
        out_proj,
        out_up,
        out_down,
        norm_mine[0],
        norm_mine[1],
        norm_mine[2],
        norm_mine[3],
    )


MESH = pl.DeviceIdType.MESH
ORDERS = tuple(tuple((q + k) % 4 for k in range(4)) for q in range(4))
TILE = 128
LANES = (3 * TILE, 3 * TILE, 3 * TILE, 4 * TILE)
UNITS = 5
REM_UP, REM_QKV, REM_OUT, REM_DOWN, REM_NORM = 0, 32, 56, 64, 96


def place_of(q, dp, seq):
    z = seq // 2
    bits = (dp % 2, dp // 2, (z % 2 + z // 2) % 2, z // 2)
    return sum(bits[dim] * 2**k for k, dim in enumerate(ORDERS[q]))


def partner(dim):
    dp, seq = lax.axis_index("dp"), lax.axis_index("seq")
    z, core = seq // 2, seq % 2
    if dim == 0:
        return (dp + 1 - 2 * (dp % 2), seq)
    if dim == 1:
        return (dp + 2 - 4 * (dp // 2), seq)
    if dim == 2:
        return (dp, (z + 1 - 2 * (z % 2)) * 2 + core)
    return (dp, (3 - z) * 2 + core)


def sibling():
    dp, seq = lax.axis_index("dp"), lax.axis_index("seq")
    return (dp, seq + 1 - 2 * (seq % 2))


def greet(devices):
    barrier = pltpu.get_barrier_semaphore()
    for device in devices:
        pl.semaphore_signal(barrier, inc=1, device_id=device, device_id_type=MESH)
    pl.semaphore_wait(barrier, len(devices))


def send(src, dst, send_sem, recv_sem, device):
    copy = pltpu.make_async_remote_copy(
        src_ref=src, dst_ref=dst, send_sem=send_sem, recv_sem=recv_sem,
        device_id=device, device_id_type=MESH,
    )
    copy.start()
    return copy


def gather_kernel(*refs):
    shards_in, full = refs[:4], refs[4:8]
    own_sem, link_send, link_recv, sib_send, sib_recv = refs[8:]
    dp, seq = lax.axis_index("dp"), lax.axis_index("seq")
    core = seq % 2
    greet([partner(dim) for dim in range(4)] + [sibling()])
    at = [place_of(q, dp, seq) for q in range(4)]
    links, sides, owns = {}, [], []
    for q in range(4):
        links[q] = send(
            shards_in[q], full[q].at[core, at[q]], link_send.at[q, 0], link_recv.at[q, 0],
            partner(ORDERS[q][0]),
        )
        own = pltpu.make_async_copy(shards_in[q], full[q].at[core, at[q]], own_sem.at[q])
        own.start()
        owns.append(own)
        sides.append(
            send(
                shards_in[q], full[q].at[core, at[q]], sib_send.at[q, 0], sib_recv.at[q, 0],
                sibling(),
            )
        )
    for own in owns:
        own.wait()
    for stage in range(4):
        for q in range(4):
            links[q].wait()
            size = 2**stage
            if stage < 3:
                held = full[q].at[core, pl.ds(at[q] // (2 * size) * (2 * size), 2 * size)]
                links[q] = send(
                    held, held, link_send.at[q, stage + 1], link_recv.at[q, stage + 1],
                    partner(ORDERS[q][stage + 1]),
                )
            mine = at[q] // size
            got = full[q].at[core, pl.ds((mine + 1 - 2 * (mine % 2)) * size, size)]
            sides.append(
                send(
                    got, got, sib_send.at[q, stage + 1], sib_recv.at[q, stage + 1], sibling()
                )
            )
    for side in sides:
        side.wait()


def gather_weights(chunks):
    rows = chunks[0].shape[0]
    anywhere = pl.BlockSpec(memory_space=pl.ANY)
    dma = pltpu.SemaphoreType.DMA
    return pl.pallas_call(
        gather_kernel,
        out_shape=[jax.ShapeDtypeStruct((2, 16, rows, lanes), jnp.bfloat16) for lanes in LANES],
        in_specs=[anywhere] * 4,
        out_specs=[anywhere] * 4,
        scratch_shapes=[dma((4,)), dma((4, 4)), dma((4, 4)), dma((4, 5)), dma((4, 5))],
        compiler_params=pltpu.CompilerParams(collective_id=0, has_side_effects=True),
        name="gather_weights",
    )(*chunks)


def scatter_kernel(*refs):
    parts, outs = refs[:4], refs[4:8]
    own, acc, got3, got2, got1, got0 = (refs[8 + 4 * i : 12 + 4 * i] for i in range(6))
    got = (got0, got1, got2, got3)
    own_sem, link_send, link_recv, sib_send, sib_recv = refs[32:]
    dp, seq = lax.axis_index("dp"), lax.axis_index("seq")
    core = seq % 2
    greet([partner(dim) for dim in range(4)] + [sibling()])
    at = [place_of(q, dp, seq) for q in range(4)]
    side, load = {}, {}
    for part in range(2):
        for q in range(4):
            high = at[q] // 8
            span = pl.ds(((1 - high) if part == 0 else high) * 8, 8)
            side[q, part] = send(
                parts[q].at[1 - core, span], acc[q].at[span],
                sib_send.at[q, part], sib_recv.at[q, part], sibling(),
            )
            load[q, part] = pltpu.make_async_copy(
                parts[q].at[core, span], own[q].at[span], own_sem.at[q, part]
            )
            load[q, part].start()

    def add(q, base, other, other_base, count):
        def one(b, carry):
            acc[q][base + b] = acc[q][base + b] + other[other_base + b]
            return carry

        lax.fori_loop(0, count, one, 0)

    links = {}
    for part in range(2):
        for q in range(4):
            side[q, part].wait_recv()
            load[q, part].wait()
            high = at[q] // 8
            base = ((1 - high) if part == 0 else high) * 8
            add(q, base, own[q], base, 8)
            if part == 0:
                links[q, 3] = send(
                    acc[q].at[pl.ds(base, 8)], got3[q], link_send.at[q, 3], link_recv.at[q, 3],
                    partner(ORDERS[q][3]),
                )
    for stage in (3, 2, 1):
        half = 2 ** (stage - 1)
        for q in range(4):
            links[q, stage].wait_recv()
            base = at[q] // (2 * half) * (2 * half)
            high = at[q] // half % 2
            away, keep = (1 - high) * half, high * half
            add(q, base + away, got[stage][q], away, half)
            links[q, stage - 1] = send(
                acc[q].at[pl.ds(base + away, half)], got[stage - 1][q],
                link_send.at[q, stage - 1], link_recv.at[q, stage - 1],
                partner(ORDERS[q][stage - 1]),
            )
            add(q, base + keep, got[stage][q], keep, half)
    for q in range(4):
        links[q, 0].wait_recv()
        outs[q][...] = acc[q][at[q]] + got0[q][0]
    for copy in list(side.values()) + list(links.values()):
        copy.wait_send()


def scatter_grads(parts):
    rows = parts[0].shape[2]
    dma = pltpu.SemaphoreType.DMA
    bf16 = jnp.bfloat16
    buffers = [
        pltpu.VMEM((count, rows, lanes), bf16) for count in (16, 16, 8, 4, 2, 1) for lanes in LANES
    ]
    return pl.pallas_call(
        scatter_kernel,
        out_shape=[jax.ShapeDtypeStruct((rows, lanes), bf16) for lanes in LANES],
        in_specs=[pl.BlockSpec(memory_space=pl.ANY)] * 4,
        out_specs=[pl.BlockSpec(memory_space=pltpu.VMEM)] * 4,
        scratch_shapes=buffers + [dma((4, 2)), dma((4, 4)), dma((4, 4)), dma((4, 2)), dma((4, 2))],
        compiler_params=pltpu.CompilerParams(
            collective_id=1, has_side_effects=True, vmem_limit_bytes=56 * 2**20
        ),
        name="scatter_grads",
    )(*parts)


def exchange_kernel(blocks, out, own_sem, send_sem, recv_sem):
    dp, seq = lax.axis_index("dp"), lax.axis_index("seq")
    others = [(dp, (seq + k) % 8) for k in range(1, 8)]
    greet(others)
    own = pltpu.make_async_copy(blocks.at[seq], out.at[seq], own_sem)
    copies = [
        send(blocks.at[device[1]], out.at[seq], send_sem.at[k], recv_sem.at[k], device)
        for k, device in enumerate(others)
    ]
    own.start()
    own.wait()
    for copy in copies:
        copy.wait()


def exchange(blocks, which):
    dma = pltpu.SemaphoreType.DMA
    return pl.pallas_call(
        exchange_kernel,
        out_shape=jax.ShapeDtypeStruct(blocks.shape, blocks.dtype),
        in_specs=[pl.BlockSpec(memory_space=pl.ANY)],
        out_specs=pl.BlockSpec(memory_space=pl.ANY),
        scratch_shapes=[dma, dma((7,)), dma((7,))],
        compiler_params=pltpu.CompilerParams(collective_id=2 + which, has_side_effects=True),
        name=f"exchange_{which}",
    )(blocks)


def spots():
    for dp in range(4):
        for seq in range(8):
            yield dp, seq, seq % 2, [place_of(q, dp, seq) for q in range(4)]


def unpack_kernel(c0, c1, c2, c3, qkv, out, up, down, norms):
    for dp, s, core, at in spots():
        qkv[dp, :, s * 408 : s * 408 + 384] = c0[core, at[0]]
        mixed = c1[core, at[1]]
        rem = mixed[:, TILE : 2 * TILE]
        out[dp, :, s * 136 : s * 136 + 128] = mixed[:, :TILE]
        up[dp, :, s * 544 : s * 544 + 128] = mixed[:, 2 * TILE :]
        up[dp, :, s * 544 + 128 : s * 544 + 512] = c2[core, at[2]]
        up[dp, :, s * 544 + 512 : s * 544 + 544] = rem[:, REM_UP : REM_UP + 32]
        qkv[dp, :, s * 408 + 384 : s * 408 + 408] = rem[:, REM_QKV : REM_QKV + 24]
        out[dp, :, s * 136 + 128 : s * 136 + 136] = rem[:, REM_OUT : REM_OUT + 8]
        for i in range(4):
            down[dp * 4 + i, :, s * 136 : s * 136 + 128] = c3[core, at[3], :, i * TILE : (i + 1) * TILE]
            down[dp * 4 + i, :, s * 136 + 128 : s * 136 + 136] = rem[
                :, REM_DOWN + 8 * i : REM_DOWN + 8 * i + 8
            ]
        if s == 0:
            norms[dp] = rem


def unpack_weights(chunks):
    bf16 = jnp.bfloat16
    rows, step = chunks[0].shape[2], 16

    def spec(count, lanes):
        return pl.BlockSpec((count, step, lanes), lambda i: (0, i, 0))

    sizes = ((4, 3264), (4, 1088), (4, 4352), (16, 1088), (4, 128))
    return pl.pallas_call(
        unpack_kernel,
        grid=(rows // step,),
        out_shape=[jax.ShapeDtypeStruct((count, rows, lanes), bf16) for count, lanes in sizes],
        in_specs=[pl.BlockSpec((2, 16, step, lanes), lambda i: (0, 0, i, 0)) for lanes in LANES],
        out_specs=[spec(*size) for size in sizes],
        compiler_params=pltpu.CompilerParams(vmem_limit_bytes=40 * 2**20),
        name="unpack_weights",
    )(*chunks)


def pack_kernel(qkv, out, up, down, norms, c0, c1, c2, c3):
    for dp, s, core, at in spots():
        c0[core, at[0]] = qkv[dp, :, s * 408 : s * 408 + 384]
        c1[core, at[1], :, :TILE] = out[dp, :, s * 136 : s * 136 + 128]
        c1[core, at[1], :, 2 * TILE :] = up[dp, :, s * 544 : s * 544 + 128]
        c2[core, at[2]] = up[dp, :, s * 544 + 128 : s * 544 + 512]
        base = at[1]
        c1[core, base, :, TILE : 2 * TILE] = norms[dp]
        c1[core, base, :, TILE + REM_UP : TILE + REM_UP + 32] = up[dp, :, s * 544 + 512 : s * 544 + 544]
        c1[core, base, :, TILE + REM_QKV : TILE + REM_QKV + 24] = qkv[dp, :, s * 408 + 384 : s * 408 + 408]
        c1[core, base, :, TILE + REM_OUT : TILE + REM_OUT + 8] = out[dp, :, s * 136 + 128 : s * 136 + 136]
        for i in range(4):
            c3[core, at[3], :, i * TILE : (i + 1) * TILE] = down[dp * 4 + i, :, s * 136 : s * 136 + 128]
            spot = TILE + REM_DOWN + 8 * i
            c1[core, base, :, spot : spot + 8] = down[dp * 4 + i, :, s * 136 + 128 : s * 136 + 136]


def pack_grads(qkv, out, up, down, norms):
    rows, step = qkv.shape[1], 16

    def spec(count, lanes):
        return pl.BlockSpec((count, step, lanes), lambda i: (0, i, 0))

    return pl.pallas_call(
        pack_kernel,
        grid=(rows // step,),
        out_shape=[jax.ShapeDtypeStruct((2, 16, rows, lanes), jnp.bfloat16) for lanes in LANES],
        in_specs=[spec(4, 3264), spec(4, 1088), spec(4, 4352), spec(16, 1088), spec(4, 128)],
        out_specs=[pl.BlockSpec((2, 16, step, lanes), lambda i: (0, 0, i, 0)) for lanes in LANES],
        compiler_params=pltpu.CompilerParams(vmem_limit_bytes=40 * 2**20),
        name="pack_grads",
    )(qkv, out, up, down, norms)


QUERY_BLOCK = 256


def flip(block):
    return block.astype(jnp.float32).T.astype(jnp.bfloat16)


def masked_scores(k_rows, q_cols, seg_k, seg_q, start, scale):
    count, width = k_rows.shape[0], q_cols.shape[1]
    scores = dot(k_rows, q_cols) * scale
    key_at = lax.broadcasted_iota(jnp.int32, (count, width), 0)
    query_at = lax.broadcasted_iota(jnp.int32, (count, width), 1) + start
    return jnp.where((seg_k == seg_q) & (key_at <= query_at), scores, -1e30)


def attend_kernel(scale, order, x, seg_k, seg_q, out, lse, q_t, k_t, v_t, o_t):
    unit = pl.program_id(0)
    slots = x.shape[0]
    tok = x.shape[3]
    depth = q_t.shape[0]
    for b in range(slots):
        at = order[unit, b]
        for n, held in enumerate((q_t, k_t, v_t)):
            held[:, b * tok : (b + 1) * tok] = x[at, 0, n * depth : (n + 1) * depth]
    keys = flip(k_t[...])
    for start in range(0, slots * tok, QUERY_BLOCK):
        count = start + QUERY_BLOCK
        cols = slice(start, count)
        scores = masked_scores(
            keys[:count], q_t[:, cols], seg_k[0, :count], seg_q[0, :, cols], start, scale
        )
        top = jnp.max(scores, 0, keepdims=True)
        weights = jnp.exp(scores - top)
        total = jnp.sum(weights, 0, keepdims=True)
        probs = (weights * (1.0 / total)).astype(jnp.bfloat16)
        o_t[:, cols] = dot(v_t[:, :count], probs).astype(jnp.bfloat16)
        lse[0, :, cols] = top + jnp.log(total)
    for b in range(slots):
        out[order[unit, b], 0] = o_t[:, b * tok : (b + 1) * tok]


def attend(x, order, seg_k, seg_q, scale):
    slots, units, depth3, tok = x.shape
    depth, length = depth3 // 3, slots * tok
    bf16 = jnp.bfloat16
    held = [pltpu.VMEM((depth, length), bf16)] * 4
    return pl.pallas_call(
        functools.partial(attend_kernel, scale),
        grid_spec=pltpu.PrefetchScalarGridSpec(
            num_scalar_prefetch=1,
            grid=(units,),
            in_specs=[
                pl.BlockSpec((slots, 1, depth3, tok), lambda u, o: (0, u, 0, 0)),
                pl.BlockSpec((1, length, 1), lambda u, o: (u, 0, 0)),
                pl.BlockSpec((1, 1, length), lambda u, o: (u, 0, 0)),
            ],
            out_specs=[
                pl.BlockSpec((slots, 1, depth, tok), lambda u, o: (0, u, 0, 0)),
                pl.BlockSpec((1, 1, length), lambda u, o: (u, 0, 0)),
            ],
            scratch_shapes=held,
        ),
        out_shape=[
            jax.ShapeDtypeStruct((slots, units, depth, tok), bf16),
            jax.ShapeDtypeStruct((units, 1, length), jnp.float32),
        ],
        compiler_params=pltpu.CompilerParams(vmem_limit_bytes=40 * 2**20),
        name="attend",
    )(order, x, seg_k, seg_q)


def attend_back_kernel(
    scale, order, x, g, seg_k, seg_q, lse, out, q_t, k_t, v_t, g_t, dq_t, dk_t, dv_t
):
    unit = pl.program_id(0)
    slots = x.shape[0]
    tok = x.shape[3]
    depth = q_t.shape[0]
    for b in range(slots):
        at = order[unit, b]
        for n, held in enumerate((q_t, k_t, v_t)):
            held[:, b * tok : (b + 1) * tok] = x[at, 0, n * depth : (n + 1) * depth]
        g_t[:, b * tok : (b + 1) * tok] = g[at, 0]
    keys = flip(k_t[...])
    values = flip(v_t[...])
    length = slots * tok
    for start in reversed(range(0, length, QUERY_BLOCK)):
        count = start + QUERY_BLOCK
        cols = slice(start, count)
        queries, grads = q_t[:, cols], g_t[:, cols]
        scores = masked_scores(
            keys[:count], queries, seg_k[0, :count], seg_q[0, :, cols], start, scale
        )
        probs = jnp.exp(scores - lse[0, :, cols])
        grad_probs = dot(values[:count], grads)
        row_dot = jnp.sum(probs * grad_probs, 0, keepdims=True)
        grad_scores = (probs * (grad_probs - row_dot)).astype(jnp.bfloat16)
        probs_low = probs.astype(jnp.bfloat16)
        dq_t[:, cols] = dot(k_t[:, :count], grad_scores) * scale
        dk = dot_right_t(queries, grad_scores)
        dv = dot_right_t(grads, probs_low)
        if count == length:
            dk_t[...] = dk
            dv_t[...] = dv
        else:
            dk_t[:, :count] += dk
            dv_t[:, :count] += dv
    for b in range(slots):
        at = order[unit, b]
        cols = slice(b * tok, (b + 1) * tok)
        out[at, 0, :depth] = dq_t[:, cols].astype(jnp.bfloat16)
        out[at, 0, depth : 2 * depth] = (dk_t[:, cols] * scale).astype(jnp.bfloat16)
        out[at, 0, 2 * depth :] = dv_t[:, cols].astype(jnp.bfloat16)


def attend_back(x, g, order, seg_k, seg_q, lse, scale):
    slots, units, depth3, tok = x.shape
    depth, length = depth3 // 3, slots * tok
    bf16 = jnp.bfloat16
    held = [pltpu.VMEM((depth, length), bf16)] * 4 + [pltpu.VMEM((depth, length), jnp.float32)] * 3
    return pl.pallas_call(
        functools.partial(attend_back_kernel, scale),
        grid_spec=pltpu.PrefetchScalarGridSpec(
            num_scalar_prefetch=1,
            grid=(units,),
            in_specs=[
                pl.BlockSpec((slots, 1, depth3, tok), lambda u, o: (0, u, 0, 0)),
                pl.BlockSpec((slots, 1, depth, tok), lambda u, o: (0, u, 0, 0)),
                pl.BlockSpec((1, length, 1), lambda u, o: (u, 0, 0)),
                pl.BlockSpec((1, 1, length), lambda u, o: (u, 0, 0)),
                pl.BlockSpec((1, 1, length), lambda u, o: (u, 0, 0)),
            ],
            out_specs=pl.BlockSpec((slots, 1, depth3, tok), lambda u, o: (0, u, 0, 0)),
            scratch_shapes=held,
        ),
        out_shape=jax.ShapeDtypeStruct(x.shape, bf16),
        compiler_params=pltpu.CompilerParams(vmem_limit_bytes=48 * 2**20),
        name="attend_back",
    )(order, x, g, seg_k, seg_q, lse)


def to_units(flat, micro_count, kinds):
    tok = flat.shape[1] // micro_count
    units = flat.reshape(kinds, HEADS, -1, micro_count, tok).transpose(3, 1, 0, 2, 4)
    units = units.reshape(micro_count * HEADS, -1, tok)
    units = jnp.pad(units, ((0, 8 * UNITS - units.shape[0]), (0, 0), (0, 0)))
    return units.reshape(8, UNITS, -1, tok)


def from_units(units, micro_count, kinds):
    tok = units.shape[3]
    held = units.reshape(8 * UNITS, -1, tok)[: micro_count * HEADS]
    held = held.reshape(micro_count, HEADS, kinds, -1, tok).transpose(0, 4, 2, 1, 3)
    return held.reshape(micro_count * tok, -1)


def shards_fast(
    tokens,
    cotangent,
    w_qkv,
    w_out,
    w_up,
    w_down,
    gain_one,
    bias_one,
    gain_two,
    bias_two,
    lengths,
    slot_order,
):
    micro_count, tok_dev, width = tokens.shape
    rows = micro_count * tok_dev
    scale = (width // HEADS) ** (-0.5)
    bf16, f32 = jnp.bfloat16, jnp.float32
    part = w_qkv.shape[0]
    my_slot = lax.axis_index("seq")

    downs = [w_down[i * part : (i + 1) * part] for i in range(4)]
    norms = jnp.stack([gain_one, bias_one, gain_two, bias_two], 1)
    rem = jnp.concatenate(
        [w_up[:, 512:], w_qkv[:, 384:], w_out[:, 128:]]
        + [down[:, 128:] for down in downs]
        + [norms, jnp.zeros((part, 28), bf16)],
        1,
    )
    gathered = gather_weights(
        [
            w_qkv[:, :384],
            jnp.concatenate([w_out[:, :128], rem, w_up[:, :128]], 1),
            w_up[:, 128:512],
            jnp.concatenate([down[:, :128] for down in downs], 1),
        ]
    )
    full_qkv, full_out, full_up, full_down, full_norms = unpack_weights(gathered)
    full_qkv = full_qkv.reshape(width, -1)
    full_out = full_out.reshape(width, width)
    full_up = full_up.reshape(width, -1)
    full_down = full_down.reshape(-1, width)
    norm_rows = full_norms[:, :, REM_NORM : REM_NORM + 4].reshape(width, 4).T.astype(f32)
    g_one, b_one, g_two, b_two = norm_rows[0], norm_rows[1], norm_rows[2], norm_rows[3]

    unit_ids = my_slot * UNITS + jnp.arange(UNITS, dtype=jnp.int32)
    second = (unit_ids >= HEADS)[:, None]
    doc_ends = jax.vmap(running_total)(lengths[:, 0])
    places = jnp.arange(8 * tok_dev, dtype=jnp.int32)
    segments = jax.vmap(segment_of, (None, 0))(places, doc_ends)
    unit_segments = jnp.where(second, segments[1][None], segments[0][None])
    seg_k, seg_q = unit_segments[:, :, None], unit_segments[:, None, :]
    slots = jnp.arange(8, dtype=jnp.int32)
    holders = jnp.sum(
        jnp.where(slot_order[:, 0][:, None, :] == slots[None, :, None], slots[None, None, :], 0), 2
    )
    order = jnp.where(second, holders[1][None], holders[0][None])

    residual = tokens.astype(f32).reshape(rows, width)
    scaled_one, inv_one = normalize(residual)
    normed_one = (scaled_one * g_one + b_one).astype(bf16)
    qkv_t = lax.dot_general(
        full_qkv, normed_one, (((0,), (1,)), ((), ())), preferred_element_type=f32
    ).astype(bf16)
    unit_qkv = exchange(to_units(qkv_t, micro_count, 3), 0)
    unit_out, lse = attend(unit_qkv, order, seg_k, seg_q, scale)
    attn_flat = from_units(exchange(unit_out, 1), micro_count, 1)
    middle = residual + dot(attn_flat, full_out)
    scaled_two, inv_two = normalize(middle)
    normed_two = (scaled_two * g_two + b_two).astype(bf16)
    hidden = dot(normed_two, full_up)
    activated_full, gelu_back = jax.vjp(gelu_tanh, hidden)
    activated = activated_full.astype(bf16)

    grad_rows = cotangent.reshape(rows, width)
    block_out = (middle + dot(activated, full_down)).astype(bf16)
    grad_hidden = gelu_back(dot_right_t(grad_rows, full_down))[0].astype(bf16)
    sum_down = dot_left_t(activated, grad_rows).astype(bf16)
    sum_up = dot_left_t(normed_two, grad_hidden).astype(bf16)
    grad_normed_two = dot_right_t(grad_hidden, full_up)
    grad_middle = grad_rows.astype(f32) + norm_back(grad_normed_two, scaled_two, inv_two, g_two)
    grad_branch = grad_middle.astype(bf16)
    sum_proj = dot_left_t(attn_flat, grad_branch).astype(bf16)
    grad_heads_t = dot_right_t(full_out, grad_branch).astype(bf16)
    unit_grad = exchange(to_units(grad_heads_t, micro_count, 1), 2)
    unit_back = attend_back(unit_qkv, unit_grad, order, seg_k, seg_q, lse, scale)
    grad_qkv_rows = from_units(exchange(unit_back, 3), micro_count, 3)
    sum_qkv = dot_left_t(normed_one, grad_qkv_rows).astype(bf16)
    grad_normed_one = dot_right_t(grad_qkv_rows, full_qkv)
    grad_input = (
        grad_middle + norm_back(grad_normed_one, scaled_one, inv_one, g_one)
    ).astype(bf16)

    norm_sums = jnp.stack(
        [
            jnp.sum(grad_normed_one * scaled_one, 0),
            jnp.sum(grad_normed_one, 0),
            jnp.sum(grad_normed_two * scaled_two, 0),
            jnp.sum(grad_normed_two, 0),
        ]
    )
    norm_cols = jnp.pad(norm_sums.T.astype(bf16), ((0, 0), (REM_NORM, 28)))
    sum0, sum1, sum2, sum3 = (
        total.astype(f32)
        for total in scatter_grads(
            pack_grads(
                sum_qkv.reshape(4, part, -1),
                sum_proj.reshape(4, part, -1),
                sum_up.reshape(4, part, -1),
                sum_down.reshape(16, part, -1),
                norm_cols.reshape(4, part, -1),
            )
        )
    )
    rest = sum1[:, TILE : 2 * TILE]
    out_qkv = jnp.concatenate([sum0, rest[:, REM_QKV : REM_QKV + 24]], 1)
    out_proj = jnp.concatenate([sum1[:, :TILE], rest[:, REM_OUT : REM_OUT + 8]], 1)
    out_up = jnp.concatenate([sum1[:, 2 * TILE :], sum2, rest[:, REM_UP : REM_UP + 32]], 1)
    out_down = jnp.concatenate(
        [
            jnp.concatenate(
                [
                    sum3[:, i * TILE : (i + 1) * TILE],
                    rest[:, REM_DOWN + 8 * i : REM_DOWN + 8 * i + 8],
                ],
                1,
            )
            for i in range(4)
        ],
        0,
    )
    norm_mine = rest[:, REM_NORM : REM_NORM + 4].T
    return (
        block_out.reshape(tokens.shape),
        grad_input.reshape(tokens.shape),
        out_qkv,
        out_proj,
        out_up,
        out_down,
        norm_mine[0],
        norm_mine[1],
        norm_mine[2],
        norm_mine[3],
    )


def solution(mesh):
    grid = (mesh.shape["dp"], mesh.shape["seq"])
    return jax.shard_map(
        shards_fast if grid == (4, 8) else shards_plain,
        mesh=mesh,
        in_specs=(
            P(None, ("dp", "seq"), None),
            P(None, ("dp", "seq"), None),
            P("dp", "seq"),
            P("dp", "seq"),
            P("dp", "seq"),
            P("dp", "seq"),
            P("dp"),
            P("dp"),
            P("dp"),
            P("dp"),
            P(None, "dp", None),
            P(None, "dp", None),
        ),
        out_specs=(
            P(None, ("dp", "seq"), None),
            P(None, ("dp", "seq"), None),
            P("dp", "seq"),
            P("dp", "seq"),
            P("dp", "seq"),
            P("dp", "seq"),
            P("dp"),
            P("dp"),
            P("dp"),
            P("dp"),
        ),
        check_vma=False,
    )
```

```python
import functools

import jax
import jax.numpy as jnp
from jax import lax
from jax.experimental import pallas as pl
from jax.experimental.pallas import tpu as pltpu
from jax.sharding import PartitionSpec as P

HEADS = 17


EPS = 1e-05
GELU_C = 0.7978845608028654


def gelu_tanh(values):
    return 0.5 * values * (1.0 + jnp.tanh(GELU_C * (values + 0.044715 * values * values * values)))


def normalize(residual):
    row_mean = jnp.mean(residual, -1, keepdims=True)
    centered = residual - row_mean
    inv_std = lax.rsqrt(jnp.mean(centered * centered, -1, keepdims=True) + EPS)
    return (centered * inv_std, inv_std)


def norm_back(grad_normed, scaled, inv_std, gain_row):
    grad_scaled = grad_normed * gain_row
    return inv_std * (
        grad_scaled
        - jnp.mean(grad_scaled, -1, keepdims=True)
        - scaled * jnp.mean(grad_scaled * scaled, -1, keepdims=True)
    )


def running_total(counts):
    index = jnp.arange(counts.shape[0], dtype=jnp.int32)
    return jnp.sum(jnp.where(index[None, :] <= index[:, None], counts[None, :], 0), 1)


def segment_of(places, doc_ends):
    return jnp.sum((places[:, None] >= doc_ends[None, :]).astype(jnp.int32), 1)


def pair_swap(block):
    route = [(i, i ^ 1) for i in range(lax.axis_size("seq"))]
    return lax.ppermute(block, "seq", route)


def same_core():
    n_seq = lax.axis_size("seq")
    return [list(range(core, n_seq, 2)) for core in range(2)]


def gather_stack(shard):
    chips = lax.all_gather(shard, "seq", axis_index_groups=same_core())
    held = lax.all_gather(chips, "dp")
    other = pair_swap(held)
    first = lax.axis_index("seq") % 2 == 0
    both = jnp.stack([jnp.where(first, held, other), jnp.where(first, other, held)], 2)
    dp, chip_count = held.shape[:2]
    return both.transpose(1, 2, 0, 3, 4).reshape(2 * chip_count, dp, *shard.shape)


def pair_sum(parts):
    pairs = parts.reshape(parts.shape[0] // 2, 2, *parts.shape[1:])
    first = lax.axis_index("seq") % 2 == 0
    mine = jnp.where(first, pairs[:, 0], pairs[:, 1])
    other = jnp.where(first, pairs[:, 1], pairs[:, 0])
    got = pair_swap(other)
    return (mine.astype(jnp.float32) + got.astype(jnp.float32)).astype(jnp.bfloat16)


def scatter_stack(parts, after):
    held = pair_sum(parts).transpose(1, 0, 2, 3).reshape(-1, parts.shape[3])
    if after is not None:
        held, after = lax.optimization_barrier((held, after))
    held = lax.psum_scatter(held, "dp", scatter_dimension=0, tiled=True)
    held = lax.psum_scatter(
        held, "seq", scatter_dimension=0, axis_index_groups=same_core(), tiled=True
    )
    return held, after


def dot(left, right):
    return jnp.dot(left, right, preferred_element_type=jnp.float32)


def dot_right_t(left, right):
    return lax.dot_general(left, right, (((1,), (1,)), ((), ())), preferred_element_type=jnp.float32)


def dot_left_t(left, right):
    return lax.dot_general(left, right, (((0,), (0,)), ((), ())), preferred_element_type=jnp.float32)


def cols_of(rows, count):
    return rows.reshape(rows.shape[0], count, -1).transpose(1, 0, 2)


def apply_cols(rows, cols):
    lifted = jnp.broadcast_to(rows[None], (cols.shape[0],) + rows.shape)
    made = lax.dot_general(
        lifted, cols, (((2,), (1,)), ((0,), (0,))), preferred_element_type=jnp.float32
    )
    return made.transpose(1, 0, 2).reshape(rows.shape[0], -1)


def apply_cols_t(rows, cols):
    lifted = cols_of(rows, cols.shape[0])
    return lax.dot_general(
        lifted, cols, (((0, 2), (0, 2)), ((), ())), preferred_element_type=jnp.float32
    )


def grad_cols(left, right, count):
    lifted = jnp.broadcast_to(left[None], (count,) + left.shape)
    return lax.dot_general(
        lifted, cols_of(right, count), (((1,), (1,)), ((0,), (0,))),
        preferred_element_type=jnp.float32,
    )


def heads_of(rows, micro_count, head_dim):
    return rows.reshape(micro_count, -1, HEADS, head_dim).transpose(0, 2, 1, 3)


def rows_of(heads):
    micro_count, _, slots, head_dim = heads.shape
    return heads.transpose(0, 2, 1, 3).reshape(micro_count * slots, HEADS * head_dim)


def batched(left, right, left_dim, right_dim):
    return lax.dot_general(
        left,
        right,
        (((left_dim,), (right_dim,)), ((0, 1), (0, 1))),
        preferred_element_type=jnp.float32,
    )


def shards_plain(
    tokens,
    cotangent,
    w_qkv,
    w_out,
    w_up,
    w_down,
    gain_one,
    bias_one,
    gain_two,
    bias_two,
    lengths,
    slot_order,
):
    micro_count, tok_dev, width = tokens.shape
    rows = micro_count * tok_dev
    head_dim = width // HEADS
    score_scale = head_dim ** (-0.5)
    n_seq = lax.axis_size("seq")
    my_slot = lax.axis_index("seq")
    bf16 = jnp.bfloat16

    norms = lax.all_gather(
        jnp.stack([gain_one, bias_one, gain_two, bias_two]), "dp", axis=1, tiled=True
    ).astype(jnp.float32)
    g_one, b_one, g_two, b_two = norms[0], norms[1], norms[2], norms[3]
    n_dp = lax.axis_size("dp")
    part, qkv_cols = w_qkv.shape
    out_cols = w_out.shape[1]
    up_cols = w_up.shape[1]
    fold = w_down.shape[0] // up_cols
    attn_stack = gather_stack(jnp.concatenate([w_qkv, w_out], 1))
    down_t = w_down.T
    ffn_stack = gather_stack(
        jnp.concatenate([w_up, *jnp.split(down_t, fold, 1)], 0)
    )
    cols_qkv = attn_stack[..., :qkv_cols].reshape(n_seq, width, qkv_cols)
    full_out = (
        attn_stack[..., qkv_cols:].reshape(n_seq, width, out_cols).transpose(1, 0, 2)
    ).reshape(width, width)
    cols_up = ffn_stack[:, :, :part].reshape(n_seq, width, up_cols)
    full_down_t = (
        ffn_stack[:, :, part:]
        .reshape(n_seq, n_dp, fold, out_cols, up_cols)
        .transpose(0, 3, 1, 2, 4)
        .reshape(width, fold * n_dp * up_cols)
    )

    doc_ends = jax.vmap(running_total)(lengths[:, 0])
    k_place = (
        slot_order[:, 0, :, None] * tok_dev + jnp.arange(tok_dev, dtype=jnp.int32)
    ).reshape(micro_count, n_seq * tok_dev)
    k_segment = jax.vmap(segment_of)(k_place, doc_ends)
    base_slot = lax.dynamic_slice_in_dim(slot_order[:, 0], my_slot, 1, 1)
    q_place = base_slot * tok_dev + jnp.arange(tok_dev, dtype=jnp.int32)
    q_segment = jax.vmap(segment_of)(q_place, doc_ends)
    allowed = (q_segment[:, :, None] == k_segment[:, None, :]) & (
        k_place[:, None, :] <= q_place[:, :, None]
    )

    residual = tokens.astype(jnp.float32).reshape(rows, width)
    scaled_one, inv_one = normalize(residual)
    normed_one = (scaled_one * g_one + b_one).astype(bf16)
    qkv_all = apply_cols(normed_one, cols_qkv).astype(bf16)
    queries = heads_of(qkv_all[:, :width], micro_count, head_dim)
    local_kv = qkv_all[:, width:].reshape(micro_count, tok_dev, 2 * width)
    group_kv = lax.all_gather(local_kv, "seq", axis=1, tiled=True)
    keys = heads_of(group_kv[..., :width], micro_count, head_dim)
    values = heads_of(group_kv[..., width:], micro_count, head_dim)

    scores = batched(queries, keys, 3, 3) * score_scale
    scores = jnp.where(allowed[:, None], scores, -jnp.inf)
    weights = jnp.exp(scores - jnp.max(scores, -1, keepdims=True))
    probs = weights * (1.0 / jnp.sum(weights, -1, keepdims=True))
    probs_low = probs.astype(bf16)
    attended = batched(probs_low, values, 3, 2)
    attn_flat = rows_of(attended.astype(bf16))
    middle = residual + dot(attn_flat, full_out)
    scaled_two, inv_two = normalize(middle)
    normed_two = (scaled_two * g_two + b_two).astype(bf16)
    hidden = apply_cols(normed_two, cols_up)
    activated_full, gelu_back = jax.vjp(gelu_tanh, hidden)
    activated = activated_full.astype(bf16)

    grad_rows = cotangent.reshape(rows, width)
    block_out = (middle + dot_right_t(activated, full_down_t)).astype(bf16)
    grad_hidden = gelu_back(dot(grad_rows, full_down_t))[0].astype(bf16)
    sum_down_t = dot_left_t(grad_rows, activated).astype(bf16)
    sum_down_t = (
        sum_down_t.reshape(n_seq, out_cols, n_dp, fold, up_cols)
        .transpose(0, 2, 3, 1, 4)
        .reshape(n_seq, n_dp, fold * out_cols, up_cols)
    )
    sum_up = grad_cols(normed_two, grad_hidden, n_seq).astype(bf16)
    sum_ffn, _ = scatter_stack(
        jnp.concatenate([sum_up.reshape(n_seq, n_dp, part, up_cols), sum_down_t], 2), None
    )
    grad_normed_two = apply_cols_t(grad_hidden, cols_up)
    grad_middle = grad_rows.astype(jnp.float32) + norm_back(
        grad_normed_two, scaled_two, inv_two, g_two
    )
    grad_branch = grad_middle.astype(bf16)
    sum_proj = grad_cols(attn_flat, grad_branch, n_seq).astype(bf16)
    grad_heads = heads_of(
        dot_right_t(grad_branch, full_out).astype(bf16), micro_count, head_dim
    )

    grad_probs = batched(grad_heads, values, 3, 3)
    row_dot = jnp.sum(probs * grad_probs, -1, keepdims=True)
    grad_scores = (probs * (grad_probs - row_dot)).astype(bf16)
    grad_query = rows_of(batched(grad_scores, keys, 3, 2) * score_scale)
    grad_keys = rows_of(batched(grad_scores, queries, 2, 2) * score_scale)
    grad_values = rows_of(batched(probs_low, grad_heads, 2, 2))
    grad_kv = jnp.concatenate([grad_keys.astype(bf16), grad_values.astype(bf16)], 1)
    grad_kv = grad_kv.reshape(micro_count, n_seq, tok_dev, 2 * width).transpose(1, 0, 2, 3)
    grad_kv = lax.psum_scatter(
        pair_sum(grad_kv), "seq", scatter_dimension=0, axis_index_groups=same_core()
    ).reshape(rows, 2 * width)
    grad_qkv_rows = jnp.concatenate([grad_query.astype(bf16), grad_kv], 1)
    sum_qkv = grad_cols(normed_one, grad_qkv_rows, n_seq).astype(bf16)
    sum_attn, sum_ffn = scatter_stack(
        jnp.concatenate([sum_qkv, sum_proj], 2).reshape(n_seq, n_dp, part, qkv_cols + out_cols),
        sum_ffn,
    )
    sum_attn = sum_attn.astype(jnp.float32)
    sum_ffn = sum_ffn.astype(jnp.float32)
    out_up = sum_ffn[:part]
    out_down = jnp.concatenate(jnp.split(sum_ffn[part:], fold, 0), 1).T
    out_qkv = sum_attn[:, :qkv_cols]
    out_proj = sum_attn[:, qkv_cols:]
    grad_normed_one = apply_cols_t(grad_qkv_rows, cols_qkv)
    grad_input = (
        grad_middle + norm_back(grad_normed_one, scaled_one, inv_one, g_one)
    ).astype(bf16)

    norm_sums = jnp.stack(
        [
            jnp.sum(grad_normed_one * scaled_one, 0),
            jnp.sum(grad_normed_one, 0),
            jnp.sum(grad_normed_two * scaled_two, 0),
            jnp.sum(grad_normed_two, 0),
        ]
    )
    norm_totals = lax.psum(norm_sums, ("dp", "seq"))
    norm_mine = lax.dynamic_slice_in_dim(norm_totals, lax.axis_index("dp") * part, part, 1)
    return (
        block_out.reshape(tokens.shape),
        grad_input.reshape(tokens.shape),
        out_qkv,
        out_proj,
        out_up,
        out_down,
        norm_mine[0],
        norm_mine[1],
        norm_mine[2],
        norm_mine[3],
    )


MESH = pl.DeviceIdType.MESH
ORDERS = ((2, 0, 3, 1), (2, 1, 3, 0), (3, 0, 2, 1), (3, 1, 2, 0))
ROW_CUTS = ((0, 64), (64, 64), (128, 64), (192, 80))
CHUNKS = tuple((q, r) for pair in ((0, 1), (2, 3)) for r in range(4) for q in pair)
GATHER_LAGS = (0, 1, 2, 3, 5)
SCATTER_LAGS = (0, 2, 3, 4, 6)
TILE = 128
LANES = (3 * TILE, 3 * TILE, 3 * TILE, 4 * TILE)
UNITS = 5
REM_UP, REM_QKV, REM_OUT, REM_DOWN, REM_NORM = 0, 32, 56, 64, 96


def place_of(q, dp, seq):
    z = seq // 2
    bits = (dp % 2, dp // 2, (z % 2 + z // 2) % 2, z // 2)
    return sum(bits[dim] * 2**k for k, dim in enumerate(ORDERS[q]))


def partner(dim):
    dp, seq = lax.axis_index("dp"), lax.axis_index("seq")
    z, core = seq // 2, seq % 2
    if dim == 0:
        return (dp + 1 - 2 * (dp % 2), seq)
    if dim == 1:
        return (dp + 2 - 4 * (dp // 2), seq)
    if dim == 2:
        return (dp, (z + 1 - 2 * (z % 2)) * 2 + core)
    return (dp, (3 - z) * 2 + core)


def sibling():
    dp, seq = lax.axis_index("dp"), lax.axis_index("seq")
    return (dp, seq + 1 - 2 * (seq % 2))


def greet(devices):
    barrier = pltpu.get_barrier_semaphore()
    for device in devices:
        pl.semaphore_signal(barrier, inc=1, device_id=device, device_id_type=MESH)
    pl.semaphore_wait(barrier, len(devices))


def send(src, dst, send_sem, recv_sem, device):
    copy = pltpu.make_async_remote_copy(
        src_ref=src, dst_ref=dst, send_sem=send_sem, recv_sem=recv_sem,
        device_id=device, device_id_type=MESH,
    )
    copy.start()
    return copy


def gather_kernel(*refs):
    shards_in, full = refs[:4], refs[4:8]
    own_sem, link_send, link_recv, sib_send, sib_recv = refs[8:]
    dp, seq = lax.axis_index("dp"), lax.axis_index("seq")
    core = seq % 2
    greet([partner(dim) for dim in range(4)] + [sibling()])
    at = [place_of(q, dp, seq) for q in range(4)]
    owns, links, sides = {}, {}, []

    def step(chunk, stage):
        q, r = CHUNKS[chunk]
        span = pl.ds(*ROW_CUTS[r])
        size = 2**stage
        if stage == 0:
            fresh, target = shards_in[q].at[span], full[q].at[core, at[q], span]
            links[chunk] = send(
                fresh, target, link_send.at[chunk, 0], link_recv.at[chunk, 0],
                partner(ORDERS[q][0]),
            )
            owns[chunk] = pltpu.make_async_copy(fresh, target, own_sem.at[chunk])
            owns[chunk].start()
            sides.append(
                send(fresh, target, sib_send.at[chunk, 0], sib_recv.at[chunk, 0], sibling())
            )
            return
        links[chunk].wait()
        if stage == 1:
            owns[chunk].wait()
        if stage < 4:
            held = full[q].at[core, pl.ds(at[q] // size * size, size), span]
            links[chunk] = send(
                held, held, link_send.at[chunk, stage], link_recv.at[chunk, stage],
                partner(ORDERS[q][stage]),
            )
        half = size // 2
        mine = at[q] // half
        got = full[q].at[core, pl.ds((mine + 1 - 2 * (mine % 2)) * half, half), span]
        sides.append(
            send(got, got, sib_send.at[chunk, stage], sib_recv.at[chunk, stage], sibling())
        )

    for turn in range(len(CHUNKS) + GATHER_LAGS[4]):
        for stage in (4, 3, 2, 1, 0):
            lag = GATHER_LAGS[stage]
            if 0 <= turn - lag < len(CHUNKS):
                step(turn - lag, stage)
    for side in sides:
        side.wait()


def gather_weights(chunks):
    rows = chunks[0].shape[0]
    anywhere = pl.BlockSpec(memory_space=pl.ANY)
    dma = pltpu.SemaphoreType.DMA
    return pl.pallas_call(
        gather_kernel,
        out_shape=[jax.ShapeDtypeStruct((2, 16, rows, lanes), jnp.bfloat16) for lanes in LANES],
        in_specs=[anywhere] * 4,
        out_specs=[anywhere] * 4,
        scratch_shapes=[dma((16,)), dma((16, 4)), dma((16, 4)), dma((16, 5)), dma((16, 5))],
        compiler_params=pltpu.CompilerParams(collective_id=0, has_side_effects=True),
        name="gather_weights",
    )(*chunks)


def scatter_kernel(*refs):
    parts, outs = refs[:4], refs[4:8]
    own, acc, got3, got2, got1, got0 = (refs[8 + 4 * i : 12 + 4 * i] for i in range(6))
    got = (got0, got1, got2, got3)
    own_sem, link_send, link_recv, sib_send, sib_recv = refs[32:]
    dp, seq = lax.axis_index("dp"), lax.axis_index("seq")
    core = seq % 2
    greet([partner(dim) for dim in range(4)] + [sibling()])
    at = [place_of(q, dp, seq) for q in range(4)]
    side, load, links = {}, {}, {}
    for chunk, (q, r) in enumerate(CHUNKS):
        rows = pl.ds(*ROW_CUTS[r])
        side[chunk] = send(
            parts[q].at[1 - core, :, rows], acc[q].at[:, rows],
            sib_send.at[chunk], sib_recv.at[chunk], sibling(),
        )
        load[chunk] = pltpu.make_async_copy(
            parts[q].at[core, :, rows], own[q].at[:, rows], own_sem.at[chunk]
        )
        load[chunk].start()

    def add(chunk, base, other, other_base, count):
        q, r = CHUNKS[chunk]
        rows = pl.ds(*ROW_CUTS[r])

        def one(b, carry):
            acc[q][base + b, rows] = acc[q][base + b, rows] + other[other_base + b, rows]
            return carry

        lax.fori_loop(0, count, one, 0)

    def step(chunk, stage):
        q, r = CHUNKS[chunk]
        rows = pl.ds(*ROW_CUTS[r])
        half = 2**stage
        base = at[q] // (2 * half) * (2 * half)
        high = at[q] // half % 2
        away, keep = (1 - high) * half, high * half
        if stage == 3:
            side[chunk].wait_recv()
            load[chunk].wait()
            other = own[q]
        else:
            links[chunk, stage + 1].wait_recv()
            other = got[stage + 1][q]
        add(chunk, base + away, other, away, half)
        links[chunk, stage] = send(
            acc[q].at[pl.ds(base + away, half), rows], got[stage][q].at[:, rows],
            link_send.at[chunk, stage], link_recv.at[chunk, stage], partner(ORDERS[q][stage]),
        )
        add(chunk, base + keep, other, keep, half)

    for turn in range(len(CHUNKS) + SCATTER_LAGS[4]):
        for stage in (-1, 0, 1, 2, 3):
            lag = SCATTER_LAGS[3 - stage]
            chunk = turn - lag
            if 0 <= chunk < len(CHUNKS):
                if stage >= 0:
                    step(chunk, stage)
                    continue
                q, r = CHUNKS[chunk]
                rows = pl.ds(*ROW_CUTS[r])
                links[chunk, 0].wait_recv()
                outs[q][rows] = acc[q][at[q], rows] + got0[q][0, rows]
    for copy in list(side.values()) + list(links.values()):
        copy.wait_send()


def scatter_grads(parts):
    rows = parts[0].shape[2]
    dma = pltpu.SemaphoreType.DMA
    bf16 = jnp.bfloat16
    buffers = [
        pltpu.VMEM((count, rows, lanes), bf16) for count in (16, 16, 8, 4, 2, 1) for lanes in LANES
    ]
    return pl.pallas_call(
        scatter_kernel,
        out_shape=[jax.ShapeDtypeStruct((rows, lanes), bf16) for lanes in LANES],
        in_specs=[pl.BlockSpec(memory_space=pl.ANY)] * 4,
        out_specs=[pl.BlockSpec(memory_space=pltpu.VMEM)] * 4,
        scratch_shapes=buffers + [dma((16,)), dma((16, 4)), dma((16, 4)), dma((16,)), dma((16,))],
        compiler_params=pltpu.CompilerParams(
            collective_id=1, has_side_effects=True, vmem_limit_bytes=56 * 2**20
        ),
        name="scatter_grads",
    )(*parts)


def exchange_kernel(blocks, out, own_sem, send_sem, recv_sem):
    dp, seq = lax.axis_index("dp"), lax.axis_index("seq")
    others = [(dp, (seq + k) % 8) for k in range(1, 8)]
    greet(others)
    own = pltpu.make_async_copy(blocks.at[seq], out.at[seq], own_sem)
    copies = [
        send(blocks.at[device[1]], out.at[seq], send_sem.at[k], recv_sem.at[k], device)
        for k, device in enumerate(others)
    ]
    own.start()
    own.wait()
    for copy in copies:
        copy.wait()


def exchange(blocks, which):
    dma = pltpu.SemaphoreType.DMA
    return pl.pallas_call(
        exchange_kernel,
        out_shape=jax.ShapeDtypeStruct(blocks.shape, blocks.dtype),
        in_specs=[pl.BlockSpec(memory_space=pl.ANY)],
        out_specs=pl.BlockSpec(memory_space=pl.ANY),
        scratch_shapes=[dma, dma((7,)), dma((7,))],
        compiler_params=pltpu.CompilerParams(collective_id=2 + which, has_side_effects=True),
        name=f"exchange_{which}",
    )(blocks)


def spots():
    for dp in range(4):
        for seq in range(8):
            yield dp, seq, seq % 2, [place_of(q, dp, seq) for q in range(4)]


def unpack_kernel(c0, c1, c2, c3, qkv, out, up, down, norms):
    for dp in range(4):
        pieces = [[] for _ in range(7)]
        for s in range(8):
            at = [place_of(q, dp, s) for q in range(4)]
            core = s % 2
            rem = c1[core, at[1], :, TILE : 2 * TILE]
            if s == 0:
                norms[dp] = rem
            pieces[0] += [c0[core, at[0]], rem[:, REM_QKV : REM_QKV + 24]]
            pieces[1] += [c1[core, at[1], :, :TILE], rem[:, REM_OUT : REM_OUT + 8]]
            pieces[2] += [
                c1[core, at[1], :, 2 * TILE :], c2[core, at[2]], rem[:, REM_UP : REM_UP + 32]
            ]
            for i in range(4):
                pieces[3 + i] += [
                    c3[core, at[3], :, i * TILE : (i + 1) * TILE],
                    rem[:, REM_DOWN + 8 * i : REM_DOWN + 8 * i + 8],
                ]
        qkv[dp] = jnp.concatenate(pieces[0], 1)
        out[dp] = jnp.concatenate(pieces[1], 1)
        up[dp] = jnp.concatenate(pieces[2], 1)
        for i in range(4):
            down[dp * 4 + i] = jnp.concatenate(pieces[3 + i], 1)


def unpack_weights(chunks):
    bf16 = jnp.bfloat16
    rows, step = chunks[0].shape[2], 16

    def spec(count, lanes):
        return pl.BlockSpec((count, step, lanes), lambda i: (0, i, 0))

    sizes = ((4, 3264), (4, 1088), (4, 4352), (16, 1088), (4, 128))
    return pl.pallas_call(
        unpack_kernel,
        grid=(rows // step,),
        out_shape=[jax.ShapeDtypeStruct((count, rows, lanes), bf16) for count, lanes in sizes],
        in_specs=[pl.BlockSpec((2, 16, step, lanes), lambda i: (0, 0, i, 0)) for lanes in LANES],
        out_specs=[spec(*size) for size in sizes],
        compiler_params=pltpu.CompilerParams(vmem_limit_bytes=40 * 2**20),
        name="unpack_weights",
    )(*chunks)


def pack_kernel(qkv, out, up, down, norms, c0, c1, c2, c3):
    for dp, s, core, at in spots():
        c0[core, at[0]] = qkv[dp, :, s * 408 : s * 408 + 384]
        c1[core, at[1], :, :TILE] = out[dp, :, s * 136 : s * 136 + 128]
        c1[core, at[1], :, 2 * TILE :] = up[dp, :, s * 544 : s * 544 + 128]
        c2[core, at[2]] = up[dp, :, s * 544 + 128 : s * 544 + 512]
        base = at[1]
        c1[core, base, :, TILE : 2 * TILE] = norms[dp]
        c1[core, base, :, TILE + REM_UP : TILE + REM_UP + 32] = up[dp, :, s * 544 + 512 : s * 544 + 544]
        c1[core, base, :, TILE + REM_QKV : TILE + REM_QKV + 24] = qkv[dp, :, s * 408 + 384 : s * 408 + 408]
        c1[core, base, :, TILE + REM_OUT : TILE + REM_OUT + 8] = out[dp, :, s * 136 + 128 : s * 136 + 136]
        for i in range(4):
            c3[core, at[3], :, i * TILE : (i + 1) * TILE] = down[dp * 4 + i, :, s * 136 : s * 136 + 128]
            spot = TILE + REM_DOWN + 8 * i
            c1[core, base, :, spot : spot + 8] = down[dp * 4 + i, :, s * 136 + 128 : s * 136 + 136]


def pack_grads(qkv, out, up, down, norms):
    rows, step = qkv.shape[1], 16

    def spec(count, lanes):
        return pl.BlockSpec((count, step, lanes), lambda i: (0, i, 0))

    return pl.pallas_call(
        pack_kernel,
        grid=(rows // step,),
        out_shape=[jax.ShapeDtypeStruct((2, 16, rows, lanes), jnp.bfloat16) for lanes in LANES],
        in_specs=[spec(4, 3264), spec(4, 1088), spec(4, 4352), spec(16, 1088), spec(4, 128)],
        out_specs=[pl.BlockSpec((2, 16, step, lanes), lambda i: (0, 0, i, 0)) for lanes in LANES],
        compiler_params=pltpu.CompilerParams(vmem_limit_bytes=40 * 2**20),
        name="pack_grads",
    )(qkv, out, up, down, norms)


QUERY_BLOCK = 256


def flip(block):
    return block.astype(jnp.float32).T.astype(jnp.bfloat16)


def masked_scores(k_rows, q_cols, seg_k, seg_q, start, scale):
    count, width = k_rows.shape[0], q_cols.shape[1]
    scores = dot(k_rows, q_cols) * scale
    key_at = lax.broadcasted_iota(jnp.int32, (count, width), 0)
    query_at = lax.broadcasted_iota(jnp.int32, (count, width), 1) + start
    return jnp.where((seg_k == seg_q) & (key_at <= query_at), scores, -1e30)


def attend_kernel(scale, order, x, seg_k, seg_q, out, lse, q_t, k_t, v_t, o_t):
    unit = pl.program_id(0)
    slots = x.shape[0]
    tok = x.shape[3]
    depth = q_t.shape[0]
    for b in range(slots):
        at = order[unit, b]
        for n, held in enumerate((q_t, k_t, v_t)):
            held[:, b * tok : (b + 1) * tok] = x[at, 0, n * depth : (n + 1) * depth]
    keys = flip(k_t[...])
    for start in range(0, slots * tok, QUERY_BLOCK):
        count = start + QUERY_BLOCK
        cols = slice(start, count)
        scores = masked_scores(
            keys[:count], q_t[:, cols], seg_k[0, :count], seg_q[0, :, cols], start, scale
        )
        top = jnp.max(scores, 0, keepdims=True)
        weights = jnp.exp(scores - top)
        total = jnp.sum(weights, 0, keepdims=True)
        probs = (weights * (1.0 / total)).astype(jnp.bfloat16)
        o_t[:, cols] = dot(v_t[:, :count], probs).astype(jnp.bfloat16)
        lse[0, :, cols] = top + jnp.log(total)
    for b in range(slots):
        out[order[unit, b], 0] = o_t[:, b * tok : (b + 1) * tok]


def attend(x, order, seg_k, seg_q, scale):
    slots, units, depth3, tok = x.shape
    depth, length = depth3 // 3, slots * tok
    bf16 = jnp.bfloat16
    held = [pltpu.VMEM((depth, length), bf16)] * 4
    return pl.pallas_call(
        functools.partial(attend_kernel, scale),
        grid_spec=pltpu.PrefetchScalarGridSpec(
            num_scalar_prefetch=1,
            grid=(units,),
            in_specs=[
                pl.BlockSpec((slots, 1, depth3, tok), lambda u, o: (0, u, 0, 0)),
                pl.BlockSpec((1, length, 1), lambda u, o: (u, 0, 0)),
                pl.BlockSpec((1, 1, length), lambda u, o: (u, 0, 0)),
            ],
            out_specs=[
                pl.BlockSpec((slots, 1, depth, tok), lambda u, o: (0, u, 0, 0)),
                pl.BlockSpec((1, 1, length), lambda u, o: (u, 0, 0)),
            ],
            scratch_shapes=held,
        ),
        out_shape=[
            jax.ShapeDtypeStruct((slots, units, depth, tok), bf16),
            jax.ShapeDtypeStruct((units, 1, length), jnp.float32),
        ],
        compiler_params=pltpu.CompilerParams(vmem_limit_bytes=40 * 2**20),
        name="attend",
    )(order, x, seg_k, seg_q)


def attend_back_kernel(
    scale, order, x, g, seg_k, seg_q, lse, out, q_t, k_t, v_t, g_t, dq_t, dk_t, dv_t
):
    unit = pl.program_id(0)
    slots = x.shape[0]
    tok = x.shape[3]
    depth = q_t.shape[0]
    for b in range(slots):
        at = order[unit, b]
        for n, held in enumerate((q_t, k_t, v_t)):
            held[:, b * tok : (b + 1) * tok] = x[at, 0, n * depth : (n + 1) * depth]
        g_t[:, b * tok : (b + 1) * tok] = g[at, 0]
    keys = flip(k_t[...])
    values = flip(v_t[...])
    length = slots * tok
    for start in reversed(range(0, length, QUERY_BLOCK)):
        count = start + QUERY_BLOCK
        cols = slice(start, count)
        queries, grads = q_t[:, cols], g_t[:, cols]
        scores = masked_scores(
            keys[:count], queries, seg_k[0, :count], seg_q[0, :, cols], start, scale
        )
        probs = jnp.exp(scores - lse[0, :, cols])
        grad_probs = dot(values[:count], grads)
        row_dot = jnp.sum(probs * grad_probs, 0, keepdims=True)
        grad_scores = (probs * (grad_probs - row_dot)).astype(jnp.bfloat16)
        probs_low = probs.astype(jnp.bfloat16)
        dq_t[:, cols] = dot(k_t[:, :count], grad_scores) * scale
        dk = dot_right_t(queries, grad_scores)
        dv = dot_right_t(grads, probs_low)
        if count == length:
            dk_t[...] = dk
            dv_t[...] = dv
        else:
            dk_t[:, :count] += dk
            dv_t[:, :count] += dv
    for b in range(slots):
        at = order[unit, b]
        cols = slice(b * tok, (b + 1) * tok)
        out[at, 0, :depth] = dq_t[:, cols].astype(jnp.bfloat16)
        out[at, 0, depth : 2 * depth] = (dk_t[:, cols] * scale).astype(jnp.bfloat16)
        out[at, 0, 2 * depth :] = dv_t[:, cols].astype(jnp.bfloat16)


def attend_back(x, g, order, seg_k, seg_q, lse, scale):
    slots, units, depth3, tok = x.shape
    depth, length = depth3 // 3, slots * tok
    bf16 = jnp.bfloat16
    held = [pltpu.VMEM((depth, length), bf16)] * 4 + [pltpu.VMEM((depth, length), jnp.float32)] * 3
    return pl.pallas_call(
        functools.partial(attend_back_kernel, scale),
        grid_spec=pltpu.PrefetchScalarGridSpec(
            num_scalar_prefetch=1,
            grid=(units,),
            in_specs=[
                pl.BlockSpec((slots, 1, depth3, tok), lambda u, o: (0, u, 0, 0)),
                pl.BlockSpec((slots, 1, depth, tok), lambda u, o: (0, u, 0, 0)),
                pl.BlockSpec((1, length, 1), lambda u, o: (u, 0, 0)),
                pl.BlockSpec((1, 1, length), lambda u, o: (u, 0, 0)),
                pl.BlockSpec((1, 1, length), lambda u, o: (u, 0, 0)),
            ],
            out_specs=pl.BlockSpec((slots, 1, depth3, tok), lambda u, o: (0, u, 0, 0)),
            scratch_shapes=held,
        ),
        out_shape=jax.ShapeDtypeStruct(x.shape, bf16),
        compiler_params=pltpu.CompilerParams(vmem_limit_bytes=48 * 2**20),
        name="attend_back",
    )(order, x, g, seg_k, seg_q, lse)


def to_units(flat, micro_count, kinds):
    tok = flat.shape[1] // micro_count
    units = flat.reshape(kinds, HEADS, -1, micro_count, tok).transpose(3, 1, 0, 2, 4)
    units = units.reshape(micro_count * HEADS, -1, tok)
    units = jnp.pad(units, ((0, 8 * UNITS - units.shape[0]), (0, 0), (0, 0)))
    return units.reshape(8, UNITS, -1, tok)


def from_units(units, micro_count, kinds):
    tok = units.shape[3]
    held = units.reshape(8 * UNITS, -1, tok)[: micro_count * HEADS]
    held = held.reshape(micro_count, HEADS, kinds, -1, tok).transpose(0, 4, 2, 1, 3)
    return held.reshape(micro_count * tok, -1)


def shards_fast(
    tokens,
    cotangent,
    w_qkv,
    w_out,
    w_up,
    w_down,
    gain_one,
    bias_one,
    gain_two,
    bias_two,
    lengths,
    slot_order,
):
    micro_count, tok_dev, width = tokens.shape
    rows = micro_count * tok_dev
    scale = (width // HEADS) ** (-0.5)
    bf16, f32 = jnp.bfloat16, jnp.float32
    part = w_qkv.shape[0]
    my_slot = lax.axis_index("seq")

    downs = [w_down[i * part : (i + 1) * part] for i in range(4)]
    norms = jnp.stack([gain_one, bias_one, gain_two, bias_two], 1)
    rem = jnp.concatenate(
        [w_up[:, 512:], w_qkv[:, 384:], w_out[:, 128:]]
        + [down[:, 128:] for down in downs]
        + [norms, jnp.zeros((part, 28), bf16)],
        1,
    )
    gathered = gather_weights(
        [
            w_qkv[:, :384],
            jnp.concatenate([w_out[:, :128], rem, w_up[:, :128]], 1),
            w_up[:, 128:512],
            jnp.concatenate([down[:, :128] for down in downs], 1),
        ]
    )
    full_qkv, full_out, full_up, full_down, full_norms = unpack_weights(gathered)
    full_qkv = full_qkv.reshape(width, -1)
    full_out = full_out.reshape(width, width)
    full_up = full_up.reshape(width, -1)
    full_down = full_down.reshape(-1, width)
    norm_rows = full_norms[:, :, REM_NORM : REM_NORM + 4].reshape(width, 4).T.astype(f32)
    g_one, b_one, g_two, b_two = norm_rows[0], norm_rows[1], norm_rows[2], norm_rows[3]

    unit_ids = my_slot * UNITS + jnp.arange(UNITS, dtype=jnp.int32)
    second = (unit_ids >= HEADS)[:, None]
    doc_ends = jax.vmap(running_total)(lengths[:, 0])
    places = jnp.arange(8 * tok_dev, dtype=jnp.int32)
    segments = jax.vmap(segment_of, (None, 0))(places, doc_ends)
    unit_segments = jnp.where(second, segments[1][None], segments[0][None])
    seg_k, seg_q = unit_segments[:, :, None], unit_segments[:, None, :]
    slots = jnp.arange(8, dtype=jnp.int32)
    holders = jnp.sum(
        jnp.where(slot_order[:, 0][:, None, :] == slots[None, :, None], slots[None, None, :], 0), 2
    )
    order = jnp.where(second, holders[1][None], holders[0][None])

    residual = tokens.astype(f32).reshape(rows, width)
    scaled_one, inv_one = normalize(residual)
    normed_one = (scaled_one * g_one + b_one).astype(bf16)
    qkv_t = lax.dot_general(
        full_qkv, normed_one, (((0,), (1,)), ((), ())), preferred_element_type=f32
    ).astype(bf16)
    unit_qkv = exchange(to_units(qkv_t, micro_count, 3), 0)
    unit_out, lse = attend(unit_qkv, order, seg_k, seg_q, scale)
    attn_flat = from_units(exchange(unit_out, 1), micro_count, 1)
    middle = residual + dot(attn_flat, full_out)
    scaled_two, inv_two = normalize(middle)
    normed_two = (scaled_two * g_two + b_two).astype(bf16)
    hidden = dot(normed_two, full_up)
    activated_full, gelu_back = jax.vjp(gelu_tanh, hidden)
    activated = activated_full.astype(bf16)

    grad_rows = cotangent.reshape(rows, width)
    block_out = (middle + dot(activated, full_down)).astype(bf16)
    grad_hidden = gelu_back(dot_right_t(grad_rows, full_down))[0].astype(bf16)
    sum_down = dot_left_t(activated, grad_rows).astype(bf16)
    sum_up = dot_left_t(normed_two, grad_hidden).astype(bf16)
    grad_normed_two = dot_right_t(grad_hidden, full_up)
    grad_middle = grad_rows.astype(f32) + norm_back(grad_normed_two, scaled_two, inv_two, g_two)
    grad_branch = grad_middle.astype(bf16)
    sum_proj = dot_left_t(attn_flat, grad_branch).astype(bf16)
    grad_heads_t = dot_right_t(full_out, grad_branch).astype(bf16)
    unit_grad = exchange(to_units(grad_heads_t, micro_count, 1), 2)
    unit_back = attend_back(unit_qkv, unit_grad, order, seg_k, seg_q, lse, scale)
    grad_qkv_rows = from_units(exchange(unit_back, 3), micro_count, 3)
    sum_qkv = dot_left_t(normed_one, grad_qkv_rows).astype(bf16)
    grad_normed_one = dot_right_t(grad_qkv_rows, full_qkv)
    grad_input = (
        grad_middle + norm_back(grad_normed_one, scaled_one, inv_one, g_one)
    ).astype(bf16)

    norm_sums = jnp.stack(
        [
            jnp.sum(grad_normed_one * scaled_one, 0),
            jnp.sum(grad_normed_one, 0),
            jnp.sum(grad_normed_two * scaled_two, 0),
            jnp.sum(grad_normed_two, 0),
        ]
    )
    norm_cols = jnp.pad(norm_sums.T.astype(bf16), ((0, 0), (REM_NORM, 28)))
    sum0, sum1, sum2, sum3 = (
        total.astype(f32)
        for total in scatter_grads(
            pack_grads(
                sum_qkv.reshape(4, part, -1),
                sum_proj.reshape(4, part, -1),
                sum_up.reshape(4, part, -1),
                sum_down.reshape(16, part, -1),
                norm_cols.reshape(4, part, -1),
            )
        )
    )
    rest = sum1[:, TILE : 2 * TILE]
    out_qkv = jnp.concatenate([sum0, rest[:, REM_QKV : REM_QKV + 24]], 1)
    out_proj = jnp.concatenate([sum1[:, :TILE], rest[:, REM_OUT : REM_OUT + 8]], 1)
    out_up = jnp.concatenate([sum1[:, 2 * TILE :], sum2, rest[:, REM_UP : REM_UP + 32]], 1)
    out_down = jnp.concatenate(
        [
            jnp.concatenate(
                [
                    sum3[:, i * TILE : (i + 1) * TILE],
                    rest[:, REM_DOWN + 8 * i : REM_DOWN + 8 * i + 8],
                ],
                1,
            )
            for i in range(4)
        ],
        0,
    )
    norm_mine = rest[:, REM_NORM : REM_NORM + 4].T
    return (
        block_out.reshape(tokens.shape),
        grad_input.reshape(tokens.shape),
        out_qkv,
        out_proj,
        out_up,
        out_down,
        norm_mine[0],
        norm_mine[1],
        norm_mine[2],
        norm_mine[3],
    )


def solution(mesh):
    grid = (mesh.shape["dp"], mesh.shape["seq"])
    return jax.shard_map(
        shards_fast if grid == (4, 8) else shards_plain,
        mesh=mesh,
        in_specs=(
            P(None, ("dp", "seq"), None),
            P(None, ("dp", "seq"), None),
            P("dp", "seq"),
            P("dp", "seq"),
            P("dp", "seq"),
            P("dp", "seq"),
            P("dp"),
            P("dp"),
            P("dp"),
            P("dp"),
            P(None, "dp", None),
            P(None, "dp", None),
        ),
        out_specs=(
            P(None, ("dp", "seq"), None),
            P(None, ("dp", "seq"), None),
            P("dp", "seq"),
            P("dp", "seq"),
            P("dp", "seq"),
            P("dp", "seq"),
            P("dp"),
            P("dp"),
            P("dp"),
            P("dp"),
        ),
        check_vma=False,
    )
```

```python
import functools

import jax
import jax.numpy as jnp
from jax import lax
from jax.experimental import pallas as pl
from jax.experimental.pallas import tpu as pltpu
from jax.sharding import PartitionSpec as P

HEADS = 17


EPS = 1e-05
GELU_C = 0.7978845608028654


def gelu_tanh(values):
    return 0.5 * values * (1.0 + jnp.tanh(GELU_C * (values + 0.044715 * values * values * values)))


def normalize(residual):
    row_mean = jnp.mean(residual, -1, keepdims=True)
    centered = residual - row_mean
    inv_std = lax.rsqrt(jnp.mean(centered * centered, -1, keepdims=True) + EPS)
    return (centered * inv_std, inv_std)


def norm_back(grad_normed, scaled, inv_std, gain_row):
    grad_scaled = grad_normed * gain_row
    return inv_std * (
        grad_scaled
        - jnp.mean(grad_scaled, -1, keepdims=True)
        - scaled * jnp.mean(grad_scaled * scaled, -1, keepdims=True)
    )


def running_total(counts):
    index = jnp.arange(counts.shape[0], dtype=jnp.int32)
    return jnp.sum(jnp.where(index[None, :] <= index[:, None], counts[None, :], 0), 1)


def segment_of(places, doc_ends):
    return jnp.sum((places[:, None] >= doc_ends[None, :]).astype(jnp.int32), 1)


def pair_swap(block):
    route = [(i, i ^ 1) for i in range(lax.axis_size("seq"))]
    return lax.ppermute(block, "seq", route)


def same_core():
    n_seq = lax.axis_size("seq")
    return [list(range(core, n_seq, 2)) for core in range(2)]


def gather_stack(shard):
    chips = lax.all_gather(shard, "seq", axis_index_groups=same_core())
    held = lax.all_gather(chips, "dp")
    other = pair_swap(held)
    first = lax.axis_index("seq") % 2 == 0
    both = jnp.stack([jnp.where(first, held, other), jnp.where(first, other, held)], 2)
    dp, chip_count = held.shape[:2]
    return both.transpose(1, 2, 0, 3, 4).reshape(2 * chip_count, dp, *shard.shape)


def pair_sum(parts):
    pairs = parts.reshape(parts.shape[0] // 2, 2, *parts.shape[1:])
    first = lax.axis_index("seq") % 2 == 0
    mine = jnp.where(first, pairs[:, 0], pairs[:, 1])
    other = jnp.where(first, pairs[:, 1], pairs[:, 0])
    got = pair_swap(other)
    return (mine.astype(jnp.float32) + got.astype(jnp.float32)).astype(jnp.bfloat16)


def scatter_stack(parts, after):
    held = pair_sum(parts).transpose(1, 0, 2, 3).reshape(-1, parts.shape[3])
    if after is not None:
        held, after = lax.optimization_barrier((held, after))
    held = lax.psum_scatter(held, "dp", scatter_dimension=0, tiled=True)
    held = lax.psum_scatter(
        held, "seq", scatter_dimension=0, axis_index_groups=same_core(), tiled=True
    )
    return held, after


def dot(left, right):
    return jnp.dot(left, right, preferred_element_type=jnp.float32)


def dot_right_t(left, right):
    return lax.dot_general(left, right, (((1,), (1,)), ((), ())), preferred_element_type=jnp.float32)


def dot_left_t(left, right):
    return lax.dot_general(left, right, (((0,), (0,)), ((), ())), preferred_element_type=jnp.float32)


def cols_of(rows, count):
    return rows.reshape(rows.shape[0], count, -1).transpose(1, 0, 2)


def apply_cols(rows, cols):
    lifted = jnp.broadcast_to(rows[None], (cols.shape[0],) + rows.shape)
    made = lax.dot_general(
        lifted, cols, (((2,), (1,)), ((0,), (0,))), preferred_element_type=jnp.float32
    )
    return made.transpose(1, 0, 2).reshape(rows.shape[0], -1)


def apply_cols_t(rows, cols):
    lifted = cols_of(rows, cols.shape[0])
    return lax.dot_general(
        lifted, cols, (((0, 2), (0, 2)), ((), ())), preferred_element_type=jnp.float32
    )


def grad_cols(left, right, count):
    lifted = jnp.broadcast_to(left[None], (count,) + left.shape)
    return lax.dot_general(
        lifted, cols_of(right, count), (((1,), (1,)), ((0,), (0,))),
        preferred_element_type=jnp.float32,
    )


def heads_of(rows, micro_count, head_dim):
    return rows.reshape(micro_count, -1, HEADS, head_dim).transpose(0, 2, 1, 3)


def rows_of(heads):
    micro_count, _, slots, head_dim = heads.shape
    return heads.transpose(0, 2, 1, 3).reshape(micro_count * slots, HEADS * head_dim)


def batched(left, right, left_dim, right_dim):
    return lax.dot_general(
        left,
        right,
        (((left_dim,), (right_dim,)), ((0, 1), (0, 1))),
        preferred_element_type=jnp.float32,
    )


def shards_plain(
    tokens,
    cotangent,
    w_qkv,
    w_out,
    w_up,
    w_down,
    gain_one,
    bias_one,
    gain_two,
    bias_two,
    lengths,
    slot_order,
):
    micro_count, tok_dev, width = tokens.shape
    rows = micro_count * tok_dev
    head_dim = width // HEADS
    score_scale = head_dim ** (-0.5)
    n_seq = lax.axis_size("seq")
    my_slot = lax.axis_index("seq")
    bf16 = jnp.bfloat16

    norms = lax.all_gather(
        jnp.stack([gain_one, bias_one, gain_two, bias_two]), "dp", axis=1, tiled=True
    ).astype(jnp.float32)
    g_one, b_one, g_two, b_two = norms[0], norms[1], norms[2], norms[3]
    n_dp = lax.axis_size("dp")
    part, qkv_cols = w_qkv.shape
    out_cols = w_out.shape[1]
    up_cols = w_up.shape[1]
    fold = w_down.shape[0] // up_cols
    attn_stack = gather_stack(jnp.concatenate([w_qkv, w_out], 1))
    down_t = w_down.T
    ffn_stack = gather_stack(
        jnp.concatenate([w_up, *jnp.split(down_t, fold, 1)], 0)
    )
    cols_qkv = attn_stack[..., :qkv_cols].reshape(n_seq, width, qkv_cols)
    full_out = (
        attn_stack[..., qkv_cols:].reshape(n_seq, width, out_cols).transpose(1, 0, 2)
    ).reshape(width, width)
    cols_up = ffn_stack[:, :, :part].reshape(n_seq, width, up_cols)
    full_down_t = (
        ffn_stack[:, :, part:]
        .reshape(n_seq, n_dp, fold, out_cols, up_cols)
        .transpose(0, 3, 1, 2, 4)
        .reshape(width, fold * n_dp * up_cols)
    )

    doc_ends = jax.vmap(running_total)(lengths[:, 0])
    k_place = (
        slot_order[:, 0, :, None] * tok_dev + jnp.arange(tok_dev, dtype=jnp.int32)
    ).reshape(micro_count, n_seq * tok_dev)
    k_segment = jax.vmap(segment_of)(k_place, doc_ends)
    base_slot = lax.dynamic_slice_in_dim(slot_order[:, 0], my_slot, 1, 1)
    q_place = base_slot * tok_dev + jnp.arange(tok_dev, dtype=jnp.int32)
    q_segment = jax.vmap(segment_of)(q_place, doc_ends)
    allowed = (q_segment[:, :, None] == k_segment[:, None, :]) & (
        k_place[:, None, :] <= q_place[:, :, None]
    )

    residual = tokens.astype(jnp.float32).reshape(rows, width)
    scaled_one, inv_one = normalize(residual)
    normed_one = (scaled_one * g_one + b_one).astype(bf16)
    qkv_all = apply_cols(normed_one, cols_qkv).astype(bf16)
    queries = heads_of(qkv_all[:, :width], micro_count, head_dim)
    local_kv = qkv_all[:, width:].reshape(micro_count, tok_dev, 2 * width)
    group_kv = lax.all_gather(local_kv, "seq", axis=1, tiled=True)
    keys = heads_of(group_kv[..., :width], micro_count, head_dim)
    values = heads_of(group_kv[..., width:], micro_count, head_dim)

    scores = batched(queries, keys, 3, 3) * score_scale
    scores = jnp.where(allowed[:, None], scores, -jnp.inf)
    weights = jnp.exp(scores - jnp.max(scores, -1, keepdims=True))
    probs = weights * (1.0 / jnp.sum(weights, -1, keepdims=True))
    probs_low = probs.astype(bf16)
    attended = batched(probs_low, values, 3, 2)
    attn_flat = rows_of(attended.astype(bf16))
    middle = residual + dot(attn_flat, full_out)
    scaled_two, inv_two = normalize(middle)
    normed_two = (scaled_two * g_two + b_two).astype(bf16)
    hidden = apply_cols(normed_two, cols_up)
    activated_full, gelu_back = jax.vjp(gelu_tanh, hidden)
    activated = activated_full.astype(bf16)

    grad_rows = cotangent.reshape(rows, width)
    block_out = (middle + dot_right_t(activated, full_down_t)).astype(bf16)
    grad_hidden = gelu_back(dot(grad_rows, full_down_t))[0].astype(bf16)
    sum_down_t = dot_left_t(grad_rows, activated).astype(bf16)
    sum_down_t = (
        sum_down_t.reshape(n_seq, out_cols, n_dp, fold, up_cols)
        .transpose(0, 2, 3, 1, 4)
        .reshape(n_seq, n_dp, fold * out_cols, up_cols)
    )
    sum_up = grad_cols(normed_two, grad_hidden, n_seq).astype(bf16)
    sum_ffn, _ = scatter_stack(
        jnp.concatenate([sum_up.reshape(n_seq, n_dp, part, up_cols), sum_down_t], 2), None
    )
    grad_normed_two = apply_cols_t(grad_hidden, cols_up)
    grad_middle = grad_rows.astype(jnp.float32) + norm_back(
        grad_normed_two, scaled_two, inv_two, g_two
    )
    grad_branch = grad_middle.astype(bf16)
    sum_proj = grad_cols(attn_flat, grad_branch, n_seq).astype(bf16)
    grad_heads = heads_of(
        dot_right_t(grad_branch, full_out).astype(bf16), micro_count, head_dim
    )

    grad_probs = batched(grad_heads, values, 3, 3)
    row_dot = jnp.sum(probs * grad_probs, -1, keepdims=True)
    grad_scores = (probs * (grad_probs - row_dot)).astype(bf16)
    grad_query = rows_of(batched(grad_scores, keys, 3, 2) * score_scale)
    grad_keys = rows_of(batched(grad_scores, queries, 2, 2) * score_scale)
    grad_values = rows_of(batched(probs_low, grad_heads, 2, 2))
    grad_kv = jnp.concatenate([grad_keys.astype(bf16), grad_values.astype(bf16)], 1)
    grad_kv = grad_kv.reshape(micro_count, n_seq, tok_dev, 2 * width).transpose(1, 0, 2, 3)
    grad_kv = lax.psum_scatter(
        pair_sum(grad_kv), "seq", scatter_dimension=0, axis_index_groups=same_core()
    ).reshape(rows, 2 * width)
    grad_qkv_rows = jnp.concatenate([grad_query.astype(bf16), grad_kv], 1)
    sum_qkv = grad_cols(normed_one, grad_qkv_rows, n_seq).astype(bf16)
    sum_attn, sum_ffn = scatter_stack(
        jnp.concatenate([sum_qkv, sum_proj], 2).reshape(n_seq, n_dp, part, qkv_cols + out_cols),
        sum_ffn,
    )
    sum_attn = sum_attn.astype(jnp.float32)
    sum_ffn = sum_ffn.astype(jnp.float32)
    out_up = sum_ffn[:part]
    out_down = jnp.concatenate(jnp.split(sum_ffn[part:], fold, 0), 1).T
    out_qkv = sum_attn[:, :qkv_cols]
    out_proj = sum_attn[:, qkv_cols:]
    grad_normed_one = apply_cols_t(grad_qkv_rows, cols_qkv)
    grad_input = (
        grad_middle + norm_back(grad_normed_one, scaled_one, inv_one, g_one)
    ).astype(bf16)

    norm_sums = jnp.stack(
        [
            jnp.sum(grad_normed_one * scaled_one, 0),
            jnp.sum(grad_normed_one, 0),
            jnp.sum(grad_normed_two * scaled_two, 0),
            jnp.sum(grad_normed_two, 0),
        ]
    )
    norm_totals = lax.psum(norm_sums, ("dp", "seq"))
    norm_mine = lax.dynamic_slice_in_dim(norm_totals, lax.axis_index("dp") * part, part, 1)
    return (
        block_out.reshape(tokens.shape),
        grad_input.reshape(tokens.shape),
        out_qkv,
        out_proj,
        out_up,
        out_down,
        norm_mine[0],
        norm_mine[1],
        norm_mine[2],
        norm_mine[3],
    )


MESH = pl.DeviceIdType.MESH
ORDERS = ((2, 0, 3, 1), (2, 1, 3, 0), (3, 0, 2, 1), (3, 1, 2, 0))
ROW_CUTS = ((0, 64), (64, 64), (128, 64), (192, 80))
CHUNKS = tuple((q, r) for pair in ((0, 1), (2, 3)) for r in range(4) for q in pair)
GATHER_LAGS = (0, 2, 4, 6, 9)
SCATTER_LAGS = (0, 3, 5, 7, 9)
AHEAD = 4
TILE = 128
LANES = (3 * TILE, 3 * TILE, 3 * TILE, 4 * TILE)
UNITS = 5
REM_UP, REM_QKV, REM_OUT, REM_DOWN, REM_NORM = 0, 32, 56, 64, 96


def place_of(q, dp, seq):
    z = seq // 2
    bits = (dp % 2, dp // 2, (z % 2 + z // 2) % 2, z // 2)
    return sum(bits[dim] * 2**k for k, dim in enumerate(ORDERS[q]))


def partner(dim):
    dp, seq = lax.axis_index("dp"), lax.axis_index("seq")
    z, core = seq // 2, seq % 2
    if dim == 0:
        return (dp + 1 - 2 * (dp % 2), seq)
    if dim == 1:
        return (dp + 2 - 4 * (dp // 2), seq)
    if dim == 2:
        return (dp, (z + 1 - 2 * (z % 2)) * 2 + core)
    return (dp, (3 - z) * 2 + core)


def sibling():
    dp, seq = lax.axis_index("dp"), lax.axis_index("seq")
    return (dp, seq + 1 - 2 * (seq % 2))


def greet(devices):
    barrier = pltpu.get_barrier_semaphore()
    for device in devices:
        pl.semaphore_signal(barrier, inc=1, device_id=device, device_id_type=MESH)
    pl.semaphore_wait(barrier, len(devices))


def send(src, dst, send_sem, recv_sem, device):
    copy = pltpu.make_async_remote_copy(
        src_ref=src, dst_ref=dst, send_sem=send_sem, recv_sem=recv_sem,
        device_id=device, device_id_type=MESH,
    )
    copy.start()
    return copy


def gather_kernel(*refs):
    shards_in, full = refs[:4], refs[4:8]
    own_sem, link_send, link_recv, sib_send, sib_recv = refs[8:]
    dp, seq = lax.axis_index("dp"), lax.axis_index("seq")
    core = seq % 2
    greet([partner(dim) for dim in range(4)] + [sibling()])
    at = [place_of(q, dp, seq) for q in range(4)]
    owns, links, sides = {}, {}, []

    def step(chunk, stage):
        q, r = CHUNKS[chunk]
        span = pl.ds(*ROW_CUTS[r])
        size = 2**stage
        if stage == 0:
            fresh, target = shards_in[q].at[span], full[q].at[core, at[q], span]
            links[chunk] = send(
                fresh, target, link_send.at[chunk, 0], link_recv.at[chunk, 0],
                partner(ORDERS[q][0]),
            )
            owns[chunk] = pltpu.make_async_copy(fresh, target, own_sem.at[chunk])
            owns[chunk].start()
            sides.append(
                send(fresh, target, sib_send.at[chunk, 0], sib_recv.at[chunk, 0], sibling())
            )
            return
        links[chunk].wait()
        if stage == 1:
            owns[chunk].wait()
        if stage < 4:
            held = full[q].at[core, pl.ds(at[q] // size * size, size), span]
            links[chunk] = send(
                held, held, link_send.at[chunk, stage], link_recv.at[chunk, stage],
                partner(ORDERS[q][stage]),
            )
        half = size // 2
        mine = at[q] // half
        got = full[q].at[core, pl.ds((mine + 1 - 2 * (mine % 2)) * half, half), span]
        sides.append(
            send(got, got, sib_send.at[chunk, stage], sib_recv.at[chunk, stage], sibling())
        )

    for turn in range(len(CHUNKS) + GATHER_LAGS[4]):
        for stage in (4, 3, 2, 1, 0):
            lag = GATHER_LAGS[stage]
            if 0 <= turn - lag < len(CHUNKS):
                step(turn - lag, stage)
    for side in sides:
        side.wait()


def gather_weights(chunks):
    rows = chunks[0].shape[0]
    anywhere = pl.BlockSpec(memory_space=pl.ANY)
    dma = pltpu.SemaphoreType.DMA
    return pl.pallas_call(
        gather_kernel,
        out_shape=[jax.ShapeDtypeStruct((2, 16, rows, lanes), jnp.bfloat16) for lanes in LANES],
        in_specs=[anywhere] * 4,
        out_specs=[anywhere] * 4,
        scratch_shapes=[dma((16,)), dma((16, 4)), dma((16, 4)), dma((16, 5)), dma((16, 5))],
        compiler_params=pltpu.CompilerParams(collective_id=0, has_side_effects=True),
        name="gather_weights",
    )(*chunks)


def scatter_kernel(*refs):
    parts, outs = refs[:4], refs[4:8]
    own, acc, got3, got2, got1, got0 = (refs[8 + 4 * i : 12 + 4 * i] for i in range(6))
    got = (got0, got1, got2, got3)
    own_sem, link_send, link_recv, sib_send, sib_recv = refs[32:]
    dp, seq = lax.axis_index("dp"), lax.axis_index("seq")
    core = seq % 2
    greet([partner(dim) for dim in range(4)] + [sibling()])
    at = [place_of(q, dp, seq) for q in range(4)]
    side, load, links = {}, {}, {}

    def begin(chunk):
        q, r = CHUNKS[chunk]
        rows = pl.ds(*ROW_CUTS[r])
        side[chunk] = send(
            parts[q].at[1 - core, :, rows], acc[q].at[:, rows],
            sib_send.at[chunk], sib_recv.at[chunk], sibling(),
        )
        load[chunk] = pltpu.make_async_copy(
            parts[q].at[core, :, rows], own[q].at[:, rows], own_sem.at[chunk]
        )
        load[chunk].start()

    for chunk in range(AHEAD):
        begin(chunk)

    def add(chunk, base, other, other_base, count):
        q, r = CHUNKS[chunk]
        rows = pl.ds(*ROW_CUTS[r])

        def one(b, carry):
            acc[q][base + b, rows] = acc[q][base + b, rows] + other[other_base + b, rows]
            return carry

        lax.fori_loop(0, count, one, 0)

    def step(chunk, stage):
        q, r = CHUNKS[chunk]
        rows = pl.ds(*ROW_CUTS[r])
        half = 2**stage
        base = at[q] // (2 * half) * (2 * half)
        high = at[q] // half % 2
        away, keep = (1 - high) * half, high * half
        if stage == 3:
            side[chunk].wait_recv()
            load[chunk].wait()
            other = own[q]
        else:
            links[chunk, stage + 1].wait_recv()
            other = got[stage + 1][q]
        add(chunk, base + away, other, away, half)
        links[chunk, stage] = send(
            acc[q].at[pl.ds(base + away, half), rows], got[stage][q].at[:, rows],
            link_send.at[chunk, stage], link_recv.at[chunk, stage], partner(ORDERS[q][stage]),
        )
        add(chunk, base + keep, other, keep, half)

    for turn in range(len(CHUNKS) + SCATTER_LAGS[4]):
        if turn + AHEAD < len(CHUNKS):
            begin(turn + AHEAD)
        for stage in (-1, 0, 1, 2, 3):
            lag = SCATTER_LAGS[3 - stage]
            chunk = turn - lag
            if 0 <= chunk < len(CHUNKS):
                if stage >= 0:
                    step(chunk, stage)
                    continue
                q, r = CHUNKS[chunk]
                rows = pl.ds(*ROW_CUTS[r])
                links[chunk, 0].wait_recv()
                outs[q][rows] = acc[q][at[q], rows] + got0[q][0, rows]
    for copy in list(side.values()) + list(links.values()):
        copy.wait_send()


def scatter_grads(parts):
    rows = parts[0].shape[2]
    dma = pltpu.SemaphoreType.DMA
    bf16 = jnp.bfloat16
    buffers = [
        pltpu.VMEM((count, rows, lanes), bf16) for count in (16, 16, 8, 4, 2, 1) for lanes in LANES
    ]
    return pl.pallas_call(
        scatter_kernel,
        out_shape=[jax.ShapeDtypeStruct((rows, lanes), bf16) for lanes in LANES],
        in_specs=[pl.BlockSpec(memory_space=pl.ANY)] * 4,
        out_specs=[pl.BlockSpec(memory_space=pltpu.VMEM)] * 4,
        scratch_shapes=buffers + [dma((16,)), dma((16, 4)), dma((16, 4)), dma((16,)), dma((16,))],
        compiler_params=pltpu.CompilerParams(
            collective_id=1, has_side_effects=True, vmem_limit_bytes=56 * 2**20
        ),
        name="scatter_grads",
    )(*parts)


def exchange_kernel(blocks, out, own_sem, send_sem, recv_sem):
    dp, seq = lax.axis_index("dp"), lax.axis_index("seq")
    others = [(dp, (seq + k) % 8) for k in range(1, 8)]
    greet(others)
    own = pltpu.make_async_copy(blocks.at[seq], out.at[seq], own_sem)
    copies = [
        send(blocks.at[device[1]], out.at[seq], send_sem.at[k], recv_sem.at[k], device)
        for k, device in enumerate(others)
    ]
    own.start()
    own.wait()
    for copy in copies:
        copy.wait()


def exchange(blocks, which):
    dma = pltpu.SemaphoreType.DMA
    return pl.pallas_call(
        exchange_kernel,
        out_shape=jax.ShapeDtypeStruct(blocks.shape, blocks.dtype),
        in_specs=[pl.BlockSpec(memory_space=pl.ANY)],
        out_specs=pl.BlockSpec(memory_space=pl.ANY),
        scratch_shapes=[dma, dma((7,)), dma((7,))],
        compiler_params=pltpu.CompilerParams(collective_id=2 + which, has_side_effects=True),
        name=f"exchange_{which}",
    )(blocks)


def spots():
    for dp in range(4):
        for seq in range(8):
            yield dp, seq, seq % 2, [place_of(q, dp, seq) for q in range(4)]


def unpack_kernel(c0, c1, c2, c3, qkv, out, up, down, norms):
    for dp in range(4):
        pieces = [[] for _ in range(7)]
        for s in range(8):
            at = [place_of(q, dp, s) for q in range(4)]
            core = s % 2
            rem = c1[core, at[1], :, TILE : 2 * TILE]
            if s == 0:
                norms[dp] = rem
            pieces[0] += [c0[core, at[0]], rem[:, REM_QKV : REM_QKV + 24]]
            pieces[1] += [c1[core, at[1], :, :TILE], rem[:, REM_OUT : REM_OUT + 8]]
            pieces[2] += [
                c1[core, at[1], :, 2 * TILE :], c2[core, at[2]], rem[:, REM_UP : REM_UP + 32]
            ]
            for i in range(4):
                pieces[3 + i] += [
                    c3[core, at[3], :, i * TILE : (i + 1) * TILE],
                    rem[:, REM_DOWN + 8 * i : REM_DOWN + 8 * i + 8],
                ]
        qkv[dp] = jnp.concatenate(pieces[0], 1)
        out[dp] = jnp.concatenate(pieces[1], 1)
        up[dp] = jnp.concatenate(pieces[2], 1)
        for i in range(4):
            down[dp * 4 + i] = jnp.concatenate(pieces[3 + i], 1)


def unpack_weights(chunks):
    bf16 = jnp.bfloat16
    rows, step = chunks[0].shape[2], 16

    def spec(count, lanes):
        return pl.BlockSpec((count, step, lanes), lambda i: (0, i, 0))

    sizes = ((4, 3264), (4, 1088), (4, 4352), (16, 1088), (4, 128))
    return pl.pallas_call(
        unpack_kernel,
        grid=(rows // step,),
        out_shape=[jax.ShapeDtypeStruct((count, rows, lanes), bf16) for count, lanes in sizes],
        in_specs=[pl.BlockSpec((2, 16, step, lanes), lambda i: (0, 0, i, 0)) for lanes in LANES],
        out_specs=[spec(*size) for size in sizes],
        compiler_params=pltpu.CompilerParams(vmem_limit_bytes=40 * 2**20),
        name="unpack_weights",
    )(*chunks)


def pack_kernel(qkv, out, up, down, norms, c0, c1, c2, c3):
    for dp, s, core, at in spots():
        c0[core, at[0]] = qkv[dp, :, s * 408 : s * 408 + 384]
        c1[core, at[1], :, :TILE] = out[dp, :, s * 136 : s * 136 + 128]
        c1[core, at[1], :, 2 * TILE :] = up[dp, :, s * 544 : s * 544 + 128]
        c2[core, at[2]] = up[dp, :, s * 544 + 128 : s * 544 + 512]
        base = at[1]
        c1[core, base, :, TILE : 2 * TILE] = norms[dp]
        c1[core, base, :, TILE + REM_UP : TILE + REM_UP + 32] = up[dp, :, s * 544 + 512 : s * 544 + 544]
        c1[core, base, :, TILE + REM_QKV : TILE + REM_QKV + 24] = qkv[dp, :, s * 408 + 384 : s * 408 + 408]
        c1[core, base, :, TILE + REM_OUT : TILE + REM_OUT + 8] = out[dp, :, s * 136 + 128 : s * 136 + 136]
        for i in range(4):
            c3[core, at[3], :, i * TILE : (i + 1) * TILE] = down[dp * 4 + i, :, s * 136 : s * 136 + 128]
            spot = TILE + REM_DOWN + 8 * i
            c1[core, base, :, spot : spot + 8] = down[dp * 4 + i, :, s * 136 + 128 : s * 136 + 136]


def pack_grads(qkv, out, up, down, norms):
    rows, step = qkv.shape[1], 16

    def spec(count, lanes):
        return pl.BlockSpec((count, step, lanes), lambda i: (0, i, 0))

    return pl.pallas_call(
        pack_kernel,
        grid=(rows // step,),
        out_shape=[jax.ShapeDtypeStruct((2, 16, rows, lanes), jnp.bfloat16) for lanes in LANES],
        in_specs=[spec(4, 3264), spec(4, 1088), spec(4, 4352), spec(16, 1088), spec(4, 128)],
        out_specs=[pl.BlockSpec((2, 16, step, lanes), lambda i: (0, 0, i, 0)) for lanes in LANES],
        compiler_params=pltpu.CompilerParams(vmem_limit_bytes=40 * 2**20),
        name="pack_grads",
    )(qkv, out, up, down, norms)


QUERY_BLOCK = 256


def flip(block):
    return block.astype(jnp.float32).T.astype(jnp.bfloat16)


def outer_kernel(left, right, out):
    out[...] = dot(flip(left[...]), right[...]).astype(out.dtype)


def outer(left, right):
    rows, width = left.shape
    step = 2 * TILE
    return pl.pallas_call(
        outer_kernel,
        grid=(width // step,),
        out_shape=jax.ShapeDtypeStruct((width, right.shape[1]), jnp.bfloat16),
        in_specs=[
            pl.BlockSpec((rows, step), lambda i: (0, i)),
            pl.BlockSpec(right.shape, lambda i: (0, 0)),
        ],
        out_specs=pl.BlockSpec((step, right.shape[1]), lambda i: (i, 0)),
        compiler_params=pltpu.CompilerParams(vmem_limit_bytes=24 * 2**20),
        cost_estimate=pl.CostEstimate(
            flops=2 * rows * width * right.shape[1],
            bytes_accessed=2 * width * (right.shape[1] + rows),
            transcendentals=0,
        ),
        name="outer",
    )(left, right)


def masked_scores(k_rows, q_cols, seg_k, seg_q, start, scale):
    count, width = k_rows.shape[0], q_cols.shape[1]
    scores = dot(k_rows, q_cols) * scale
    key_at = lax.broadcasted_iota(jnp.int32, (count, width), 0)
    query_at = lax.broadcasted_iota(jnp.int32, (count, width), 1) + start
    return jnp.where((seg_k == seg_q) & (key_at <= query_at), scores, -1e30)


def attend_kernel(scale, order, x, seg_k, seg_q, out, lse, q_t, k_t, v_t, o_t):
    unit = pl.program_id(0)
    slots = x.shape[0]
    tok = x.shape[3]
    depth = q_t.shape[0]
    for b in range(slots):
        at = order[unit, b]
        for n, held in enumerate((q_t, k_t, v_t)):
            held[:, b * tok : (b + 1) * tok] = x[at, 0, n * depth : (n + 1) * depth]
    keys = flip(k_t[...])
    for start in range(0, slots * tok, QUERY_BLOCK):
        count = start + QUERY_BLOCK
        cols = slice(start, count)
        scores = masked_scores(
            keys[:count], q_t[:, cols], seg_k[0, :count], seg_q[0, :, cols], start, scale
        )
        top = jnp.max(scores, 0, keepdims=True)
        weights = jnp.exp(scores - top)
        total = jnp.sum(weights, 0, keepdims=True)
        probs = (weights * (1.0 / total)).astype(jnp.bfloat16)
        o_t[:, cols] = dot(v_t[:, :count], probs).astype(jnp.bfloat16)
        lse[0, :, cols] = top + jnp.log(total)
    for b in range(slots):
        out[order[unit, b], 0] = o_t[:, b * tok : (b + 1) * tok]


def attend(x, order, seg_k, seg_q, scale):
    slots, units, depth3, tok = x.shape
    depth, length = depth3 // 3, slots * tok
    bf16 = jnp.bfloat16
    held = [pltpu.VMEM((depth, length), bf16)] * 4
    return pl.pallas_call(
        functools.partial(attend_kernel, scale),
        grid_spec=pltpu.PrefetchScalarGridSpec(
            num_scalar_prefetch=1,
            grid=(units,),
            in_specs=[
                pl.BlockSpec((slots, 1, depth3, tok), lambda u, o: (0, u, 0, 0)),
                pl.BlockSpec((1, length, 1), lambda u, o: (u, 0, 0)),
                pl.BlockSpec((1, 1, length), lambda u, o: (u, 0, 0)),
            ],
            out_specs=[
                pl.BlockSpec((slots, 1, depth, tok), lambda u, o: (0, u, 0, 0)),
                pl.BlockSpec((1, 1, length), lambda u, o: (u, 0, 0)),
            ],
            scratch_shapes=held,
        ),
        out_shape=[
            jax.ShapeDtypeStruct((slots, units, depth, tok), bf16),
            jax.ShapeDtypeStruct((units, 1, length), jnp.float32),
        ],
        compiler_params=pltpu.CompilerParams(vmem_limit_bytes=40 * 2**20),
        name="attend",
    )(order, x, seg_k, seg_q)


def attend_back_kernel(
    scale, order, x, g, seg_k, seg_q, lse, out, q_t, k_t, v_t, g_t, dq_t, dk_t, dv_t
):
    unit = pl.program_id(0)
    slots = x.shape[0]
    tok = x.shape[3]
    depth = q_t.shape[0]
    for b in range(slots):
        at = order[unit, b]
        for n, held in enumerate((q_t, k_t, v_t)):
            held[:, b * tok : (b + 1) * tok] = x[at, 0, n * depth : (n + 1) * depth]
        g_t[:, b * tok : (b + 1) * tok] = g[at, 0]
    keys = flip(k_t[...])
    values = flip(v_t[...])
    length = slots * tok
    for start in reversed(range(0, length, QUERY_BLOCK)):
        count = start + QUERY_BLOCK
        cols = slice(start, count)
        queries, grads = q_t[:, cols], g_t[:, cols]
        scores = masked_scores(
            keys[:count], queries, seg_k[0, :count], seg_q[0, :, cols], start, scale
        )
        probs = jnp.exp(scores - lse[0, :, cols])
        grad_probs = dot(values[:count], grads)
        row_dot = jnp.sum(probs * grad_probs, 0, keepdims=True)
        grad_scores = (probs * (grad_probs - row_dot)).astype(jnp.bfloat16)
        probs_low = probs.astype(jnp.bfloat16)
        dq_t[:, cols] = dot(k_t[:, :count], grad_scores) * scale
        dk = dot_right_t(queries, grad_scores)
        dv = dot_right_t(grads, probs_low)
        if count == length:
            dk_t[...] = dk
            dv_t[...] = dv
        else:
            dk_t[:, :count] += dk
            dv_t[:, :count] += dv
    for b in range(slots):
        at = order[unit, b]
        cols = slice(b * tok, (b + 1) * tok)
        out[at, 0, :depth] = dq_t[:, cols].astype(jnp.bfloat16)
        out[at, 0, depth : 2 * depth] = (dk_t[:, cols] * scale).astype(jnp.bfloat16)
        out[at, 0, 2 * depth :] = dv_t[:, cols].astype(jnp.bfloat16)


def attend_back(x, g, order, seg_k, seg_q, lse, scale):
    slots, units, depth3, tok = x.shape
    depth, length = depth3 // 3, slots * tok
    bf16 = jnp.bfloat16
    held = [pltpu.VMEM((depth, length), bf16)] * 4 + [pltpu.VMEM((depth, length), jnp.float32)] * 3
    return pl.pallas_call(
        functools.partial(attend_back_kernel, scale),
        grid_spec=pltpu.PrefetchScalarGridSpec(
            num_scalar_prefetch=1,
            grid=(units,),
            in_specs=[
                pl.BlockSpec((slots, 1, depth3, tok), lambda u, o: (0, u, 0, 0)),
                pl.BlockSpec((slots, 1, depth, tok), lambda u, o: (0, u, 0, 0)),
                pl.BlockSpec((1, length, 1), lambda u, o: (u, 0, 0)),
                pl.BlockSpec((1, 1, length), lambda u, o: (u, 0, 0)),
                pl.BlockSpec((1, 1, length), lambda u, o: (u, 0, 0)),
            ],
            out_specs=pl.BlockSpec((slots, 1, depth3, tok), lambda u, o: (0, u, 0, 0)),
            scratch_shapes=held,
        ),
        out_shape=jax.ShapeDtypeStruct(x.shape, bf16),
        compiler_params=pltpu.CompilerParams(vmem_limit_bytes=48 * 2**20),
        name="attend_back",
    )(order, x, g, seg_k, seg_q, lse)


def to_units(flat, micro_count, kinds):
    tok = flat.shape[1] // micro_count
    units = flat.reshape(kinds, HEADS, -1, micro_count, tok).transpose(3, 1, 0, 2, 4)
    units = units.reshape(micro_count * HEADS, -1, tok)
    units = jnp.pad(units, ((0, 8 * UNITS - units.shape[0]), (0, 0), (0, 0)))
    return units.reshape(8, UNITS, -1, tok)


def from_units(units, micro_count, kinds):
    tok = units.shape[3]
    held = units.reshape(8 * UNITS, -1, tok)[: micro_count * HEADS]
    held = held.reshape(micro_count, HEADS, kinds, -1, tok).transpose(0, 4, 2, 1, 3)
    return held.reshape(micro_count * tok, -1)


def shards_fast(
    tokens,
    cotangent,
    w_qkv,
    w_out,
    w_up,
    w_down,
    gain_one,
    bias_one,
    gain_two,
    bias_two,
    lengths,
    slot_order,
):
    micro_count, tok_dev, width = tokens.shape
    rows = micro_count * tok_dev
    scale = (width // HEADS) ** (-0.5)
    bf16, f32 = jnp.bfloat16, jnp.float32
    part = w_qkv.shape[0]
    my_slot = lax.axis_index("seq")

    downs = [w_down[i * part : (i + 1) * part] for i in range(4)]
    norms = jnp.stack([gain_one, bias_one, gain_two, bias_two], 1)
    rem = jnp.concatenate(
        [w_up[:, 512:], w_qkv[:, 384:], w_out[:, 128:]]
        + [down[:, 128:] for down in downs]
        + [norms, jnp.zeros((part, 28), bf16)],
        1,
    )
    gathered = gather_weights(
        [
            w_qkv[:, :384],
            jnp.concatenate([w_out[:, :128], rem, w_up[:, :128]], 1),
            w_up[:, 128:512],
            jnp.concatenate([down[:, :128] for down in downs], 1),
        ]
    )
    full_qkv, full_out, full_up, full_down, full_norms = unpack_weights(gathered)
    full_qkv = full_qkv.reshape(width, -1)
    full_out = full_out.reshape(width, width)
    full_up = full_up.reshape(width, -1)
    full_down = full_down.reshape(-1, width)
    norm_rows = full_norms[:, :, REM_NORM : REM_NORM + 4].reshape(width, 4).T.astype(f32)
    g_one, b_one, g_two, b_two = norm_rows[0], norm_rows[1], norm_rows[2], norm_rows[3]

    unit_ids = my_slot * UNITS + jnp.arange(UNITS, dtype=jnp.int32)
    second = (unit_ids >= HEADS)[:, None]
    doc_ends = jax.vmap(running_total)(lengths[:, 0])
    places = jnp.arange(8 * tok_dev, dtype=jnp.int32)
    segments = jax.vmap(segment_of, (None, 0))(places, doc_ends)
    unit_segments = jnp.where(second, segments[1][None], segments[0][None])
    seg_k, seg_q = unit_segments[:, :, None], unit_segments[:, None, :]
    slots = jnp.arange(8, dtype=jnp.int32)
    holders = jnp.sum(
        jnp.where(slot_order[:, 0][:, None, :] == slots[None, :, None], slots[None, None, :], 0), 2
    )
    order = jnp.where(second, holders[1][None], holders[0][None])

    residual = tokens.astype(f32).reshape(rows, width)
    scaled_one, inv_one = normalize(residual)
    normed_one = (scaled_one * g_one + b_one).astype(bf16)
    qkv_t = lax.dot_general(
        full_qkv, normed_one, (((0,), (1,)), ((), ())), preferred_element_type=f32
    ).astype(bf16)
    unit_qkv = exchange(to_units(qkv_t, micro_count, 3), 0)
    unit_out, lse = attend(unit_qkv, order, seg_k, seg_q, scale)
    attn_flat = from_units(exchange(unit_out, 1), micro_count, 1)
    middle = residual + dot(attn_flat, full_out)
    scaled_two, inv_two = normalize(middle)
    normed_two = (scaled_two * g_two + b_two).astype(bf16)
    hidden = dot(normed_two, full_up)
    activated_full, gelu_back = jax.vjp(gelu_tanh, hidden)
    activated = activated_full.astype(bf16)

    grad_rows = cotangent.reshape(rows, width)
    block_out = (middle + dot(activated, full_down)).astype(bf16)
    grad_hidden = gelu_back(dot_right_t(grad_rows, full_down))[0].astype(bf16)
    sum_down = outer(activated, grad_rows)
    sum_up = dot_left_t(normed_two, grad_hidden).astype(bf16)
    grad_normed_two = dot_right_t(grad_hidden, full_up)
    grad_middle = grad_rows.astype(f32) + norm_back(grad_normed_two, scaled_two, inv_two, g_two)
    grad_branch = grad_middle.astype(bf16)
    sum_proj = dot_left_t(attn_flat, grad_branch).astype(bf16)
    grad_heads_t = dot_right_t(full_out, grad_branch).astype(bf16)
    unit_grad = exchange(to_units(grad_heads_t, micro_count, 1), 2)
    unit_back = attend_back(unit_qkv, unit_grad, order, seg_k, seg_q, lse, scale)
    grad_qkv_rows = from_units(exchange(unit_back, 3), micro_count, 3)
    sum_qkv = dot_left_t(normed_one, grad_qkv_rows).astype(bf16)
    grad_normed_one = dot_right_t(grad_qkv_rows, full_qkv)
    grad_input = (
        grad_middle + norm_back(grad_normed_one, scaled_one, inv_one, g_one)
    ).astype(bf16)

    norm_sums = jnp.stack(
        [
            jnp.sum(grad_normed_one * scaled_one, 0),
            jnp.sum(grad_normed_one, 0),
            jnp.sum(grad_normed_two * scaled_two, 0),
            jnp.sum(grad_normed_two, 0),
        ]
    )
    norm_cols = jnp.pad(norm_sums.T.astype(bf16), ((0, 0), (REM_NORM, 28)))
    sum0, sum1, sum2, sum3 = (
        total.astype(f32)
        for total in scatter_grads(
            pack_grads(
                sum_qkv.reshape(4, part, -1),
                sum_proj.reshape(4, part, -1),
                sum_up.reshape(4, part, -1),
                sum_down.reshape(16, part, -1),
                norm_cols.reshape(4, part, -1),
            )
        )
    )
    rest = sum1[:, TILE : 2 * TILE]
    out_qkv = jnp.concatenate([sum0, rest[:, REM_QKV : REM_QKV + 24]], 1)
    out_proj = jnp.concatenate([sum1[:, :TILE], rest[:, REM_OUT : REM_OUT + 8]], 1)
    out_up = jnp.concatenate([sum1[:, 2 * TILE :], sum2, rest[:, REM_UP : REM_UP + 32]], 1)
    out_down = jnp.concatenate(
        [
            jnp.concatenate(
                [
                    sum3[:, i * TILE : (i + 1) * TILE],
                    rest[:, REM_DOWN + 8 * i : REM_DOWN + 8 * i + 8],
                ],
                1,
            )
            for i in range(4)
        ],
        0,
    )
    norm_mine = rest[:, REM_NORM : REM_NORM + 4].T
    return (
        block_out.reshape(tokens.shape),
        grad_input.reshape(tokens.shape),
        out_qkv,
        out_proj,
        out_up,
        out_down,
        norm_mine[0],
        norm_mine[1],
        norm_mine[2],
        norm_mine[3],
    )


def solution(mesh):
    grid = (mesh.shape["dp"], mesh.shape["seq"])
    return jax.shard_map(
        shards_fast if grid == (4, 8) else shards_plain,
        mesh=mesh,
        in_specs=(
            P(None, ("dp", "seq"), None),
            P(None, ("dp", "seq"), None),
            P("dp", "seq"),
            P("dp", "seq"),
            P("dp", "seq"),
            P("dp", "seq"),
            P("dp"),
            P("dp"),
            P("dp"),
            P("dp"),
            P(None, "dp", None),
            P(None, "dp", None),
        ),
        out_specs=(
            P(None, ("dp", "seq"), None),
            P(None, ("dp", "seq"), None),
            P("dp", "seq"),
            P("dp", "seq"),
            P("dp", "seq"),
            P("dp", "seq"),
            P("dp"),
            P("dp"),
            P("dp"),
            P("dp"),
        ),
        check_vma=False,
    )
```

```python
import functools

import jax
import jax.numpy as jnp
from jax import lax
from jax.experimental import pallas as pl
from jax.experimental.pallas import tpu as pltpu
from jax.sharding import PartitionSpec as P

HEADS = 17


EPS = 1e-05
GELU_C = 0.7978845608028654


def gelu_tanh(values):
    return 0.5 * values * (1.0 + jnp.tanh(GELU_C * (values + 0.044715 * values * values * values)))


def normalize(residual):
    row_mean = jnp.mean(residual, -1, keepdims=True)
    centered = residual - row_mean
    inv_std = lax.rsqrt(jnp.mean(centered * centered, -1, keepdims=True) + EPS)
    return (centered * inv_std, inv_std)


def norm_back(grad_normed, scaled, inv_std, gain_row):
    grad_scaled = grad_normed * gain_row
    return inv_std * (
        grad_scaled
        - jnp.mean(grad_scaled, -1, keepdims=True)
        - scaled * jnp.mean(grad_scaled * scaled, -1, keepdims=True)
    )


def running_total(counts):
    index = jnp.arange(counts.shape[0], dtype=jnp.int32)
    return jnp.sum(jnp.where(index[None, :] <= index[:, None], counts[None, :], 0), 1)


def segment_of(places, doc_ends):
    return jnp.sum((places[:, None] >= doc_ends[None, :]).astype(jnp.int32), 1)


def pair_swap(block):
    route = [(i, i ^ 1) for i in range(lax.axis_size("seq"))]
    return lax.ppermute(block, "seq", route)


def same_core():
    n_seq = lax.axis_size("seq")
    return [list(range(core, n_seq, 2)) for core in range(2)]


def gather_stack(shard):
    chips = lax.all_gather(shard, "seq", axis_index_groups=same_core())
    held = lax.all_gather(chips, "dp")
    other = pair_swap(held)
    first = lax.axis_index("seq") % 2 == 0
    both = jnp.stack([jnp.where(first, held, other), jnp.where(first, other, held)], 2)
    dp, chip_count = held.shape[:2]
    return both.transpose(1, 2, 0, 3, 4).reshape(2 * chip_count, dp, *shard.shape)


def pair_sum(parts):
    pairs = parts.reshape(parts.shape[0] // 2, 2, *parts.shape[1:])
    first = lax.axis_index("seq") % 2 == 0
    mine = jnp.where(first, pairs[:, 0], pairs[:, 1])
    other = jnp.where(first, pairs[:, 1], pairs[:, 0])
    got = pair_swap(other)
    return (mine.astype(jnp.float32) + got.astype(jnp.float32)).astype(jnp.bfloat16)


def scatter_stack(parts, after):
    held = pair_sum(parts).transpose(1, 0, 2, 3).reshape(-1, parts.shape[3])
    if after is not None:
        held, after = lax.optimization_barrier((held, after))
    held = lax.psum_scatter(held, "dp", scatter_dimension=0, tiled=True)
    held = lax.psum_scatter(
        held, "seq", scatter_dimension=0, axis_index_groups=same_core(), tiled=True
    )
    return held, after


def dot(left, right):
    return jnp.dot(left, right, preferred_element_type=jnp.float32)


def dot_right_t(left, right):
    return lax.dot_general(left, right, (((1,), (1,)), ((), ())), preferred_element_type=jnp.float32)


def dot_left_t(left, right):
    return lax.dot_general(left, right, (((0,), (0,)), ((), ())), preferred_element_type=jnp.float32)


def cols_of(rows, count):
    return rows.reshape(rows.shape[0], count, -1).transpose(1, 0, 2)


def apply_cols(rows, cols):
    lifted = jnp.broadcast_to(rows[None], (cols.shape[0],) + rows.shape)
    made = lax.dot_general(
        lifted, cols, (((2,), (1,)), ((0,), (0,))), preferred_element_type=jnp.float32
    )
    return made.transpose(1, 0, 2).reshape(rows.shape[0], -1)


def apply_cols_t(rows, cols):
    lifted = cols_of(rows, cols.shape[0])
    return lax.dot_general(
        lifted, cols, (((0, 2), (0, 2)), ((), ())), preferred_element_type=jnp.float32
    )


def grad_cols(left, right, count):
    lifted = jnp.broadcast_to(left[None], (count,) + left.shape)
    return lax.dot_general(
        lifted, cols_of(right, count), (((1,), (1,)), ((0,), (0,))),
        preferred_element_type=jnp.float32,
    )


def heads_of(rows, micro_count, head_dim):
    return rows.reshape(micro_count, -1, HEADS, head_dim).transpose(0, 2, 1, 3)


def rows_of(heads):
    micro_count, _, slots, head_dim = heads.shape
    return heads.transpose(0, 2, 1, 3).reshape(micro_count * slots, HEADS * head_dim)


def batched(left, right, left_dim, right_dim):
    return lax.dot_general(
        left,
        right,
        (((left_dim,), (right_dim,)), ((0, 1), (0, 1))),
        preferred_element_type=jnp.float32,
    )


def shards_plain(
    tokens,
    cotangent,
    w_qkv,
    w_out,
    w_up,
    w_down,
    gain_one,
    bias_one,
    gain_two,
    bias_two,
    lengths,
    slot_order,
):
    micro_count, tok_dev, width = tokens.shape
    rows = micro_count * tok_dev
    head_dim = width // HEADS
    score_scale = head_dim ** (-0.5)
    n_seq = lax.axis_size("seq")
    my_slot = lax.axis_index("seq")
    bf16 = jnp.bfloat16

    norms = lax.all_gather(
        jnp.stack([gain_one, bias_one, gain_two, bias_two]), "dp", axis=1, tiled=True
    ).astype(jnp.float32)
    g_one, b_one, g_two, b_two = norms[0], norms[1], norms[2], norms[3]
    n_dp = lax.axis_size("dp")
    part, qkv_cols = w_qkv.shape
    out_cols = w_out.shape[1]
    up_cols = w_up.shape[1]
    fold = w_down.shape[0] // up_cols
    attn_stack = gather_stack(jnp.concatenate([w_qkv, w_out], 1))
    down_t = w_down.T
    ffn_stack = gather_stack(
        jnp.concatenate([w_up, *jnp.split(down_t, fold, 1)], 0)
    )
    cols_qkv = attn_stack[..., :qkv_cols].reshape(n_seq, width, qkv_cols)
    full_out = (
        attn_stack[..., qkv_cols:].reshape(n_seq, width, out_cols).transpose(1, 0, 2)
    ).reshape(width, width)
    cols_up = ffn_stack[:, :, :part].reshape(n_seq, width, up_cols)
    full_down_t = (
        ffn_stack[:, :, part:]
        .reshape(n_seq, n_dp, fold, out_cols, up_cols)
        .transpose(0, 3, 1, 2, 4)
        .reshape(width, fold * n_dp * up_cols)
    )

    doc_ends = jax.vmap(running_total)(lengths[:, 0])
    k_place = (
        slot_order[:, 0, :, None] * tok_dev + jnp.arange(tok_dev, dtype=jnp.int32)
    ).reshape(micro_count, n_seq * tok_dev)
    k_segment = jax.vmap(segment_of)(k_place, doc_ends)
    base_slot = lax.dynamic_slice_in_dim(slot_order[:, 0], my_slot, 1, 1)
    q_place = base_slot * tok_dev + jnp.arange(tok_dev, dtype=jnp.int32)
    q_segment = jax.vmap(segment_of)(q_place, doc_ends)
    allowed = (q_segment[:, :, None] == k_segment[:, None, :]) & (
        k_place[:, None, :] <= q_place[:, :, None]
    )

    residual = tokens.astype(jnp.float32).reshape(rows, width)
    scaled_one, inv_one = normalize(residual)
    normed_one = (scaled_one * g_one + b_one).astype(bf16)
    qkv_all = apply_cols(normed_one, cols_qkv).astype(bf16)
    queries = heads_of(qkv_all[:, :width], micro_count, head_dim)
    local_kv = qkv_all[:, width:].reshape(micro_count, tok_dev, 2 * width)
    group_kv = lax.all_gather(local_kv, "seq", axis=1, tiled=True)
    keys = heads_of(group_kv[..., :width], micro_count, head_dim)
    values = heads_of(group_kv[..., width:], micro_count, head_dim)

    scores = batched(queries, keys, 3, 3) * score_scale
    scores = jnp.where(allowed[:, None], scores, -jnp.inf)
    weights = jnp.exp(scores - jnp.max(scores, -1, keepdims=True))
    probs = weights * (1.0 / jnp.sum(weights, -1, keepdims=True))
    probs_low = probs.astype(bf16)
    attended = batched(probs_low, values, 3, 2)
    attn_flat = rows_of(attended.astype(bf16))
    middle = residual + dot(attn_flat, full_out)
    scaled_two, inv_two = normalize(middle)
    normed_two = (scaled_two * g_two + b_two).astype(bf16)
    hidden = apply_cols(normed_two, cols_up)
    activated_full, gelu_back = jax.vjp(gelu_tanh, hidden)
    activated = activated_full.astype(bf16)

    grad_rows = cotangent.reshape(rows, width)
    block_out = (middle + dot_right_t(activated, full_down_t)).astype(bf16)
    grad_hidden = gelu_back(dot(grad_rows, full_down_t))[0].astype(bf16)
    sum_down_t = dot_left_t(grad_rows, activated).astype(bf16)
    sum_down_t = (
        sum_down_t.reshape(n_seq, out_cols, n_dp, fold, up_cols)
        .transpose(0, 2, 3, 1, 4)
        .reshape(n_seq, n_dp, fold * out_cols, up_cols)
    )
    sum_up = grad_cols(normed_two, grad_hidden, n_seq).astype(bf16)
    sum_ffn, _ = scatter_stack(
        jnp.concatenate([sum_up.reshape(n_seq, n_dp, part, up_cols), sum_down_t], 2), None
    )
    grad_normed_two = apply_cols_t(grad_hidden, cols_up)
    grad_middle = grad_rows.astype(jnp.float32) + norm_back(
        grad_normed_two, scaled_two, inv_two, g_two
    )
    grad_branch = grad_middle.astype(bf16)
    sum_proj = grad_cols(attn_flat, grad_branch, n_seq).astype(bf16)
    grad_heads = heads_of(
        dot_right_t(grad_branch, full_out).astype(bf16), micro_count, head_dim
    )

    grad_probs = batched(grad_heads, values, 3, 3)
    row_dot = jnp.sum(probs * grad_probs, -1, keepdims=True)
    grad_scores = (probs * (grad_probs - row_dot)).astype(bf16)
    grad_query = rows_of(batched(grad_scores, keys, 3, 2) * score_scale)
    grad_keys = rows_of(batched(grad_scores, queries, 2, 2) * score_scale)
    grad_values = rows_of(batched(probs_low, grad_heads, 2, 2))
    grad_kv = jnp.concatenate([grad_keys.astype(bf16), grad_values.astype(bf16)], 1)
    grad_kv = grad_kv.reshape(micro_count, n_seq, tok_dev, 2 * width).transpose(1, 0, 2, 3)
    grad_kv = lax.psum_scatter(
        pair_sum(grad_kv), "seq", scatter_dimension=0, axis_index_groups=same_core()
    ).reshape(rows, 2 * width)
    grad_qkv_rows = jnp.concatenate([grad_query.astype(bf16), grad_kv], 1)
    sum_qkv = grad_cols(normed_one, grad_qkv_rows, n_seq).astype(bf16)
    sum_attn, sum_ffn = scatter_stack(
        jnp.concatenate([sum_qkv, sum_proj], 2).reshape(n_seq, n_dp, part, qkv_cols + out_cols),
        sum_ffn,
    )
    sum_attn = sum_attn.astype(jnp.float32)
    sum_ffn = sum_ffn.astype(jnp.float32)
    out_up = sum_ffn[:part]
    out_down = jnp.concatenate(jnp.split(sum_ffn[part:], fold, 0), 1).T
    out_qkv = sum_attn[:, :qkv_cols]
    out_proj = sum_attn[:, qkv_cols:]
    grad_normed_one = apply_cols_t(grad_qkv_rows, cols_qkv)
    grad_input = (
        grad_middle + norm_back(grad_normed_one, scaled_one, inv_one, g_one)
    ).astype(bf16)

    norm_sums = jnp.stack(
        [
            jnp.sum(grad_normed_one * scaled_one, 0),
            jnp.sum(grad_normed_one, 0),
            jnp.sum(grad_normed_two * scaled_two, 0),
            jnp.sum(grad_normed_two, 0),
        ]
    )
    norm_totals = lax.psum(norm_sums, ("dp", "seq"))
    norm_mine = lax.dynamic_slice_in_dim(norm_totals, lax.axis_index("dp") * part, part, 1)
    return (
        block_out.reshape(tokens.shape),
        grad_input.reshape(tokens.shape),
        out_qkv,
        out_proj,
        out_up,
        out_down,
        norm_mine[0],
        norm_mine[1],
        norm_mine[2],
        norm_mine[3],
    )


MESH = pl.DeviceIdType.MESH
GATHER_ORDERS = ((2, 3, 0, 1), (2, 3, 1, 0), (2, 3, 0, 1), (2, 3, 1, 0))
SCATTER_ORDERS = ((2, 3, 0, 1), (2, 3, 1, 0), (0, 2, 3, 1), (1, 3, 2, 0))
ROW_CUTS = ((0, 64), (64, 64), (128, 64), (192, 80))
CHUNKS = tuple((q, r) for pair in ((0, 1), (2, 3)) for r in range(4) for q in pair)
GATHER_LAGS = (0, 2, 4, 6, 9)
SCATTER_LAGS = (0, 3, 5, 7, 9)
AHEAD = 4
TILE = 128
LANES = (3 * TILE, 3 * TILE, 3 * TILE, 4 * TILE)
UNITS = 5
REM_UP, REM_QKV, REM_OUT, REM_DOWN, REM_NORM = 0, 32, 56, 64, 96


def place_of(order, dp, seq):
    z = seq // 2
    bits = (dp % 2, dp // 2, (z % 2 + z // 2) % 2, z // 2)
    return sum(bits[dim] * 2**k for k, dim in enumerate(order))


def partner(dim):
    dp, seq = lax.axis_index("dp"), lax.axis_index("seq")
    z, core = seq // 2, seq % 2
    if dim == 0:
        return (dp + 1 - 2 * (dp % 2), seq)
    if dim == 1:
        return (dp + 2 - 4 * (dp // 2), seq)
    if dim == 2:
        return (dp, (z + 1 - 2 * (z % 2)) * 2 + core)
    return (dp, (3 - z) * 2 + core)


def sibling():
    dp, seq = lax.axis_index("dp"), lax.axis_index("seq")
    return (dp, seq + 1 - 2 * (seq % 2))


def greet(devices):
    barrier = pltpu.get_barrier_semaphore()
    for device in devices:
        pl.semaphore_signal(barrier, inc=1, device_id=device, device_id_type=MESH)
    pl.semaphore_wait(barrier, len(devices))


def send(src, dst, send_sem, recv_sem, device):
    copy = pltpu.make_async_remote_copy(
        src_ref=src, dst_ref=dst, send_sem=send_sem, recv_sem=recv_sem,
        device_id=device, device_id_type=MESH,
    )
    copy.start()
    return copy


def gather_kernel(*refs):
    shards_in, full = refs[:4], refs[4:8]
    own_sem, link_send, link_recv, sib_send, sib_recv = refs[8:]
    dp, seq = lax.axis_index("dp"), lax.axis_index("seq")
    core = seq % 2
    greet([partner(dim) for dim in range(4)] + [sibling()])
    at = [place_of(GATHER_ORDERS[q], dp, seq) for q in range(4)]
    owns, links, sides = {}, {}, []

    def step(chunk, stage):
        q, r = CHUNKS[chunk]
        span = pl.ds(*ROW_CUTS[r])
        size = 2**stage
        if stage == 0:
            fresh, target = shards_in[q].at[span], full[q].at[core, at[q], span]
            links[chunk] = send(
                fresh, target, link_send.at[chunk, 0], link_recv.at[chunk, 0],
                partner(GATHER_ORDERS[q][0]),
            )
            owns[chunk] = pltpu.make_async_copy(fresh, target, own_sem.at[chunk])
            owns[chunk].start()
            sides.append(
                send(fresh, target, sib_send.at[chunk, 0], sib_recv.at[chunk, 0], sibling())
            )
            return
        links[chunk].wait()
        if stage == 1:
            owns[chunk].wait()
        if stage < 4:
            held = full[q].at[core, pl.ds(at[q] // size * size, size), span]
            links[chunk] = send(
                held, held, link_send.at[chunk, stage], link_recv.at[chunk, stage],
                partner(GATHER_ORDERS[q][stage]),
            )
        half = size // 2
        mine = at[q] // half
        got = full[q].at[core, pl.ds((mine + 1 - 2 * (mine % 2)) * half, half), span]
        sides.append(
            send(got, got, sib_send.at[chunk, stage], sib_recv.at[chunk, stage], sibling())
        )

    for turn in range(len(CHUNKS) + GATHER_LAGS[4]):
        for stage in (4, 3, 2, 1, 0):
            lag = GATHER_LAGS[stage]
            if 0 <= turn - lag < len(CHUNKS):
                step(turn - lag, stage)
    for side in sides:
        side.wait()


def gather_weights(chunks):
    rows = chunks[0].shape[0]
    anywhere = pl.BlockSpec(memory_space=pl.ANY)
    dma = pltpu.SemaphoreType.DMA
    return pl.pallas_call(
        gather_kernel,
        out_shape=[jax.ShapeDtypeStruct((2, 16, rows, lanes), jnp.bfloat16) for lanes in LANES],
        in_specs=[anywhere] * 4,
        out_specs=[anywhere] * 4,
        scratch_shapes=[dma((16,)), dma((16, 4)), dma((16, 4)), dma((16, 5)), dma((16, 5))],
        compiler_params=pltpu.CompilerParams(collective_id=0, has_side_effects=True),
        name="gather_weights",
    )(*chunks)


def scatter_kernel(*refs):
    parts, outs = refs[:4], refs[4:8]
    own, acc, got3, got2, got1, got0 = (refs[8 + 4 * i : 12 + 4 * i] for i in range(6))
    got = (got0, got1, got2, got3)
    own_sem, link_send, link_recv, sib_send, sib_recv = refs[32:]
    dp, seq = lax.axis_index("dp"), lax.axis_index("seq")
    core = seq % 2
    greet([partner(dim) for dim in range(4)] + [sibling()])
    at = [place_of(SCATTER_ORDERS[q], dp, seq) for q in range(4)]
    side, load, links = {}, {}, {}

    def begin(chunk):
        q, r = CHUNKS[chunk]
        rows = pl.ds(*ROW_CUTS[r])
        side[chunk] = send(
            parts[q].at[1 - core, :, rows], acc[q].at[:, rows],
            sib_send.at[chunk], sib_recv.at[chunk], sibling(),
        )
        load[chunk] = pltpu.make_async_copy(
            parts[q].at[core, :, rows], own[q].at[:, rows], own_sem.at[chunk]
        )
        load[chunk].start()

    for chunk in range(AHEAD):
        begin(chunk)

    def add(chunk, base, other, other_base, count):
        q, r = CHUNKS[chunk]
        rows = pl.ds(*ROW_CUTS[r])

        def one(b, carry):
            acc[q][base + b, rows] = acc[q][base + b, rows] + other[other_base + b, rows]
            return carry

        lax.fori_loop(0, count, one, 0)

    def step(chunk, stage):
        q, r = CHUNKS[chunk]
        rows = pl.ds(*ROW_CUTS[r])
        half = 2**stage
        base = at[q] // (2 * half) * (2 * half)
        high = at[q] // half % 2
        away, keep = (1 - high) * half, high * half
        if stage == 3:
            side[chunk].wait_recv()
            load[chunk].wait()
            other = own[q]
        else:
            links[chunk, stage + 1].wait_recv()
            other = got[stage + 1][q]
        add(chunk, base + away, other, away, half)
        links[chunk, stage] = send(
            acc[q].at[pl.ds(base + away, half), rows], got[stage][q].at[:, rows],
            link_send.at[chunk, stage], link_recv.at[chunk, stage], partner(SCATTER_ORDERS[q][stage]),
        )
        add(chunk, base + keep, other, keep, half)

    for turn in range(len(CHUNKS) + SCATTER_LAGS[4]):
        if turn + AHEAD < len(CHUNKS):
            begin(turn + AHEAD)
        for stage in (-1, 0, 1, 2, 3):
            lag = SCATTER_LAGS[3 - stage]
            chunk = turn - lag
            if 0 <= chunk < len(CHUNKS):
                if stage >= 0:
                    step(chunk, stage)
                    continue
                q, r = CHUNKS[chunk]
                rows = pl.ds(*ROW_CUTS[r])
                links[chunk, 0].wait_recv()
                outs[q][rows] = acc[q][at[q], rows] + got0[q][0, rows]
    for copy in list(side.values()) + list(links.values()):
        copy.wait_send()


def scatter_grads(parts):
    rows = parts[0].shape[2]
    dma = pltpu.SemaphoreType.DMA
    bf16 = jnp.bfloat16
    buffers = [
        pltpu.VMEM((count, rows, lanes), bf16) for count in (16, 16, 8, 4, 2, 1) for lanes in LANES
    ]
    return pl.pallas_call(
        scatter_kernel,
        out_shape=[jax.ShapeDtypeStruct((rows, lanes), bf16) for lanes in LANES],
        in_specs=[pl.BlockSpec(memory_space=pl.ANY)] * 4,
        out_specs=[pl.BlockSpec(memory_space=pltpu.VMEM)] * 4,
        scratch_shapes=buffers + [dma((16,)), dma((16, 4)), dma((16, 4)), dma((16,)), dma((16,))],
        compiler_params=pltpu.CompilerParams(
            collective_id=1, has_side_effects=True, vmem_limit_bytes=56 * 2**20
        ),
        name="scatter_grads",
    )(*parts)


def exchange_kernel(blocks, out, own_sem, send_sem, recv_sem):
    dp, seq = lax.axis_index("dp"), lax.axis_index("seq")
    others = [(dp, (seq + k) % 8) for k in range(1, 8)]
    greet(others)
    own = pltpu.make_async_copy(blocks.at[seq], out.at[seq], own_sem)
    copies = [
        send(blocks.at[device[1]], out.at[seq], send_sem.at[k], recv_sem.at[k], device)
        for k, device in enumerate(others)
    ]
    own.start()
    own.wait()
    for copy in copies:
        copy.wait()


def exchange(blocks, which):
    dma = pltpu.SemaphoreType.DMA
    return pl.pallas_call(
        exchange_kernel,
        out_shape=jax.ShapeDtypeStruct(blocks.shape, blocks.dtype),
        in_specs=[pl.BlockSpec(memory_space=pl.ANY)],
        out_specs=pl.BlockSpec(memory_space=pl.ANY),
        scratch_shapes=[dma, dma((7,)), dma((7,))],
        compiler_params=pltpu.CompilerParams(collective_id=2 + which, has_side_effects=True),
        name=f"exchange_{which}",
    )(blocks)


def spots():
    for dp in range(4):
        for seq in range(8):
            yield dp, seq, seq % 2, [place_of(SCATTER_ORDERS[q], dp, seq) for q in range(4)]


def unpack_kernel(c0, c1, c2, c3, qkv, out, up, down, norms):
    for dp in range(4):
        pieces = [[] for _ in range(7)]
        for s in range(8):
            at = [place_of(GATHER_ORDERS[q], dp, s) for q in range(4)]
            core = s % 2
            rem = c1[core, at[1], :, TILE : 2 * TILE]
            if s == 0:
                norms[dp] = rem
            pieces[0] += [c0[core, at[0]], rem[:, REM_QKV : REM_QKV + 24]]
            pieces[1] += [c1[core, at[1], :, :TILE], rem[:, REM_OUT : REM_OUT + 8]]
            pieces[2] += [
                c1[core, at[1], :, 2 * TILE :], c2[core, at[2]], rem[:, REM_UP : REM_UP + 32]
            ]
            for i in range(4):
                pieces[3 + i] += [
                    c3[core, at[3], :, i * TILE : (i + 1) * TILE],
                    rem[:, REM_DOWN + 8 * i : REM_DOWN + 8 * i + 8],
                ]
        qkv[dp] = jnp.concatenate(pieces[0], 1)
        out[dp] = jnp.concatenate(pieces[1], 1)
        up[dp] = jnp.concatenate(pieces[2], 1)
        for i in range(4):
            down[dp * 4 + i] = jnp.concatenate(pieces[3 + i], 1)


def unpack_weights(chunks):
    bf16 = jnp.bfloat16
    rows, step = chunks[0].shape[2], 16

    def spec(count, lanes):
        return pl.BlockSpec((count, step, lanes), lambda i: (0, i, 0))

    sizes = ((4, 3264), (4, 1088), (4, 4352), (16, 1088), (4, 128))
    return pl.pallas_call(
        unpack_kernel,
        grid=(rows // step,),
        out_shape=[jax.ShapeDtypeStruct((count, rows, lanes), bf16) for count, lanes in sizes],
        in_specs=[pl.BlockSpec((2, 16, step, lanes), lambda i: (0, 0, i, 0)) for lanes in LANES],
        out_specs=[spec(*size) for size in sizes],
        compiler_params=pltpu.CompilerParams(vmem_limit_bytes=40 * 2**20),
        name="unpack_weights",
    )(*chunks)


def pack_kernel(qkv, out, up, down, norms, c0, c1, c2, c3):
    for dp, s, core, at in spots():
        c0[core, at[0]] = qkv[dp, :, s * 408 : s * 408 + 384]
        c1[core, at[1], :, :TILE] = out[dp, :, s * 136 : s * 136 + 128]
        c1[core, at[1], :, 2 * TILE :] = up[dp, :, s * 544 : s * 544 + 128]
        c2[core, at[2]] = up[dp, :, s * 544 + 128 : s * 544 + 512]
        base = at[1]
        c1[core, base, :, TILE : 2 * TILE] = norms[dp]
        c1[core, base, :, TILE + REM_UP : TILE + REM_UP + 32] = up[dp, :, s * 544 + 512 : s * 544 + 544]
        c1[core, base, :, TILE + REM_QKV : TILE + REM_QKV + 24] = qkv[dp, :, s * 408 + 384 : s * 408 + 408]
        c1[core, base, :, TILE + REM_OUT : TILE + REM_OUT + 8] = out[dp, :, s * 136 + 128 : s * 136 + 136]
        for i in range(4):
            c3[core, at[3], :, i * TILE : (i + 1) * TILE] = down[dp * 4 + i, :, s * 136 : s * 136 + 128]
            spot = TILE + REM_DOWN + 8 * i
            c1[core, base, :, spot : spot + 8] = down[dp * 4 + i, :, s * 136 + 128 : s * 136 + 136]


def pack_grads(qkv, out, up, down, norms):
    rows, step = qkv.shape[1], 16

    def spec(count, lanes):
        return pl.BlockSpec((count, step, lanes), lambda i: (0, i, 0))

    return pl.pallas_call(
        pack_kernel,
        grid=(rows // step,),
        out_shape=[jax.ShapeDtypeStruct((2, 16, rows, lanes), jnp.bfloat16) for lanes in LANES],
        in_specs=[spec(4, 3264), spec(4, 1088), spec(4, 4352), spec(16, 1088), spec(4, 128)],
        out_specs=[pl.BlockSpec((2, 16, step, lanes), lambda i: (0, 0, i, 0)) for lanes in LANES],
        compiler_params=pltpu.CompilerParams(vmem_limit_bytes=40 * 2**20),
        name="pack_grads",
    )(qkv, out, up, down, norms)


QUERY_BLOCK = 256


def flip(block):
    return block.astype(jnp.float32).T.astype(jnp.bfloat16)


def outer_kernel(left, right, out):
    out[...] = dot(flip(left[...]), right[...]).astype(out.dtype)


def outer(left, right):
    rows, width = left.shape
    step = 2 * TILE
    return pl.pallas_call(
        outer_kernel,
        grid=(width // step,),
        out_shape=jax.ShapeDtypeStruct((width, right.shape[1]), jnp.bfloat16),
        in_specs=[
            pl.BlockSpec((rows, step), lambda i: (0, i)),
            pl.BlockSpec(right.shape, lambda i: (0, 0)),
        ],
        out_specs=pl.BlockSpec((step, right.shape[1]), lambda i: (i, 0)),
        compiler_params=pltpu.CompilerParams(vmem_limit_bytes=24 * 2**20),
        cost_estimate=pl.CostEstimate(
            flops=2 * rows * width * right.shape[1],
            bytes_accessed=2 * width * (right.shape[1] + rows),
            transcendentals=0,
        ),
        name="outer",
    )(left, right)


def masked_scores(k_rows, q_cols, seg_k, seg_q, start, scale):
    count, width = k_rows.shape[0], q_cols.shape[1]
    scores = dot(k_rows, q_cols) * scale
    key_at = lax.broadcasted_iota(jnp.int32, (count, width), 0)
    query_at = lax.broadcasted_iota(jnp.int32, (count, width), 1) + start
    return jnp.where((seg_k == seg_q) & (key_at <= query_at), scores, -1e30)


def attend_kernel(scale, order, x, seg_k, seg_q, out, lse, q_t, k_t, v_t, o_t):
    unit = pl.program_id(0)
    slots = x.shape[0]
    tok = x.shape[3]
    depth = q_t.shape[0]
    for b in range(slots):
        at = order[unit, b]
        for n, held in enumerate((q_t, k_t, v_t)):
            held[:, b * tok : (b + 1) * tok] = x[at, 0, n * depth : (n + 1) * depth]
    keys = flip(k_t[...])
    for start in range(0, slots * tok, QUERY_BLOCK):
        count = start + QUERY_BLOCK
        cols = slice(start, count)
        scores = masked_scores(
            keys[:count], q_t[:, cols], seg_k[0, :count], seg_q[0, :, cols], start, scale
        )
        top = jnp.max(scores, 0, keepdims=True)
        weights = jnp.exp(scores - top)
        total = jnp.sum(weights, 0, keepdims=True)
        probs = (weights * (1.0 / total)).astype(jnp.bfloat16)
        o_t[:, cols] = dot(v_t[:, :count], probs).astype(jnp.bfloat16)
        lse[0, :, cols] = top + jnp.log(total)
    for b in range(slots):
        out[order[unit, b], 0] = o_t[:, b * tok : (b + 1) * tok]


def attend(x, order, seg_k, seg_q, scale):
    slots, units, depth3, tok = x.shape
    depth, length = depth3 // 3, slots * tok
    bf16 = jnp.bfloat16
    held = [pltpu.VMEM((depth, length), bf16)] * 4
    return pl.pallas_call(
        functools.partial(attend_kernel, scale),
        grid_spec=pltpu.PrefetchScalarGridSpec(
            num_scalar_prefetch=1,
            grid=(units,),
            in_specs=[
                pl.BlockSpec((slots, 1, depth3, tok), lambda u, o: (0, u, 0, 0)),
                pl.BlockSpec((1, length, 1), lambda u, o: (u, 0, 0)),
                pl.BlockSpec((1, 1, length), lambda u, o: (u, 0, 0)),
            ],
            out_specs=[
                pl.BlockSpec((slots, 1, depth, tok), lambda u, o: (0, u, 0, 0)),
                pl.BlockSpec((1, 1, length), lambda u, o: (u, 0, 0)),
            ],
            scratch_shapes=held,
        ),
        out_shape=[
            jax.ShapeDtypeStruct((slots, units, depth, tok), bf16),
            jax.ShapeDtypeStruct((units, 1, length), jnp.float32),
        ],
        compiler_params=pltpu.CompilerParams(vmem_limit_bytes=40 * 2**20),
        name="attend",
    )(order, x, seg_k, seg_q)


def attend_back_kernel(
    scale, order, x, g, seg_k, seg_q, lse, out, q_t, k_t, v_t, g_t, dq_t, dk_t, dv_t
):
    unit = pl.program_id(0)
    slots = x.shape[0]
    tok = x.shape[3]
    depth = q_t.shape[0]
    for b in range(slots):
        at = order[unit, b]
        for n, held in enumerate((q_t, k_t, v_t)):
            held[:, b * tok : (b + 1) * tok] = x[at, 0, n * depth : (n + 1) * depth]
        g_t[:, b * tok : (b + 1) * tok] = g[at, 0]
    keys = flip(k_t[...])
    values = flip(v_t[...])
    length = slots * tok
    for start in reversed(range(0, length, QUERY_BLOCK)):
        count = start + QUERY_BLOCK
        cols = slice(start, count)
        queries, grads = q_t[:, cols], g_t[:, cols]
        scores = masked_scores(
            keys[:count], queries, seg_k[0, :count], seg_q[0, :, cols], start, scale
        )
        probs = jnp.exp(scores - lse[0, :, cols])
        grad_probs = dot(values[:count], grads)
        row_dot = jnp.sum(probs * grad_probs, 0, keepdims=True)
        grad_scores = (probs * (grad_probs - row_dot)).astype(jnp.bfloat16)
        probs_low = probs.astype(jnp.bfloat16)
        dq_t[:, cols] = dot(k_t[:, :count], grad_scores) * scale
        dk = dot_right_t(queries, grad_scores)
        dv = dot_right_t(grads, probs_low)
        if count == length:
            dk_t[...] = dk
            dv_t[...] = dv
        else:
            dk_t[:, :count] += dk
            dv_t[:, :count] += dv
    for b in range(slots):
        at = order[unit, b]
        cols = slice(b * tok, (b + 1) * tok)
        out[at, 0, :depth] = dq_t[:, cols].astype(jnp.bfloat16)
        out[at, 0, depth : 2 * depth] = (dk_t[:, cols] * scale).astype(jnp.bfloat16)
        out[at, 0, 2 * depth :] = dv_t[:, cols].astype(jnp.bfloat16)


def attend_back(x, g, order, seg_k, seg_q, lse, scale):
    slots, units, depth3, tok = x.shape
    depth, length = depth3 // 3, slots * tok
    bf16 = jnp.bfloat16
    held = [pltpu.VMEM((depth, length), bf16)] * 4 + [pltpu.VMEM((depth, length), jnp.float32)] * 3
    return pl.pallas_call(
        functools.partial(attend_back_kernel, scale),
        grid_spec=pltpu.PrefetchScalarGridSpec(
            num_scalar_prefetch=1,
            grid=(units,),
            in_specs=[
                pl.BlockSpec((slots, 1, depth3, tok), lambda u, o: (0, u, 0, 0)),
                pl.BlockSpec((slots, 1, depth, tok), lambda u, o: (0, u, 0, 0)),
                pl.BlockSpec((1, length, 1), lambda u, o: (u, 0, 0)),
                pl.BlockSpec((1, 1, length), lambda u, o: (u, 0, 0)),
                pl.BlockSpec((1, 1, length), lambda u, o: (u, 0, 0)),
            ],
            out_specs=pl.BlockSpec((slots, 1, depth3, tok), lambda u, o: (0, u, 0, 0)),
            scratch_shapes=held,
        ),
        out_shape=jax.ShapeDtypeStruct(x.shape, bf16),
        compiler_params=pltpu.CompilerParams(vmem_limit_bytes=48 * 2**20),
        name="attend_back",
    )(order, x, g, seg_k, seg_q, lse)


def to_units(flat, micro_count, kinds):
    tok = flat.shape[1] // micro_count
    units = flat.reshape(kinds, HEADS, -1, micro_count, tok).transpose(3, 1, 0, 2, 4)
    units = units.reshape(micro_count * HEADS, -1, tok)
    units = jnp.pad(units, ((0, 8 * UNITS - units.shape[0]), (0, 0), (0, 0)))
    return units.reshape(8, UNITS, -1, tok)


def from_units(units, micro_count, kinds):
    tok = units.shape[3]
    held = units.reshape(8 * UNITS, -1, tok)[: micro_count * HEADS]
    held = held.reshape(micro_count, HEADS, kinds, -1, tok).transpose(0, 4, 2, 1, 3)
    return held.reshape(micro_count * tok, -1)


def shards_fast(
    tokens,
    cotangent,
    w_qkv,
    w_out,
    w_up,
    w_down,
    gain_one,
    bias_one,
    gain_two,
    bias_two,
    lengths,
    slot_order,
):
    micro_count, tok_dev, width = tokens.shape
    rows = micro_count * tok_dev
    scale = (width // HEADS) ** (-0.5)
    bf16, f32 = jnp.bfloat16, jnp.float32
    part = w_qkv.shape[0]
    my_slot = lax.axis_index("seq")

    downs = [w_down[i * part : (i + 1) * part] for i in range(4)]
    norms = jnp.stack([gain_one, bias_one, gain_two, bias_two], 1)
    rem = jnp.concatenate(
        [w_up[:, 512:], w_qkv[:, 384:], w_out[:, 128:]]
        + [down[:, 128:] for down in downs]
        + [norms, jnp.zeros((part, 28), bf16)],
        1,
    )
    gathered = gather_weights(
        [
            w_qkv[:, :384],
            jnp.concatenate([w_out[:, :128], rem, w_up[:, :128]], 1),
            w_up[:, 128:512],
            jnp.concatenate([down[:, :128] for down in downs], 1),
        ]
    )
    full_qkv, full_out, full_up, full_down, full_norms = unpack_weights(gathered)
    full_qkv = full_qkv.reshape(width, -1)
    full_out = full_out.reshape(width, width)
    full_up = full_up.reshape(width, -1)
    full_down = full_down.reshape(-1, width)
    norm_rows = full_norms[:, :, REM_NORM : REM_NORM + 4].reshape(width, 4).T.astype(f32)
    g_one, b_one, g_two, b_two = norm_rows[0], norm_rows[1], norm_rows[2], norm_rows[3]

    unit_ids = my_slot * UNITS + jnp.arange(UNITS, dtype=jnp.int32)
    second = (unit_ids >= HEADS)[:, None]
    doc_ends = jax.vmap(running_total)(lengths[:, 0])
    places = jnp.arange(8 * tok_dev, dtype=jnp.int32)
    segments = jax.vmap(segment_of, (None, 0))(places, doc_ends)
    unit_segments = jnp.where(second, segments[1][None], segments[0][None])
    seg_k, seg_q = unit_segments[:, :, None], unit_segments[:, None, :]
    slots = jnp.arange(8, dtype=jnp.int32)
    holders = jnp.sum(
        jnp.where(slot_order[:, 0][:, None, :] == slots[None, :, None], slots[None, None, :], 0), 2
    )
    order = jnp.where(second, holders[1][None], holders[0][None])

    residual = tokens.astype(f32).reshape(rows, width)
    scaled_one, inv_one = normalize(residual)
    normed_one = (scaled_one * g_one + b_one).astype(bf16)
    qkv_t = lax.dot_general(
        full_qkv, normed_one, (((0,), (1,)), ((), ())), preferred_element_type=f32
    ).astype(bf16)
    unit_qkv = exchange(to_units(qkv_t, micro_count, 3), 0)
    unit_out, lse = attend(unit_qkv, order, seg_k, seg_q, scale)
    attn_flat = from_units(exchange(unit_out, 1), micro_count, 1)
    middle = residual + dot(attn_flat, full_out)
    scaled_two, inv_two = normalize(middle)
    normed_two = (scaled_two * g_two + b_two).astype(bf16)
    hidden = dot(normed_two, full_up)
    activated_full, gelu_back = jax.vjp(gelu_tanh, hidden)
    activated = activated_full.astype(bf16)

    grad_rows = cotangent.reshape(rows, width)
    block_out = (middle + dot(activated, full_down)).astype(bf16)
    grad_hidden = gelu_back(dot_right_t(grad_rows, full_down))[0].astype(bf16)
    sum_down = outer(activated, grad_rows)
    sum_up = dot_left_t(normed_two, grad_hidden).astype(bf16)
    grad_normed_two = dot_right_t(grad_hidden, full_up)
    grad_middle = grad_rows.astype(f32) + norm_back(grad_normed_two, scaled_two, inv_two, g_two)
    grad_branch = grad_middle.astype(bf16)
    sum_proj = dot_left_t(attn_flat, grad_branch).astype(bf16)
    grad_heads_t = dot_right_t(full_out, grad_branch).astype(bf16)
    unit_grad = exchange(to_units(grad_heads_t, micro_count, 1), 2)
    unit_back = attend_back(unit_qkv, unit_grad, order, seg_k, seg_q, lse, scale)
    grad_qkv_rows = from_units(exchange(unit_back, 3), micro_count, 3)
    sum_qkv = dot_left_t(normed_one, grad_qkv_rows).astype(bf16)
    grad_normed_one = dot_right_t(grad_qkv_rows, full_qkv)
    grad_input = (
        grad_middle + norm_back(grad_normed_one, scaled_one, inv_one, g_one)
    ).astype(bf16)

    norm_sums = jnp.stack(
        [
            jnp.sum(grad_normed_one * scaled_one, 0),
            jnp.sum(grad_normed_one, 0),
            jnp.sum(grad_normed_two * scaled_two, 0),
            jnp.sum(grad_normed_two, 0),
        ]
    )
    norm_cols = jnp.pad(norm_sums.T.astype(bf16), ((0, 0), (REM_NORM, 28)))
    sum0, sum1, sum2, sum3 = (
        total.astype(f32)
        for total in scatter_grads(
            pack_grads(
                sum_qkv.reshape(4, part, -1),
                sum_proj.reshape(4, part, -1),
                sum_up.reshape(4, part, -1),
                sum_down.reshape(16, part, -1),
                norm_cols.reshape(4, part, -1),
            )
        )
    )
    rest = sum1[:, TILE : 2 * TILE]
    out_qkv = jnp.concatenate([sum0, rest[:, REM_QKV : REM_QKV + 24]], 1)
    out_proj = jnp.concatenate([sum1[:, :TILE], rest[:, REM_OUT : REM_OUT + 8]], 1)
    out_up = jnp.concatenate([sum1[:, 2 * TILE :], sum2, rest[:, REM_UP : REM_UP + 32]], 1)
    out_down = jnp.concatenate(
        [
            jnp.concatenate(
                [
                    sum3[:, i * TILE : (i + 1) * TILE],
                    rest[:, REM_DOWN + 8 * i : REM_DOWN + 8 * i + 8],
                ],
                1,
            )
            for i in range(4)
        ],
        0,
    )
    norm_mine = rest[:, REM_NORM : REM_NORM + 4].T
    return (
        block_out.reshape(tokens.shape),
        grad_input.reshape(tokens.shape),
        out_qkv,
        out_proj,
        out_up,
        out_down,
        norm_mine[0],
        norm_mine[1],
        norm_mine[2],
        norm_mine[3],
    )


def solution(mesh):
    grid = (mesh.shape["dp"], mesh.shape["seq"])
    return jax.shard_map(
        shards_fast if grid == (4, 8) else shards_plain,
        mesh=mesh,
        in_specs=(
            P(None, ("dp", "seq"), None),
            P(None, ("dp", "seq"), None),
            P("dp", "seq"),
            P("dp", "seq"),
            P("dp", "seq"),
            P("dp", "seq"),
            P("dp"),
            P("dp"),
            P("dp"),
            P("dp"),
            P(None, "dp", None),
            P(None, "dp", None),
        ),
        out_specs=(
            P(None, ("dp", "seq"), None),
            P(None, ("dp", "seq"), None),
            P("dp", "seq"),
            P("dp", "seq"),
            P("dp", "seq"),
            P("dp", "seq"),
            P("dp"),
            P("dp"),
            P("dp"),
            P("dp"),
        ),
        check_vma=False,
    )
```

```python
import functools

import jax
import jax.numpy as jnp
from jax import lax
from jax.experimental import pallas as pl
from jax.experimental.pallas import tpu as pltpu
from jax.sharding import PartitionSpec as P

HEADS = 17


EPS = 1e-05
GELU_C = 0.7978845608028654


def gelu_tanh(values):
    return 0.5 * values * (1.0 + jnp.tanh(GELU_C * (values + 0.044715 * values * values * values)))


def normalize(residual):
    row_mean = jnp.mean(residual, -1, keepdims=True)
    centered = residual - row_mean
    inv_std = lax.rsqrt(jnp.mean(centered * centered, -1, keepdims=True) + EPS)
    return (centered * inv_std, inv_std)


def norm_back(grad_normed, scaled, inv_std, gain_row):
    grad_scaled = grad_normed * gain_row
    return inv_std * (
        grad_scaled
        - jnp.mean(grad_scaled, -1, keepdims=True)
        - scaled * jnp.mean(grad_scaled * scaled, -1, keepdims=True)
    )


def running_total(counts):
    index = jnp.arange(counts.shape[0], dtype=jnp.int32)
    return jnp.sum(jnp.where(index[None, :] <= index[:, None], counts[None, :], 0), 1)


def segment_of(places, doc_ends):
    return jnp.sum((places[:, None] >= doc_ends[None, :]).astype(jnp.int32), 1)


def pair_swap(block):
    route = [(i, i ^ 1) for i in range(lax.axis_size("seq"))]
    return lax.ppermute(block, "seq", route)


def same_core():
    n_seq = lax.axis_size("seq")
    return [list(range(core, n_seq, 2)) for core in range(2)]


def gather_stack(shard):
    chips = lax.all_gather(shard, "seq", axis_index_groups=same_core())
    held = lax.all_gather(chips, "dp")
    other = pair_swap(held)
    first = lax.axis_index("seq") % 2 == 0
    both = jnp.stack([jnp.where(first, held, other), jnp.where(first, other, held)], 2)
    dp, chip_count = held.shape[:2]
    return both.transpose(1, 2, 0, 3, 4).reshape(2 * chip_count, dp, *shard.shape)


def pair_sum(parts):
    pairs = parts.reshape(parts.shape[0] // 2, 2, *parts.shape[1:])
    first = lax.axis_index("seq") % 2 == 0
    mine = jnp.where(first, pairs[:, 0], pairs[:, 1])
    other = jnp.where(first, pairs[:, 1], pairs[:, 0])
    got = pair_swap(other)
    return (mine.astype(jnp.float32) + got.astype(jnp.float32)).astype(jnp.bfloat16)


def scatter_stack(parts, after):
    held = pair_sum(parts).transpose(1, 0, 2, 3).reshape(-1, parts.shape[3])
    if after is not None:
        held, after = lax.optimization_barrier((held, after))
    held = lax.psum_scatter(held, "dp", scatter_dimension=0, tiled=True)
    held = lax.psum_scatter(
        held, "seq", scatter_dimension=0, axis_index_groups=same_core(), tiled=True
    )
    return held, after


def dot(left, right):
    return jnp.dot(left, right, preferred_element_type=jnp.float32)


def dot_right_t(left, right):
    return lax.dot_general(left, right, (((1,), (1,)), ((), ())), preferred_element_type=jnp.float32)


def dot_left_t(left, right):
    return lax.dot_general(left, right, (((0,), (0,)), ((), ())), preferred_element_type=jnp.float32)


def cols_of(rows, count):
    return rows.reshape(rows.shape[0], count, -1).transpose(1, 0, 2)


def apply_cols(rows, cols):
    lifted = jnp.broadcast_to(rows[None], (cols.shape[0],) + rows.shape)
    made = lax.dot_general(
        lifted, cols, (((2,), (1,)), ((0,), (0,))), preferred_element_type=jnp.float32
    )
    return made.transpose(1, 0, 2).reshape(rows.shape[0], -1)


def apply_cols_t(rows, cols):
    lifted = cols_of(rows, cols.shape[0])
    return lax.dot_general(
        lifted, cols, (((0, 2), (0, 2)), ((), ())), preferred_element_type=jnp.float32
    )


def grad_cols(left, right, count):
    lifted = jnp.broadcast_to(left[None], (count,) + left.shape)
    return lax.dot_general(
        lifted, cols_of(right, count), (((1,), (1,)), ((0,), (0,))),
        preferred_element_type=jnp.float32,
    )


def heads_of(rows, micro_count, head_dim):
    return rows.reshape(micro_count, -1, HEADS, head_dim).transpose(0, 2, 1, 3)


def rows_of(heads):
    micro_count, _, slots, head_dim = heads.shape
    return heads.transpose(0, 2, 1, 3).reshape(micro_count * slots, HEADS * head_dim)


def batched(left, right, left_dim, right_dim):
    return lax.dot_general(
        left,
        right,
        (((left_dim,), (right_dim,)), ((0, 1), (0, 1))),
        preferred_element_type=jnp.float32,
    )


def shards_plain(
    tokens,
    cotangent,
    w_qkv,
    w_out,
    w_up,
    w_down,
    gain_one,
    bias_one,
    gain_two,
    bias_two,
    lengths,
    slot_order,
):
    micro_count, tok_dev, width = tokens.shape
    rows = micro_count * tok_dev
    head_dim = width // HEADS
    score_scale = head_dim ** (-0.5)
    n_seq = lax.axis_size("seq")
    my_slot = lax.axis_index("seq")
    bf16 = jnp.bfloat16

    norms = lax.all_gather(
        jnp.stack([gain_one, bias_one, gain_two, bias_two]), "dp", axis=1, tiled=True
    ).astype(jnp.float32)
    g_one, b_one, g_two, b_two = norms[0], norms[1], norms[2], norms[3]
    n_dp = lax.axis_size("dp")
    part, qkv_cols = w_qkv.shape
    out_cols = w_out.shape[1]
    up_cols = w_up.shape[1]
    fold = w_down.shape[0] // up_cols
    attn_stack = gather_stack(jnp.concatenate([w_qkv, w_out], 1))
    down_t = w_down.T
    ffn_stack = gather_stack(
        jnp.concatenate([w_up, *jnp.split(down_t, fold, 1)], 0)
    )
    cols_qkv = attn_stack[..., :qkv_cols].reshape(n_seq, width, qkv_cols)
    full_out = (
        attn_stack[..., qkv_cols:].reshape(n_seq, width, out_cols).transpose(1, 0, 2)
    ).reshape(width, width)
    cols_up = ffn_stack[:, :, :part].reshape(n_seq, width, up_cols)
    full_down_t = (
        ffn_stack[:, :, part:]
        .reshape(n_seq, n_dp, fold, out_cols, up_cols)
        .transpose(0, 3, 1, 2, 4)
        .reshape(width, fold * n_dp * up_cols)
    )

    doc_ends = jax.vmap(running_total)(lengths[:, 0])
    k_place = (
        slot_order[:, 0, :, None] * tok_dev + jnp.arange(tok_dev, dtype=jnp.int32)
    ).reshape(micro_count, n_seq * tok_dev)
    k_segment = jax.vmap(segment_of)(k_place, doc_ends)
    base_slot = lax.dynamic_slice_in_dim(slot_order[:, 0], my_slot, 1, 1)
    q_place = base_slot * tok_dev + jnp.arange(tok_dev, dtype=jnp.int32)
    q_segment = jax.vmap(segment_of)(q_place, doc_ends)
    allowed = (q_segment[:, :, None] == k_segment[:, None, :]) & (
        k_place[:, None, :] <= q_place[:, :, None]
    )

    residual = tokens.astype(jnp.float32).reshape(rows, width)
    scaled_one, inv_one = normalize(residual)
    normed_one = (scaled_one * g_one + b_one).astype(bf16)
    qkv_all = apply_cols(normed_one, cols_qkv).astype(bf16)
    queries = heads_of(qkv_all[:, :width], micro_count, head_dim)
    local_kv = qkv_all[:, width:].reshape(micro_count, tok_dev, 2 * width)
    group_kv = lax.all_gather(local_kv, "seq", axis=1, tiled=True)
    keys = heads_of(group_kv[..., :width], micro_count, head_dim)
    values = heads_of(group_kv[..., width:], micro_count, head_dim)

    scores = batched(queries, keys, 3, 3) * score_scale
    scores = jnp.where(allowed[:, None], scores, -jnp.inf)
    weights = jnp.exp(scores - jnp.max(scores, -1, keepdims=True))
    probs = weights * (1.0 / jnp.sum(weights, -1, keepdims=True))
    probs_low = probs.astype(bf16)
    attended = batched(probs_low, values, 3, 2)
    attn_flat = rows_of(attended.astype(bf16))
    middle = residual + dot(attn_flat, full_out)
    scaled_two, inv_two = normalize(middle)
    normed_two = (scaled_two * g_two + b_two).astype(bf16)
    hidden = apply_cols(normed_two, cols_up)
    activated_full, gelu_back = jax.vjp(gelu_tanh, hidden)
    activated = activated_full.astype(bf16)

    grad_rows = cotangent.reshape(rows, width)
    block_out = (middle + dot_right_t(activated, full_down_t)).astype(bf16)
    grad_hidden = gelu_back(dot(grad_rows, full_down_t))[0].astype(bf16)
    sum_down_t = dot_left_t(grad_rows, activated).astype(bf16)
    sum_down_t = (
        sum_down_t.reshape(n_seq, out_cols, n_dp, fold, up_cols)
        .transpose(0, 2, 3, 1, 4)
        .reshape(n_seq, n_dp, fold * out_cols, up_cols)
    )
    sum_up = grad_cols(normed_two, grad_hidden, n_seq).astype(bf16)
    sum_ffn, _ = scatter_stack(
        jnp.concatenate([sum_up.reshape(n_seq, n_dp, part, up_cols), sum_down_t], 2), None
    )
    grad_normed_two = apply_cols_t(grad_hidden, cols_up)
    grad_middle = grad_rows.astype(jnp.float32) + norm_back(
        grad_normed_two, scaled_two, inv_two, g_two
    )
    grad_branch = grad_middle.astype(bf16)
    sum_proj = grad_cols(attn_flat, grad_branch, n_seq).astype(bf16)
    grad_heads = heads_of(
        dot_right_t(grad_branch, full_out).astype(bf16), micro_count, head_dim
    )

    grad_probs = batched(grad_heads, values, 3, 3)
    row_dot = jnp.sum(probs * grad_probs, -1, keepdims=True)
    grad_scores = (probs * (grad_probs - row_dot)).astype(bf16)
    grad_query = rows_of(batched(grad_scores, keys, 3, 2) * score_scale)
    grad_keys = rows_of(batched(grad_scores, queries, 2, 2) * score_scale)
    grad_values = rows_of(batched(probs_low, grad_heads, 2, 2))
    grad_kv = jnp.concatenate([grad_keys.astype(bf16), grad_values.astype(bf16)], 1)
    grad_kv = grad_kv.reshape(micro_count, n_seq, tok_dev, 2 * width).transpose(1, 0, 2, 3)
    grad_kv = lax.psum_scatter(
        pair_sum(grad_kv), "seq", scatter_dimension=0, axis_index_groups=same_core()
    ).reshape(rows, 2 * width)
    grad_qkv_rows = jnp.concatenate([grad_query.astype(bf16), grad_kv], 1)
    sum_qkv = grad_cols(normed_one, grad_qkv_rows, n_seq).astype(bf16)
    sum_attn, sum_ffn = scatter_stack(
        jnp.concatenate([sum_qkv, sum_proj], 2).reshape(n_seq, n_dp, part, qkv_cols + out_cols),
        sum_ffn,
    )
    sum_attn = sum_attn.astype(jnp.float32)
    sum_ffn = sum_ffn.astype(jnp.float32)
    out_up = sum_ffn[:part]
    out_down = jnp.concatenate(jnp.split(sum_ffn[part:], fold, 0), 1).T
    out_qkv = sum_attn[:, :qkv_cols]
    out_proj = sum_attn[:, qkv_cols:]
    grad_normed_one = apply_cols_t(grad_qkv_rows, cols_qkv)
    grad_input = (
        grad_middle + norm_back(grad_normed_one, scaled_one, inv_one, g_one)
    ).astype(bf16)

    norm_sums = jnp.stack(
        [
            jnp.sum(grad_normed_one * scaled_one, 0),
            jnp.sum(grad_normed_one, 0),
            jnp.sum(grad_normed_two * scaled_two, 0),
            jnp.sum(grad_normed_two, 0),
        ]
    )
    norm_totals = lax.psum(norm_sums, ("dp", "seq"))
    norm_mine = lax.dynamic_slice_in_dim(norm_totals, lax.axis_index("dp") * part, part, 1)
    return (
        block_out.reshape(tokens.shape),
        grad_input.reshape(tokens.shape),
        out_qkv,
        out_proj,
        out_up,
        out_down,
        norm_mine[0],
        norm_mine[1],
        norm_mine[2],
        norm_mine[3],
    )


MESH = pl.DeviceIdType.MESH
GATHER_ORDERS = ((2, 3, 0, 1), (2, 3, 1, 0), (0, 2, 3, 1), (3, 2, 1, 0))
SCATTER_ORDERS = GATHER_ORDERS
ROW_CUTS = ((0, 64), (64, 64), (128, 64), (192, 80))
CHUNKS = tuple((q, r) for pair in ((0, 1), (2, 3)) for r in range(4) for q in pair)
GATHER_LAGS = (0, 2, 4, 6, 9)
SCATTER_LAGS = (0, 3, 5, 7, 9)
AHEAD = 4
TILE = 128
LANES = (3 * TILE, 3 * TILE, 3 * TILE, 4 * TILE)
UNITS = 5
IDLE = 7
REM_UP, REM_QKV, REM_OUT, REM_DOWN, REM_NORM = 0, 32, 56, 64, 96


def place_of(order, dp, seq):
    z = seq // 2
    bits = (dp % 2, dp // 2, (z % 2 + z // 2) % 2, z // 2)
    return sum(bits[dim] * 2**k for k, dim in enumerate(order))


def partner(dim):
    dp, seq = lax.axis_index("dp"), lax.axis_index("seq")
    z, core = seq // 2, seq % 2
    if dim == 0:
        return (dp + 1 - 2 * (dp % 2), seq)
    if dim == 1:
        return (dp + 2 - 4 * (dp // 2), seq)
    if dim == 2:
        return (dp, (z + 1 - 2 * (z % 2)) * 2 + core)
    return (dp, (3 - z) * 2 + core)


def sibling():
    dp, seq = lax.axis_index("dp"), lax.axis_index("seq")
    return (dp, seq + 1 - 2 * (seq % 2))


def greet(devices):
    barrier = pltpu.get_barrier_semaphore()
    for device in devices:
        pl.semaphore_signal(barrier, inc=1, device_id=device, device_id_type=MESH)
    pl.semaphore_wait(barrier, len(devices))


def send(src, dst, send_sem, recv_sem, device):
    copy = pltpu.make_async_remote_copy(
        src_ref=src, dst_ref=dst, send_sem=send_sem, recv_sem=recv_sem,
        device_id=device, device_id_type=MESH,
    )
    copy.start()
    return copy


def gather_kernel(*refs):
    shards_in, full = refs[:4], refs[4:8]
    own_sem, link_send, link_recv, sib_send, sib_recv = refs[8:]
    dp, seq = lax.axis_index("dp"), lax.axis_index("seq")
    core = seq % 2
    greet([partner(dim) for dim in range(4)] + [sibling()])
    at = [place_of(GATHER_ORDERS[q], dp, seq) for q in range(4)]
    owns, links, sides = {}, {}, []

    def step(chunk, stage):
        q, r = CHUNKS[chunk]
        span = pl.ds(*ROW_CUTS[r])
        size = 2**stage
        if stage == 0:
            fresh, target = shards_in[q].at[span], full[q].at[core, at[q], span]
            links[chunk] = send(
                fresh, target, link_send.at[chunk, 0], link_recv.at[chunk, 0],
                partner(GATHER_ORDERS[q][0]),
            )
            owns[chunk] = pltpu.make_async_copy(fresh, target, own_sem.at[chunk])
            owns[chunk].start()
            sides.append(
                send(fresh, target, sib_send.at[chunk, 0], sib_recv.at[chunk, 0], sibling())
            )
            return
        links[chunk].wait()
        if stage == 1:
            owns[chunk].wait()
        if stage < 4:
            held = full[q].at[core, pl.ds(at[q] // size * size, size), span]
            links[chunk] = send(
                held, held, link_send.at[chunk, stage], link_recv.at[chunk, stage],
                partner(GATHER_ORDERS[q][stage]),
            )
        half = size // 2
        mine = at[q] // half
        got = full[q].at[core, pl.ds((mine + 1 - 2 * (mine % 2)) * half, half), span]
        sides.append(
            send(got, got, sib_send.at[chunk, stage], sib_recv.at[chunk, stage], sibling())
        )

    for turn in range(len(CHUNKS) + GATHER_LAGS[4]):
        for stage in (4, 3, 2, 1, 0):
            lag = GATHER_LAGS[stage]
            if 0 <= turn - lag < len(CHUNKS):
                step(turn - lag, stage)
    for side in sides:
        side.wait()


def gather_weights(chunks):
    rows = chunks[0].shape[0]
    anywhere = pl.BlockSpec(memory_space=pl.ANY)
    dma = pltpu.SemaphoreType.DMA
    return pl.pallas_call(
        gather_kernel,
        out_shape=[jax.ShapeDtypeStruct((2, 16, rows, lanes), jnp.bfloat16) for lanes in LANES],
        in_specs=[anywhere] * 4,
        out_specs=[anywhere] * 4,
        scratch_shapes=[dma((16,)), dma((16, 4)), dma((16, 4)), dma((16, 5)), dma((16, 5))],
        compiler_params=pltpu.CompilerParams(collective_id=0, has_side_effects=True),
        name="gather_weights",
    )(*chunks)


def scatter_kernel(*refs):
    parts, outs = refs[:4], refs[4:8]
    own, acc, got3, got2, got1, got0 = (refs[8 + 4 * i : 12 + 4 * i] for i in range(6))
    got = (got0, got1, got2, got3)
    own_sem, link_send, link_recv, sib_send, sib_recv = refs[32:]
    dp, seq = lax.axis_index("dp"), lax.axis_index("seq")
    core = seq % 2
    greet([partner(dim) for dim in range(4)] + [sibling()])
    at = [place_of(SCATTER_ORDERS[q], dp, seq) for q in range(4)]
    side, load, links = {}, {}, {}

    def begin(chunk):
        q, r = CHUNKS[chunk]
        rows = pl.ds(*ROW_CUTS[r])
        side[chunk] = send(
            parts[q].at[1 - core, :, rows], acc[q].at[:, rows],
            sib_send.at[chunk], sib_recv.at[chunk], sibling(),
        )
        load[chunk] = pltpu.make_async_copy(
            parts[q].at[core, :, rows], own[q].at[:, rows], own_sem.at[chunk]
        )
        load[chunk].start()

    for chunk in range(AHEAD):
        begin(chunk)

    def add(chunk, base, other, other_base, count):
        q, r = CHUNKS[chunk]
        rows = pl.ds(*ROW_CUTS[r])

        def one(b, carry):
            acc[q][base + b, rows] = acc[q][base + b, rows] + other[other_base + b, rows]
            return carry

        lax.fori_loop(0, count, one, 0)

    def step(chunk, stage):
        q, r = CHUNKS[chunk]
        rows = pl.ds(*ROW_CUTS[r])
        half = 2**stage
        base = at[q] // (2 * half) * (2 * half)
        high = at[q] // half % 2
        away, keep = (1 - high) * half, high * half
        if stage == 3:
            side[chunk].wait_recv()
            load[chunk].wait()
            other = own[q]
        else:
            links[chunk, stage + 1].wait_recv()
            other = got[stage + 1][q]
        add(chunk, base + away, other, away, half)
        links[chunk, stage] = send(
            acc[q].at[pl.ds(base + away, half), rows], got[stage][q].at[:, rows],
            link_send.at[chunk, stage], link_recv.at[chunk, stage], partner(SCATTER_ORDERS[q][stage]),
        )
        add(chunk, base + keep, other, keep, half)

    for turn in range(len(CHUNKS) + SCATTER_LAGS[4]):
        if turn + AHEAD < len(CHUNKS):
            begin(turn + AHEAD)
        for stage in (-1, 0, 1, 2, 3):
            lag = SCATTER_LAGS[3 - stage]
            chunk = turn - lag
            if 0 <= chunk < len(CHUNKS):
                if stage >= 0:
                    step(chunk, stage)
                    continue
                q, r = CHUNKS[chunk]
                rows = pl.ds(*ROW_CUTS[r])
                links[chunk, 0].wait_recv()
                outs[q][rows] = acc[q][at[q], rows] + got0[q][0, rows]
    for copy in list(side.values()) + list(links.values()):
        copy.wait_send()


def scatter_grads(parts):
    rows = parts[0].shape[2]
    dma = pltpu.SemaphoreType.DMA
    bf16 = jnp.bfloat16
    buffers = [
        pltpu.VMEM((count, rows, lanes), bf16) for count in (16, 16, 8, 4, 2, 1) for lanes in LANES
    ]
    return pl.pallas_call(
        scatter_kernel,
        out_shape=[jax.ShapeDtypeStruct((rows, lanes), bf16) for lanes in LANES],
        in_specs=[pl.BlockSpec(memory_space=pl.ANY)] * 4,
        out_specs=[pl.BlockSpec(memory_space=pltpu.VMEM)] * 4,
        scratch_shapes=buffers + [dma((16,)), dma((16, 4)), dma((16, 4)), dma((16,)), dma((16,))],
        compiler_params=pltpu.CompilerParams(
            collective_id=1, has_side_effects=True, vmem_limit_bytes=56 * 2**20
        ),
        name="scatter_grads",
    )(*parts)


def exchange_kernel(to_owners, blocks, out, own_sem, send_sem, recv_sem):
    dp, seq = lax.axis_index("dp"), lax.axis_index("seq")
    others = [(dp, (seq + k) % 8) for k in range(1, 8)]
    greet(others)
    own = pltpu.make_async_copy(blocks.at[seq], out.at[seq], own_sem)
    copies = [
        pltpu.make_async_remote_copy(
            src_ref=blocks.at[device[1]], dst_ref=out.at[seq], send_sem=send_sem.at[k],
            recv_sem=recv_sem.at[k], device_id=device, device_id_type=MESH,
        )
        for k, device in enumerate(others)
    ]
    for k, copy in enumerate(copies):
        pl.when((others[k][1] if to_owners else seq) != IDLE)(copy.start)
    own.start()
    own.wait()
    for k, copy in enumerate(copies):
        pl.when((others[k][1] if to_owners else seq) != IDLE)(copy.wait_send)
        pl.when((seq if to_owners else (seq + 7 - k) % 8) != IDLE)(copy.wait_recv)


def exchange(blocks, which):
    dma = pltpu.SemaphoreType.DMA
    return pl.pallas_call(
        functools.partial(exchange_kernel, which % 2 == 0),
        out_shape=jax.ShapeDtypeStruct(blocks.shape, blocks.dtype),
        in_specs=[pl.BlockSpec(memory_space=pl.ANY)],
        out_specs=pl.BlockSpec(memory_space=pl.ANY),
        scratch_shapes=[dma, dma((7,)), dma((7,))],
        compiler_params=pltpu.CompilerParams(collective_id=2 + which, has_side_effects=True),
        name=f"exchange_{which}",
    )(blocks)


def spots():
    for dp in range(4):
        for seq in range(8):
            yield dp, seq, seq % 2, [place_of(SCATTER_ORDERS[q], dp, seq) for q in range(4)]


def unpack_kernel(c0, c1, c2, c3, qkv, out, up, down, norms):
    for dp in range(4):
        pieces = [[] for _ in range(7)]
        for s in range(8):
            at = [place_of(GATHER_ORDERS[q], dp, s) for q in range(4)]
            core = s % 2
            rem = c1[core, at[1], :, TILE : 2 * TILE]
            if s == 0:
                norms[dp] = rem
            pieces[0] += [c0[core, at[0]], rem[:, REM_QKV : REM_QKV + 24]]
            pieces[1] += [c1[core, at[1], :, :TILE], rem[:, REM_OUT : REM_OUT + 8]]
            pieces[2] += [
                c1[core, at[1], :, 2 * TILE :], c2[core, at[2]], rem[:, REM_UP : REM_UP + 32]
            ]
            for i in range(4):
                pieces[3 + i] += [
                    c3[core, at[3], :, i * TILE : (i + 1) * TILE],
                    rem[:, REM_DOWN + 8 * i : REM_DOWN + 8 * i + 8],
                ]
        qkv[dp] = jnp.concatenate(pieces[0], 1)
        out[dp] = jnp.concatenate(pieces[1], 1)
        up[dp] = jnp.concatenate(pieces[2], 1)
        for i in range(4):
            down[dp * 4 + i] = jnp.concatenate(pieces[3 + i], 1)


def unpack_weights(chunks):
    bf16 = jnp.bfloat16
    rows, step = chunks[0].shape[2], 16

    def spec(count, lanes):
        return pl.BlockSpec((count, step, lanes), lambda i: (0, i, 0))

    sizes = ((4, 3264), (4, 1088), (4, 4352), (16, 1088), (4, 128))
    return pl.pallas_call(
        unpack_kernel,
        grid=(rows // step,),
        out_shape=[jax.ShapeDtypeStruct((count, rows, lanes), bf16) for count, lanes in sizes],
        in_specs=[pl.BlockSpec((2, 16, step, lanes), lambda i: (0, 0, i, 0)) for lanes in LANES],
        out_specs=[spec(*size) for size in sizes],
        compiler_params=pltpu.CompilerParams(vmem_limit_bytes=40 * 2**20),
        name="unpack_weights",
    )(*chunks)


def pack_kernel(qkv, out, up, down, norms, c0, c1, c2, c3):
    for dp, s, core, at in spots():
        c0[core, at[0]] = qkv[dp, :, s * 408 : s * 408 + 384]
        c1[core, at[1], :, :TILE] = out[dp, :, s * 136 : s * 136 + 128]
        c1[core, at[1], :, 2 * TILE :] = up[dp, :, s * 544 : s * 544 + 128]
        c2[core, at[2]] = up[dp, :, s * 544 + 128 : s * 544 + 512]
        base = at[1]
        c1[core, base, :, TILE : 2 * TILE] = norms[dp]
        c1[core, base, :, TILE + REM_UP : TILE + REM_UP + 32] = up[dp, :, s * 544 + 512 : s * 544 + 544]
        c1[core, base, :, TILE + REM_QKV : TILE + REM_QKV + 24] = qkv[dp, :, s * 408 + 384 : s * 408 + 408]
        c1[core, base, :, TILE + REM_OUT : TILE + REM_OUT + 8] = out[dp, :, s * 136 + 128 : s * 136 + 136]
        for i in range(4):
            c3[core, at[3], :, i * TILE : (i + 1) * TILE] = down[dp * 4 + i, :, s * 136 : s * 136 + 128]
            spot = TILE + REM_DOWN + 8 * i
            c1[core, base, :, spot : spot + 8] = down[dp * 4 + i, :, s * 136 + 128 : s * 136 + 136]


def pack_grads(qkv, out, up, down, norms):
    rows, step = qkv.shape[1], 16

    def spec(count, lanes):
        return pl.BlockSpec((count, step, lanes), lambda i: (0, i, 0))

    return pl.pallas_call(
        pack_kernel,
        grid=(rows // step,),
        out_shape=[jax.ShapeDtypeStruct((2, 16, rows, lanes), jnp.bfloat16) for lanes in LANES],
        in_specs=[spec(4, 3264), spec(4, 1088), spec(4, 4352), spec(16, 1088), spec(4, 128)],
        out_specs=[pl.BlockSpec((2, 16, step, lanes), lambda i: (0, 0, i, 0)) for lanes in LANES],
        compiler_params=pltpu.CompilerParams(vmem_limit_bytes=40 * 2**20),
        name="pack_grads",
    )(qkv, out, up, down, norms)


QUERY_BLOCK = 256


def flip(block):
    return block.astype(jnp.float32).T.astype(jnp.bfloat16)


def outer_kernel(left, right, out):
    out[...] = dot(flip(left[...]), right[...]).astype(out.dtype)


def outer(left, right):
    rows, width = left.shape
    step = 2 * TILE
    return pl.pallas_call(
        outer_kernel,
        grid=(width // step,),
        out_shape=jax.ShapeDtypeStruct((width, right.shape[1]), jnp.bfloat16),
        in_specs=[
            pl.BlockSpec((rows, step), lambda i: (0, i)),
            pl.BlockSpec(right.shape, lambda i: (0, 0)),
        ],
        out_specs=pl.BlockSpec((step, right.shape[1]), lambda i: (i, 0)),
        compiler_params=pltpu.CompilerParams(vmem_limit_bytes=24 * 2**20),
        cost_estimate=pl.CostEstimate(
            flops=2 * rows * width * right.shape[1],
            bytes_accessed=2 * width * (right.shape[1] + rows),
            transcendentals=0,
        ),
        name="outer",
    )(left, right)


def masked_scores(k_rows, q_cols, seg_k, seg_q, start, scale):
    count, width = k_rows.shape[0], q_cols.shape[1]
    scores = dot(k_rows, q_cols) * scale
    key_at = lax.broadcasted_iota(jnp.int32, (count, width), 0)
    query_at = lax.broadcasted_iota(jnp.int32, (count, width), 1) + start
    return jnp.where((seg_k == seg_q) & (key_at <= query_at), scores, -1e30)


def attend_kernel(scale, order, x, seg_k, seg_q, out, lse, q_t, k_t, v_t, o_t):
    unit = pl.program_id(0)
    slots = x.shape[0]
    tok = x.shape[3]
    depth = q_t.shape[0]
    for b in range(slots):
        at = order[unit, b]
        for n, held in enumerate((q_t, k_t, v_t)):
            held[:, b * tok : (b + 1) * tok] = x[at, 0, n * depth : (n + 1) * depth]
    keys = flip(k_t[...])
    for start in range(0, slots * tok, QUERY_BLOCK):
        count = start + QUERY_BLOCK
        cols = slice(start, count)
        scores = masked_scores(
            keys[:count], q_t[:, cols], seg_k[0, :count], seg_q[0, :, cols], start, scale
        )
        top = jnp.max(scores, 0, keepdims=True)
        weights = jnp.exp(scores - top)
        total = jnp.sum(weights, 0, keepdims=True)
        probs = (weights * (1.0 / total)).astype(jnp.bfloat16)
        o_t[:, cols] = dot(v_t[:, :count], probs).astype(jnp.bfloat16)
        lse[0, :, cols] = top + jnp.log(total)
    for b in range(slots):
        out[order[unit, b], 0] = o_t[:, b * tok : (b + 1) * tok]


def attend(x, order, seg_k, seg_q, scale):
    slots, units, depth3, tok = x.shape
    depth, length = depth3 // 3, slots * tok
    bf16 = jnp.bfloat16
    held = [pltpu.VMEM((depth, length), bf16)] * 4
    return pl.pallas_call(
        functools.partial(attend_kernel, scale),
        grid_spec=pltpu.PrefetchScalarGridSpec(
            num_scalar_prefetch=1,
            grid=(units,),
            in_specs=[
                pl.BlockSpec((slots, 1, depth3, tok), lambda u, o: (0, u, 0, 0)),
                pl.BlockSpec((1, length, 1), lambda u, o: (u, 0, 0)),
                pl.BlockSpec((1, 1, length), lambda u, o: (u, 0, 0)),
            ],
            out_specs=[
                pl.BlockSpec((slots, 1, depth, tok), lambda u, o: (0, u, 0, 0)),
                pl.BlockSpec((1, 1, length), lambda u, o: (u, 0, 0)),
            ],
            scratch_shapes=held,
        ),
        out_shape=[
            jax.ShapeDtypeStruct((slots, units, depth, tok), bf16),
            jax.ShapeDtypeStruct((units, 1, length), jnp.float32),
        ],
        compiler_params=pltpu.CompilerParams(vmem_limit_bytes=40 * 2**20),
        name="attend",
    )(order, x, seg_k, seg_q)


def attend_back_kernel(
    scale, order, x, g, seg_k, seg_q, lse, out, q_t, k_t, v_t, g_t, dq_t, dk_t, dv_t
):
    unit = pl.program_id(0)
    slots = x.shape[0]
    tok = x.shape[3]
    depth = q_t.shape[0]
    for b in range(slots):
        at = order[unit, b]
        for n, held in enumerate((q_t, k_t, v_t)):
            held[:, b * tok : (b + 1) * tok] = x[at, 0, n * depth : (n + 1) * depth]
        g_t[:, b * tok : (b + 1) * tok] = g[at, 0]
    keys = flip(k_t[...])
    values = flip(v_t[...])
    length = slots * tok
    for start in reversed(range(0, length, QUERY_BLOCK)):
        count = start + QUERY_BLOCK
        cols = slice(start, count)
        queries, grads = q_t[:, cols], g_t[:, cols]
        scores = masked_scores(
            keys[:count], queries, seg_k[0, :count], seg_q[0, :, cols], start, scale
        )
        probs = jnp.exp(scores - lse[0, :, cols])
        grad_probs = dot(values[:count], grads)
        row_dot = jnp.sum(probs * grad_probs, 0, keepdims=True)
        grad_scores = (probs * (grad_probs - row_dot)).astype(jnp.bfloat16)
        probs_low = probs.astype(jnp.bfloat16)
        dq_t[:, cols] = dot(k_t[:, :count], grad_scores) * scale
        dk = dot_right_t(queries, grad_scores)
        dv = dot_right_t(grads, probs_low)
        if count == length:
            dk_t[...] = dk
            dv_t[...] = dv
        else:
            dk_t[:, :count] += dk
            dv_t[:, :count] += dv
    for b in range(slots):
        at = order[unit, b]
        cols = slice(b * tok, (b + 1) * tok)
        out[at, 0, :depth] = dq_t[:, cols].astype(jnp.bfloat16)
        out[at, 0, depth : 2 * depth] = (dk_t[:, cols] * scale).astype(jnp.bfloat16)
        out[at, 0, 2 * depth :] = dv_t[:, cols].astype(jnp.bfloat16)


def attend_back(x, g, order, seg_k, seg_q, lse, scale):
    slots, units, depth3, tok = x.shape
    depth, length = depth3 // 3, slots * tok
    bf16 = jnp.bfloat16
    held = [pltpu.VMEM((depth, length), bf16)] * 4 + [pltpu.VMEM((depth, length), jnp.float32)] * 3
    return pl.pallas_call(
        functools.partial(attend_back_kernel, scale),
        grid_spec=pltpu.PrefetchScalarGridSpec(
            num_scalar_prefetch=1,
            grid=(units,),
            in_specs=[
                pl.BlockSpec((slots, 1, depth3, tok), lambda u, o: (0, u, 0, 0)),
                pl.BlockSpec((slots, 1, depth, tok), lambda u, o: (0, u, 0, 0)),
                pl.BlockSpec((1, length, 1), lambda u, o: (u, 0, 0)),
                pl.BlockSpec((1, 1, length), lambda u, o: (u, 0, 0)),
                pl.BlockSpec((1, 1, length), lambda u, o: (u, 0, 0)),
            ],
            out_specs=pl.BlockSpec((slots, 1, depth3, tok), lambda u, o: (0, u, 0, 0)),
            scratch_shapes=held,
        ),
        out_shape=jax.ShapeDtypeStruct(x.shape, bf16),
        compiler_params=pltpu.CompilerParams(vmem_limit_bytes=48 * 2**20),
        name="attend_back",
    )(order, x, g, seg_k, seg_q, lse)


def to_units(flat, micro_count, kinds):
    tok = flat.shape[1] // micro_count
    units = flat.reshape(kinds, HEADS, -1, micro_count, tok).transpose(3, 1, 0, 2, 4)
    units = units.reshape(micro_count * HEADS, -1, tok)
    units = jnp.pad(units, ((0, 8 * UNITS - units.shape[0]), (0, 0), (0, 0)))
    return units.reshape(8, UNITS, -1, tok)


def from_units(units, micro_count, kinds):
    tok = units.shape[3]
    held = units.reshape(8 * UNITS, -1, tok)[: micro_count * HEADS]
    held = held.reshape(micro_count, HEADS, kinds, -1, tok).transpose(0, 4, 2, 1, 3)
    return held.reshape(micro_count * tok, -1)


def shards_fast(
    tokens,
    cotangent,
    w_qkv,
    w_out,
    w_up,
    w_down,
    gain_one,
    bias_one,
    gain_two,
    bias_two,
    lengths,
    slot_order,
):
    micro_count, tok_dev, width = tokens.shape
    rows = micro_count * tok_dev
    scale = (width // HEADS) ** (-0.5)
    bf16, f32 = jnp.bfloat16, jnp.float32
    part = w_qkv.shape[0]
    my_slot = lax.axis_index("seq")

    downs = [w_down[i * part : (i + 1) * part] for i in range(4)]
    norms = jnp.stack([gain_one, bias_one, gain_two, bias_two], 1)
    rem = jnp.concatenate(
        [w_up[:, 512:], w_qkv[:, 384:], w_out[:, 128:]]
        + [down[:, 128:] for down in downs]
        + [norms, jnp.zeros((part, 28), bf16)],
        1,
    )
    gathered = gather_weights(
        [
            w_qkv[:, :384],
            jnp.concatenate([w_out[:, :128], rem, w_up[:, :128]], 1),
            w_up[:, 128:512],
            jnp.concatenate([down[:, :128] for down in downs], 1),
        ]
    )
    full_qkv, full_out, full_up, full_down, full_norms = unpack_weights(gathered)
    full_qkv = full_qkv.reshape(width, -1)
    full_out = full_out.reshape(width, width)
    full_up = full_up.reshape(width, -1)
    full_down = full_down.reshape(-1, width)
    norm_rows = full_norms[:, :, REM_NORM : REM_NORM + 4].reshape(width, 4).T.astype(f32)
    g_one, b_one, g_two, b_two = norm_rows[0], norm_rows[1], norm_rows[2], norm_rows[3]

    unit_ids = my_slot * UNITS + jnp.arange(UNITS, dtype=jnp.int32)
    second = (unit_ids >= HEADS)[:, None]
    doc_ends = jax.vmap(running_total)(lengths[:, 0])
    places = jnp.arange(8 * tok_dev, dtype=jnp.int32)
    segments = jax.vmap(segment_of, (None, 0))(places, doc_ends)
    unit_segments = jnp.where(second, segments[1][None], segments[0][None])
    seg_k, seg_q = unit_segments[:, :, None], unit_segments[:, None, :]
    slots = jnp.arange(8, dtype=jnp.int32)
    holders = jnp.sum(
        jnp.where(slot_order[:, 0][:, None, :] == slots[None, :, None], slots[None, None, :], 0), 2
    )
    order = jnp.where(second, holders[1][None], holders[0][None])

    residual = tokens.astype(f32).reshape(rows, width)
    scaled_one, inv_one = normalize(residual)
    normed_one = (scaled_one * g_one + b_one).astype(bf16)
    qkv_t = lax.dot_general(
        full_qkv, normed_one, (((0,), (1,)), ((), ())), preferred_element_type=f32
    ).astype(bf16)
    unit_qkv = exchange(to_units(qkv_t, micro_count, 3), 0)
    unit_out, lse = attend(unit_qkv, order, seg_k, seg_q, scale)
    attn_flat = from_units(exchange(unit_out, 1), micro_count, 1)
    middle = residual + dot(attn_flat, full_out)
    scaled_two, inv_two = normalize(middle)
    normed_two = (scaled_two * g_two + b_two).astype(bf16)
    hidden = dot(normed_two, full_up)
    activated_full, gelu_back = jax.vjp(gelu_tanh, hidden)
    activated = activated_full.astype(bf16)

    grad_rows = cotangent.reshape(rows, width)
    block_out = (middle + dot(activated, full_down)).astype(bf16)
    grad_hidden = gelu_back(dot_right_t(grad_rows, full_down))[0].astype(bf16)
    sum_down = outer(activated, grad_rows)
    sum_up = dot_left_t(normed_two, grad_hidden).astype(bf16)
    grad_normed_two = dot_right_t(grad_hidden, full_up)
    grad_middle = grad_rows.astype(f32) + norm_back(grad_normed_two, scaled_two, inv_two, g_two)
    grad_branch = grad_middle.astype(bf16)
    sum_proj = dot_left_t(attn_flat, grad_branch).astype(bf16)
    grad_heads_t = dot_right_t(full_out, grad_branch).astype(bf16)
    unit_grad = exchange(to_units(grad_heads_t, micro_count, 1), 2)
    unit_back = attend_back(unit_qkv, unit_grad, order, seg_k, seg_q, lse, scale)
    grad_qkv_rows = from_units(exchange(unit_back, 3), micro_count, 3)
    sum_qkv = dot_left_t(normed_one, grad_qkv_rows).astype(bf16)
    grad_normed_one = dot_right_t(grad_qkv_rows, full_qkv)
    grad_input = (
        grad_middle + norm_back(grad_normed_one, scaled_one, inv_one, g_one)
    ).astype(bf16)

    norm_sums = jnp.stack(
        [
            jnp.sum(grad_normed_one * scaled_one, 0),
            jnp.sum(grad_normed_one, 0),
            jnp.sum(grad_normed_two * scaled_two, 0),
            jnp.sum(grad_normed_two, 0),
        ]
    )
    norm_cols = jnp.pad(norm_sums.T.astype(bf16), ((0, 0), (REM_NORM, 28)))
    sum0, sum1, sum2, sum3 = (
        total.astype(f32)
        for total in scatter_grads(
            pack_grads(
                sum_qkv.reshape(4, part, -1),
                sum_proj.reshape(4, part, -1),
                sum_up.reshape(4, part, -1),
                sum_down.reshape(16, part, -1),
                norm_cols.reshape(4, part, -1),
            )
        )
    )
    rest = sum1[:, TILE : 2 * TILE]
    out_qkv = jnp.concatenate([sum0, rest[:, REM_QKV : REM_QKV + 24]], 1)
    out_proj = jnp.concatenate([sum1[:, :TILE], rest[:, REM_OUT : REM_OUT + 8]], 1)
    out_up = jnp.concatenate([sum1[:, 2 * TILE :], sum2, rest[:, REM_UP : REM_UP + 32]], 1)
    out_down = jnp.concatenate(
        [
            jnp.concatenate(
                [
                    sum3[:, i * TILE : (i + 1) * TILE],
                    rest[:, REM_DOWN + 8 * i : REM_DOWN + 8 * i + 8],
                ],
                1,
            )
            for i in range(4)
        ],
        0,
    )
    norm_mine = rest[:, REM_NORM : REM_NORM + 4].T
    return (
        block_out.reshape(tokens.shape),
        grad_input.reshape(tokens.shape),
        out_qkv,
        out_proj,
        out_up,
        out_down,
        norm_mine[0],
        norm_mine[1],
        norm_mine[2],
        norm_mine[3],
    )


def solution(mesh):
    grid = (mesh.shape["dp"], mesh.shape["seq"])
    return jax.shard_map(
        shards_fast if grid == (4, 8) else shards_plain,
        mesh=mesh,
        in_specs=(
            P(None, ("dp", "seq"), None),
            P(None, ("dp", "seq"), None),
            P("dp", "seq"),
            P("dp", "seq"),
            P("dp", "seq"),
            P("dp", "seq"),
            P("dp"),
            P("dp"),
            P("dp"),
            P("dp"),
            P(None, "dp", None),
            P(None, "dp", None),
        ),
        out_specs=(
            P(None, ("dp", "seq"), None),
            P(None, ("dp", "seq"), None),
            P("dp", "seq"),
            P("dp", "seq"),
            P("dp", "seq"),
            P("dp", "seq"),
            P("dp"),
            P("dp"),
            P("dp"),
            P("dp"),
        ),
        check_vma=False,
    )
```

```python
import functools

import jax
import jax.numpy as jnp
from jax import lax
from jax.experimental import pallas as pl
from jax.experimental.pallas import tpu as pltpu
from jax.sharding import PartitionSpec as P

HEADS = 17


EPS = 1e-05
GELU_C = 0.7978845608028654


def gelu_tanh(values):
    return 0.5 * values * (1.0 + jnp.tanh(GELU_C * (values + 0.044715 * values * values * values)))


def normalize(residual):
    row_mean = jnp.mean(residual, -1, keepdims=True)
    centered = residual - row_mean
    inv_std = lax.rsqrt(jnp.mean(centered * centered, -1, keepdims=True) + EPS)
    return (centered * inv_std, inv_std)


def norm_back(grad_normed, scaled, inv_std, gain_row):
    grad_scaled = grad_normed * gain_row
    return inv_std * (
        grad_scaled
        - jnp.mean(grad_scaled, -1, keepdims=True)
        - scaled * jnp.mean(grad_scaled * scaled, -1, keepdims=True)
    )


def running_total(counts):
    index = jnp.arange(counts.shape[0], dtype=jnp.int32)
    return jnp.sum(jnp.where(index[None, :] <= index[:, None], counts[None, :], 0), 1)


def segment_of(places, doc_ends):
    return jnp.sum((places[:, None] >= doc_ends[None, :]).astype(jnp.int32), 1)


def pair_swap(block):
    route = [(i, i ^ 1) for i in range(lax.axis_size("seq"))]
    return lax.ppermute(block, "seq", route)


def same_core():
    n_seq = lax.axis_size("seq")
    return [list(range(core, n_seq, 2)) for core in range(2)]


def gather_stack(shard):
    chips = lax.all_gather(shard, "seq", axis_index_groups=same_core())
    held = lax.all_gather(chips, "dp")
    other = pair_swap(held)
    first = lax.axis_index("seq") % 2 == 0
    both = jnp.stack([jnp.where(first, held, other), jnp.where(first, other, held)], 2)
    dp, chip_count = held.shape[:2]
    return both.transpose(1, 2, 0, 3, 4).reshape(2 * chip_count, dp, *shard.shape)


def pair_sum(parts):
    pairs = parts.reshape(parts.shape[0] // 2, 2, *parts.shape[1:])
    first = lax.axis_index("seq") % 2 == 0
    mine = jnp.where(first, pairs[:, 0], pairs[:, 1])
    other = jnp.where(first, pairs[:, 1], pairs[:, 0])
    got = pair_swap(other)
    return (mine.astype(jnp.float32) + got.astype(jnp.float32)).astype(jnp.bfloat16)


def scatter_stack(parts, after):
    held = pair_sum(parts).transpose(1, 0, 2, 3).reshape(-1, parts.shape[3])
    if after is not None:
        held, after = lax.optimization_barrier((held, after))
    held = lax.psum_scatter(held, "dp", scatter_dimension=0, tiled=True)
    held = lax.psum_scatter(
        held, "seq", scatter_dimension=0, axis_index_groups=same_core(), tiled=True
    )
    return held, after


def dot(left, right):
    return jnp.dot(left, right, preferred_element_type=jnp.float32)


def dot_right_t(left, right):
    return lax.dot_general(left, right, (((1,), (1,)), ((), ())), preferred_element_type=jnp.float32)


def dot_left_t(left, right):
    return lax.dot_general(left, right, (((0,), (0,)), ((), ())), preferred_element_type=jnp.float32)


def cols_of(rows, count):
    return rows.reshape(rows.shape[0], count, -1).transpose(1, 0, 2)


def apply_cols(rows, cols):
    lifted = jnp.broadcast_to(rows[None], (cols.shape[0],) + rows.shape)
    made = lax.dot_general(
        lifted, cols, (((2,), (1,)), ((0,), (0,))), preferred_element_type=jnp.float32
    )
    return made.transpose(1, 0, 2).reshape(rows.shape[0], -1)


def apply_cols_t(rows, cols):
    lifted = cols_of(rows, cols.shape[0])
    return lax.dot_general(
        lifted, cols, (((0, 2), (0, 2)), ((), ())), preferred_element_type=jnp.float32
    )


def grad_cols(left, right, count):
    lifted = jnp.broadcast_to(left[None], (count,) + left.shape)
    return lax.dot_general(
        lifted, cols_of(right, count), (((1,), (1,)), ((0,), (0,))),
        preferred_element_type=jnp.float32,
    )


def heads_of(rows, micro_count, head_dim):
    return rows.reshape(micro_count, -1, HEADS, head_dim).transpose(0, 2, 1, 3)


def rows_of(heads):
    micro_count, _, slots, head_dim = heads.shape
    return heads.transpose(0, 2, 1, 3).reshape(micro_count * slots, HEADS * head_dim)


def batched(left, right, left_dim, right_dim):
    return lax.dot_general(
        left,
        right,
        (((left_dim,), (right_dim,)), ((0, 1), (0, 1))),
        preferred_element_type=jnp.float32,
    )


def shards_plain(
    tokens,
    cotangent,
    w_qkv,
    w_out,
    w_up,
    w_down,
    gain_one,
    bias_one,
    gain_two,
    bias_two,
    lengths,
    slot_order,
):
    micro_count, tok_dev, width = tokens.shape
    rows = micro_count * tok_dev
    head_dim = width // HEADS
    score_scale = head_dim ** (-0.5)
    n_seq = lax.axis_size("seq")
    my_slot = lax.axis_index("seq")
    bf16 = jnp.bfloat16

    norms = lax.all_gather(
        jnp.stack([gain_one, bias_one, gain_two, bias_two]), "dp", axis=1, tiled=True
    ).astype(jnp.float32)
    g_one, b_one, g_two, b_two = norms[0], norms[1], norms[2], norms[3]
    n_dp = lax.axis_size("dp")
    part, qkv_cols = w_qkv.shape
    out_cols = w_out.shape[1]
    up_cols = w_up.shape[1]
    fold = w_down.shape[0] // up_cols
    attn_stack = gather_stack(jnp.concatenate([w_qkv, w_out], 1))
    down_t = w_down.T
    ffn_stack = gather_stack(
        jnp.concatenate([w_up, *jnp.split(down_t, fold, 1)], 0)
    )
    cols_qkv = attn_stack[..., :qkv_cols].reshape(n_seq, width, qkv_cols)
    full_out = (
        attn_stack[..., qkv_cols:].reshape(n_seq, width, out_cols).transpose(1, 0, 2)
    ).reshape(width, width)
    cols_up = ffn_stack[:, :, :part].reshape(n_seq, width, up_cols)
    full_down_t = (
        ffn_stack[:, :, part:]
        .reshape(n_seq, n_dp, fold, out_cols, up_cols)
        .transpose(0, 3, 1, 2, 4)
        .reshape(width, fold * n_dp * up_cols)
    )

    doc_ends = jax.vmap(running_total)(lengths[:, 0])
    k_place = (
        slot_order[:, 0, :, None] * tok_dev + jnp.arange(tok_dev, dtype=jnp.int32)
    ).reshape(micro_count, n_seq * tok_dev)
    k_segment = jax.vmap(segment_of)(k_place, doc_ends)
    base_slot = lax.dynamic_slice_in_dim(slot_order[:, 0], my_slot, 1, 1)
    q_place = base_slot * tok_dev + jnp.arange(tok_dev, dtype=jnp.int32)
    q_segment = jax.vmap(segment_of)(q_place, doc_ends)
    allowed = (q_segment[:, :, None] == k_segment[:, None, :]) & (
        k_place[:, None, :] <= q_place[:, :, None]
    )

    residual = tokens.astype(jnp.float32).reshape(rows, width)
    scaled_one, inv_one = normalize(residual)
    normed_one = (scaled_one * g_one + b_one).astype(bf16)
    qkv_all = apply_cols(normed_one, cols_qkv).astype(bf16)
    queries = heads_of(qkv_all[:, :width], micro_count, head_dim)
    local_kv = qkv_all[:, width:].reshape(micro_count, tok_dev, 2 * width)
    group_kv = lax.all_gather(local_kv, "seq", axis=1, tiled=True)
    keys = heads_of(group_kv[..., :width], micro_count, head_dim)
    values = heads_of(group_kv[..., width:], micro_count, head_dim)

    scores = batched(queries, keys, 3, 3) * score_scale
    scores = jnp.where(allowed[:, None], scores, -jnp.inf)
    weights = jnp.exp(scores - jnp.max(scores, -1, keepdims=True))
    probs = weights * (1.0 / jnp.sum(weights, -1, keepdims=True))
    probs_low = probs.astype(bf16)
    attended = batched(probs_low, values, 3, 2)
    attn_flat = rows_of(attended.astype(bf16))
    middle = residual + dot(attn_flat, full_out)
    scaled_two, inv_two = normalize(middle)
    normed_two = (scaled_two * g_two + b_two).astype(bf16)
    hidden = apply_cols(normed_two, cols_up)
    activated_full, gelu_back = jax.vjp(gelu_tanh, hidden)
    activated = activated_full.astype(bf16)

    grad_rows = cotangent.reshape(rows, width)
    block_out = (middle + dot_right_t(activated, full_down_t)).astype(bf16)
    grad_hidden = gelu_back(dot(grad_rows, full_down_t))[0].astype(bf16)
    sum_down_t = dot_left_t(grad_rows, activated).astype(bf16)
    sum_down_t = (
        sum_down_t.reshape(n_seq, out_cols, n_dp, fold, up_cols)
        .transpose(0, 2, 3, 1, 4)
        .reshape(n_seq, n_dp, fold * out_cols, up_cols)
    )
    sum_up = grad_cols(normed_two, grad_hidden, n_seq).astype(bf16)
    sum_ffn, _ = scatter_stack(
        jnp.concatenate([sum_up.reshape(n_seq, n_dp, part, up_cols), sum_down_t], 2), None
    )
    grad_normed_two = apply_cols_t(grad_hidden, cols_up)
    grad_middle = grad_rows.astype(jnp.float32) + norm_back(
        grad_normed_two, scaled_two, inv_two, g_two
    )
    grad_branch = grad_middle.astype(bf16)
    sum_proj = grad_cols(attn_flat, grad_branch, n_seq).astype(bf16)
    grad_heads = heads_of(
        dot_right_t(grad_branch, full_out).astype(bf16), micro_count, head_dim
    )

    grad_probs = batched(grad_heads, values, 3, 3)
    row_dot = jnp.sum(probs * grad_probs, -1, keepdims=True)
    grad_scores = (probs * (grad_probs - row_dot)).astype(bf16)
    grad_query = rows_of(batched(grad_scores, keys, 3, 2) * score_scale)
    grad_keys = rows_of(batched(grad_scores, queries, 2, 2) * score_scale)
    grad_values = rows_of(batched(probs_low, grad_heads, 2, 2))
    grad_kv = jnp.concatenate([grad_keys.astype(bf16), grad_values.astype(bf16)], 1)
    grad_kv = grad_kv.reshape(micro_count, n_seq, tok_dev, 2 * width).transpose(1, 0, 2, 3)
    grad_kv = lax.psum_scatter(
        pair_sum(grad_kv), "seq", scatter_dimension=0, axis_index_groups=same_core()
    ).reshape(rows, 2 * width)
    grad_qkv_rows = jnp.concatenate([grad_query.astype(bf16), grad_kv], 1)
    sum_qkv = grad_cols(normed_one, grad_qkv_rows, n_seq).astype(bf16)
    sum_attn, sum_ffn = scatter_stack(
        jnp.concatenate([sum_qkv, sum_proj], 2).reshape(n_seq, n_dp, part, qkv_cols + out_cols),
        sum_ffn,
    )
    sum_attn = sum_attn.astype(jnp.float32)
    sum_ffn = sum_ffn.astype(jnp.float32)
    out_up = sum_ffn[:part]
    out_down = jnp.concatenate(jnp.split(sum_ffn[part:], fold, 0), 1).T
    out_qkv = sum_attn[:, :qkv_cols]
    out_proj = sum_attn[:, qkv_cols:]
    grad_normed_one = apply_cols_t(grad_qkv_rows, cols_qkv)
    grad_input = (
        grad_middle + norm_back(grad_normed_one, scaled_one, inv_one, g_one)
    ).astype(bf16)

    norm_sums = jnp.stack(
        [
            jnp.sum(grad_normed_one * scaled_one, 0),
            jnp.sum(grad_normed_one, 0),
            jnp.sum(grad_normed_two * scaled_two, 0),
            jnp.sum(grad_normed_two, 0),
        ]
    )
    norm_totals = lax.psum(norm_sums, ("dp", "seq"))
    norm_mine = lax.dynamic_slice_in_dim(norm_totals, lax.axis_index("dp") * part, part, 1)
    return (
        block_out.reshape(tokens.shape),
        grad_input.reshape(tokens.shape),
        out_qkv,
        out_proj,
        out_up,
        out_down,
        norm_mine[0],
        norm_mine[1],
        norm_mine[2],
        norm_mine[3],
    )


MESH = pl.DeviceIdType.MESH
GATHER_ORDERS = ((2, 3, 0, 1), (2, 3, 1, 0), (0, 2, 3, 1), (3, 2, 1, 0))
SCATTER_ORDERS = GATHER_ORDERS
ROW_CUTS = ((0, 96), (96, 80), (176, 64), (240, 32))
GATHER_CHUNKS = tuple((q, r) for r in range(4) for q in range(4))
SCATTER_CHUNKS = tuple((q, r) for r in reversed(range(4)) for q in range(4))
GATHER_LAGS = (0, 2, 4, 6, 9)
SCATTER_LAGS = (0, 3, 5, 7, 9)
AHEAD = 4
TILE = 128
LANES = (3 * TILE, 3 * TILE, 3 * TILE, 4 * TILE)
UNITS = 5
IDLE = 7
REM_UP, REM_QKV, REM_OUT, REM_DOWN, REM_NORM = 0, 32, 56, 64, 96


def place_of(order, dp, seq):
    z = seq // 2
    bits = (dp % 2, dp // 2, (z % 2 + z // 2) % 2, z // 2)
    return sum(bits[dim] * 2**k for k, dim in enumerate(order))


def partner(dim):
    dp, seq = lax.axis_index("dp"), lax.axis_index("seq")
    z, core = seq // 2, seq % 2
    if dim == 0:
        return (dp + 1 - 2 * (dp % 2), seq)
    if dim == 1:
        return (dp + 2 - 4 * (dp // 2), seq)
    if dim == 2:
        return (dp, (z + 1 - 2 * (z % 2)) * 2 + core)
    return (dp, (3 - z) * 2 + core)


def sibling():
    dp, seq = lax.axis_index("dp"), lax.axis_index("seq")
    return (dp, seq + 1 - 2 * (seq % 2))


def greet(devices):
    barrier = pltpu.get_barrier_semaphore()
    for device in devices:
        pl.semaphore_signal(barrier, inc=1, device_id=device, device_id_type=MESH)
    pl.semaphore_wait(barrier, len(devices))


def send(src, dst, send_sem, recv_sem, device):
    copy = pltpu.make_async_remote_copy(
        src_ref=src, dst_ref=dst, send_sem=send_sem, recv_sem=recv_sem,
        device_id=device, device_id_type=MESH,
    )
    copy.start()
    return copy


def gather_kernel(*refs):
    shards_in, full = refs[:4], refs[4:8]
    own_sem, link_send, link_recv, sib_send, sib_recv = refs[8:]
    dp, seq = lax.axis_index("dp"), lax.axis_index("seq")
    core = seq % 2
    greet([partner(dim) for dim in range(4)] + [sibling()])
    at = [place_of(GATHER_ORDERS[q], dp, seq) for q in range(4)]
    owns, links, sides = {}, {}, []

    def step(chunk, stage):
        q, r = GATHER_CHUNKS[chunk]
        span = pl.ds(*ROW_CUTS[r])
        size = 2**stage
        if stage == 0:
            fresh, target = shards_in[q].at[span], full[q].at[core, at[q], span]
            links[chunk] = send(
                fresh, target, link_send.at[chunk, 0], link_recv.at[chunk, 0],
                partner(GATHER_ORDERS[q][0]),
            )
            owns[chunk] = pltpu.make_async_copy(fresh, target, own_sem.at[chunk])
            owns[chunk].start()
            sides.append(
                send(fresh, target, sib_send.at[chunk, 0], sib_recv.at[chunk, 0], sibling())
            )
            return
        links[chunk].wait()
        if stage == 1:
            owns[chunk].wait()
        if stage < 4:
            held = full[q].at[core, pl.ds(at[q] // size * size, size), span]
            links[chunk] = send(
                held, held, link_send.at[chunk, stage], link_recv.at[chunk, stage],
                partner(GATHER_ORDERS[q][stage]),
            )
        half = size // 2
        mine = at[q] // half
        got = full[q].at[core, pl.ds((mine + 1 - 2 * (mine % 2)) * half, half), span]
        sides.append(
            send(got, got, sib_send.at[chunk, stage], sib_recv.at[chunk, stage], sibling())
        )

    for turn in range(len(GATHER_CHUNKS) + GATHER_LAGS[4]):
        for stage in (4, 3, 2, 1, 0):
            lag = GATHER_LAGS[stage]
            if 0 <= turn - lag < len(GATHER_CHUNKS):
                step(turn - lag, stage)
    for side in sides:
        side.wait()


def gather_weights(chunks):
    rows = chunks[0].shape[0]
    anywhere = pl.BlockSpec(memory_space=pl.ANY)
    dma = pltpu.SemaphoreType.DMA
    return pl.pallas_call(
        gather_kernel,
        out_shape=[jax.ShapeDtypeStruct((2, 16, rows, lanes), jnp.bfloat16) for lanes in LANES],
        in_specs=[anywhere] * 4,
        out_specs=[anywhere] * 4,
        scratch_shapes=[dma((16,)), dma((16, 4)), dma((16, 4)), dma((16, 5)), dma((16, 5))],
        compiler_params=pltpu.CompilerParams(collective_id=0, has_side_effects=True),
        name="gather_weights",
    )(*chunks)


def scatter_kernel(*refs):
    parts, outs = refs[:4], refs[4:8]
    own, acc, got3, got2, got1, got0 = (refs[8 + 4 * i : 12 + 4 * i] for i in range(6))
    got = (got0, got1, got2, got3)
    own_sem, link_send, link_recv, sib_send, sib_recv = refs[32:]
    dp, seq = lax.axis_index("dp"), lax.axis_index("seq")
    core = seq % 2
    greet([partner(dim) for dim in range(4)] + [sibling()])
    at = [place_of(SCATTER_ORDERS[q], dp, seq) for q in range(4)]
    side, load, links = {}, {}, {}

    def begin(chunk):
        q, r = SCATTER_CHUNKS[chunk]
        rows = pl.ds(*ROW_CUTS[r])
        side[chunk] = send(
            parts[q].at[1 - core, :, rows], acc[q].at[:, rows],
            sib_send.at[chunk], sib_recv.at[chunk], sibling(),
        )
        load[chunk] = pltpu.make_async_copy(
            parts[q].at[core, :, rows], own[q].at[:, rows], own_sem.at[chunk]
        )
        load[chunk].start()

    for chunk in range(AHEAD):
        begin(chunk)

    def add(chunk, base, other, other_base, count):
        q, r = SCATTER_CHUNKS[chunk]
        rows = pl.ds(*ROW_CUTS[r])

        def one(b, carry):
            acc[q][base + b, rows] = acc[q][base + b, rows] + other[other_base + b, rows]
            return carry

        lax.fori_loop(0, count, one, 0)

    def step(chunk, stage):
        q, r = SCATTER_CHUNKS[chunk]
        rows = pl.ds(*ROW_CUTS[r])
        half = 2**stage
        base = at[q] // (2 * half) * (2 * half)
        high = at[q] // half % 2
        away, keep = (1 - high) * half, high * half
        if stage == 3:
            side[chunk].wait_recv()
            load[chunk].wait()
            other = own[q]
        else:
            links[chunk, stage + 1].wait_recv()
            other = got[stage + 1][q]
        add(chunk, base + away, other, away, half)
        links[chunk, stage] = send(
            acc[q].at[pl.ds(base + away, half), rows], got[stage][q].at[:, rows],
            link_send.at[chunk, stage], link_recv.at[chunk, stage], partner(SCATTER_ORDERS[q][stage]),
        )
        add(chunk, base + keep, other, keep, half)

    for turn in range(len(SCATTER_CHUNKS) + SCATTER_LAGS[4]):
        if turn + AHEAD < len(SCATTER_CHUNKS):
            begin(turn + AHEAD)
        for stage in (-1, 0, 1, 2, 3):
            lag = SCATTER_LAGS[3 - stage]
            chunk = turn - lag
            if 0 <= chunk < len(SCATTER_CHUNKS):
                if stage >= 0:
                    step(chunk, stage)
                    continue
                q, r = SCATTER_CHUNKS[chunk]
                rows = pl.ds(*ROW_CUTS[r])
                links[chunk, 0].wait_recv()
                outs[q][rows] = acc[q][at[q], rows] + got0[q][0, rows]
    for copy in list(side.values()) + list(links.values()):
        copy.wait_send()


def scatter_grads(parts):
    rows = parts[0].shape[2]
    dma = pltpu.SemaphoreType.DMA
    bf16 = jnp.bfloat16
    buffers = [
        pltpu.VMEM((count, rows, lanes), bf16) for count in (16, 16, 8, 4, 2, 1) for lanes in LANES
    ]
    return pl.pallas_call(
        scatter_kernel,
        out_shape=[jax.ShapeDtypeStruct((rows, lanes), bf16) for lanes in LANES],
        in_specs=[pl.BlockSpec(memory_space=pl.ANY)] * 4,
        out_specs=[pl.BlockSpec(memory_space=pltpu.VMEM)] * 4,
        scratch_shapes=buffers + [dma((16,)), dma((16, 4)), dma((16, 4)), dma((16,)), dma((16,))],
        compiler_params=pltpu.CompilerParams(
            collective_id=1, has_side_effects=True, vmem_limit_bytes=56 * 2**20
        ),
        name="scatter_grads",
    )(*parts)


def exchange_kernel(to_owners, blocks, out, own_sem, send_sem, recv_sem):
    dp, seq = lax.axis_index("dp"), lax.axis_index("seq")
    others = [(dp, (seq + k) % 8) for k in range(1, 8)]
    greet(others)
    own = pltpu.make_async_copy(blocks.at[seq], out.at[seq], own_sem)
    copies = [
        pltpu.make_async_remote_copy(
            src_ref=blocks.at[device[1]], dst_ref=out.at[seq], send_sem=send_sem.at[k],
            recv_sem=recv_sem.at[k], device_id=device, device_id_type=MESH,
        )
        for k, device in enumerate(others)
    ]
    for k, copy in enumerate(copies):
        pl.when((others[k][1] if to_owners else seq) != IDLE)(copy.start)
    own.start()
    own.wait()
    for k, copy in enumerate(copies):
        pl.when((others[k][1] if to_owners else seq) != IDLE)(copy.wait_send)
        pl.when((seq if to_owners else (seq + 7 - k) % 8) != IDLE)(copy.wait_recv)


def exchange(blocks, which):
    dma = pltpu.SemaphoreType.DMA
    return pl.pallas_call(
        functools.partial(exchange_kernel, which % 2 == 0),
        out_shape=jax.ShapeDtypeStruct(blocks.shape, blocks.dtype),
        in_specs=[pl.BlockSpec(memory_space=pl.ANY)],
        out_specs=pl.BlockSpec(memory_space=pl.ANY),
        scratch_shapes=[dma, dma((7,)), dma((7,))],
        compiler_params=pltpu.CompilerParams(collective_id=2 + which, has_side_effects=True),
        name=f"exchange_{which}",
    )(blocks)


def spots():
    for dp in range(4):
        for seq in range(8):
            yield dp, seq, seq % 2, [place_of(SCATTER_ORDERS[q], dp, seq) for q in range(4)]


def unpack_kernel(c0, c1, c2, c3, qkv, out, up, down, norms):
    for dp in range(4):
        pieces = [[] for _ in range(7)]
        for s in range(8):
            at = [place_of(GATHER_ORDERS[q], dp, s) for q in range(4)]
            core = s % 2
            rem = c1[core, at[1], :, TILE : 2 * TILE]
            if s == 0:
                norms[dp] = rem
            pieces[0] += [c0[core, at[0]], rem[:, REM_QKV : REM_QKV + 24]]
            pieces[1] += [c1[core, at[1], :, :TILE], rem[:, REM_OUT : REM_OUT + 8]]
            pieces[2] += [
                c1[core, at[1], :, 2 * TILE :], c2[core, at[2]], rem[:, REM_UP : REM_UP + 32]
            ]
            for i in range(4):
                pieces[3 + i] += [
                    c3[core, at[3], :, i * TILE : (i + 1) * TILE],
                    rem[:, REM_DOWN + 8 * i : REM_DOWN + 8 * i + 8],
                ]
        qkv[dp] = jnp.concatenate(pieces[0], 1)
        out[dp] = jnp.concatenate(pieces[1], 1)
        up[dp] = jnp.concatenate(pieces[2], 1)
        for i in range(4):
            down[dp * 4 + i] = jnp.concatenate(pieces[3 + i], 1)


def unpack_weights(chunks):
    bf16 = jnp.bfloat16
    rows, step = chunks[0].shape[2], 16

    def spec(count, lanes):
        return pl.BlockSpec((count, step, lanes), lambda i: (0, i, 0))

    sizes = ((4, 3264), (4, 1088), (4, 4352), (16, 1088), (4, 128))
    return pl.pallas_call(
        unpack_kernel,
        grid=(rows // step,),
        out_shape=[jax.ShapeDtypeStruct((count, rows, lanes), bf16) for count, lanes in sizes],
        in_specs=[pl.BlockSpec((2, 16, step, lanes), lambda i: (0, 0, i, 0)) for lanes in LANES],
        out_specs=[spec(*size) for size in sizes],
        compiler_params=pltpu.CompilerParams(vmem_limit_bytes=40 * 2**20),
        name="unpack_weights",
    )(*chunks)


def pack_kernel(qkv, out, up, down, norms, c0, c1, c2, c3):
    for dp, s, core, at in spots():
        c0[core, at[0]] = qkv[dp, :, s * 408 : s * 408 + 384]
        c1[core, at[1], :, :TILE] = out[dp, :, s * 136 : s * 136 + 128]
        c1[core, at[1], :, 2 * TILE :] = up[dp, :, s * 544 : s * 544 + 128]
        c2[core, at[2]] = up[dp, :, s * 544 + 128 : s * 544 + 512]
        base = at[1]
        c1[core, base, :, TILE : 2 * TILE] = norms[dp]
        c1[core, base, :, TILE + REM_UP : TILE + REM_UP + 32] = up[dp, :, s * 544 + 512 : s * 544 + 544]
        c1[core, base, :, TILE + REM_QKV : TILE + REM_QKV + 24] = qkv[dp, :, s * 408 + 384 : s * 408 + 408]
        c1[core, base, :, TILE + REM_OUT : TILE + REM_OUT + 8] = out[dp, :, s * 136 + 128 : s * 136 + 136]
        for i in range(4):
            c3[core, at[3], :, i * TILE : (i + 1) * TILE] = down[dp * 4 + i, :, s * 136 : s * 136 + 128]
            spot = TILE + REM_DOWN + 8 * i
            c1[core, base, :, spot : spot + 8] = down[dp * 4 + i, :, s * 136 + 128 : s * 136 + 136]


def pack_grads(qkv, out, up, down, norms):
    rows, step = qkv.shape[1], 16

    def spec(count, lanes):
        return pl.BlockSpec((count, step, lanes), lambda i: (0, i, 0))

    return pl.pallas_call(
        pack_kernel,
        grid=(rows // step,),
        out_shape=[jax.ShapeDtypeStruct((2, 16, rows, lanes), jnp.bfloat16) for lanes in LANES],
        in_specs=[spec(4, 3264), spec(4, 1088), spec(4, 4352), spec(16, 1088), spec(4, 128)],
        out_specs=[pl.BlockSpec((2, 16, step, lanes), lambda i: (0, 0, i, 0)) for lanes in LANES],
        compiler_params=pltpu.CompilerParams(vmem_limit_bytes=40 * 2**20),
        name="pack_grads",
    )(qkv, out, up, down, norms)


QUERY_BLOCK = 256


def flip(block):
    return block.astype(jnp.float32).T.astype(jnp.bfloat16)


def outer_kernel(left, right, out):
    out[...] = dot(flip(left[...]), right[...]).astype(out.dtype)


def outer(left, right):
    rows, width = left.shape
    step = 2 * TILE
    return pl.pallas_call(
        outer_kernel,
        grid=(width // step,),
        out_shape=jax.ShapeDtypeStruct((width, right.shape[1]), jnp.bfloat16),
        in_specs=[
            pl.BlockSpec((rows, step), lambda i: (0, i)),
            pl.BlockSpec(right.shape, lambda i: (0, 0)),
        ],
        out_specs=pl.BlockSpec((step, right.shape[1]), lambda i: (i, 0)),
        compiler_params=pltpu.CompilerParams(vmem_limit_bytes=24 * 2**20),
        cost_estimate=pl.CostEstimate(
            flops=2 * rows * width * right.shape[1],
            bytes_accessed=2 * width * (right.shape[1] + rows),
            transcendentals=0,
        ),
        name="outer",
    )(left, right)


def masked_scores(k_rows, q_cols, seg_k, seg_q, start, scale):
    count, width = k_rows.shape[0], q_cols.shape[1]
    scores = dot(k_rows, q_cols) * scale
    key_at = lax.broadcasted_iota(jnp.int32, (count, width), 0)
    query_at = lax.broadcasted_iota(jnp.int32, (count, width), 1) + start
    return jnp.where((seg_k == seg_q) & (key_at <= query_at), scores, -1e30)


def attend_kernel(scale, order, x, seg_k, seg_q, out, lse, q_t, k_t, v_t, o_t):
    unit = pl.program_id(0)
    slots = x.shape[0]
    tok = x.shape[3]
    depth = q_t.shape[0]
    for b in range(slots):
        at = order[unit, b]
        for n, held in enumerate((q_t, k_t, v_t)):
            held[:, b * tok : (b + 1) * tok] = x[at, 0, n * depth : (n + 1) * depth]
    keys = flip(k_t[...])
    for start in range(0, slots * tok, QUERY_BLOCK):
        count = start + QUERY_BLOCK
        cols = slice(start, count)
        scores = masked_scores(
            keys[:count], q_t[:, cols], seg_k[0, :count], seg_q[0, :, cols], start, scale
        )
        top = jnp.max(scores, 0, keepdims=True)
        weights = jnp.exp(scores - top)
        total = jnp.sum(weights, 0, keepdims=True)
        probs = (weights * (1.0 / total)).astype(jnp.bfloat16)
        o_t[:, cols] = dot(v_t[:, :count], probs).astype(jnp.bfloat16)
        lse[0, :, cols] = top + jnp.log(total)
    for b in range(slots):
        out[order[unit, b], 0] = o_t[:, b * tok : (b + 1) * tok]


def attend(x, order, seg_k, seg_q, scale):
    slots, units, depth3, tok = x.shape
    depth, length = depth3 // 3, slots * tok
    bf16 = jnp.bfloat16
    held = [pltpu.VMEM((depth, length), bf16)] * 4
    return pl.pallas_call(
        functools.partial(attend_kernel, scale),
        grid_spec=pltpu.PrefetchScalarGridSpec(
            num_scalar_prefetch=1,
            grid=(units,),
            in_specs=[
                pl.BlockSpec((slots, 1, depth3, tok), lambda u, o: (0, u, 0, 0)),
                pl.BlockSpec((1, length, 1), lambda u, o: (u, 0, 0)),
                pl.BlockSpec((1, 1, length), lambda u, o: (u, 0, 0)),
            ],
            out_specs=[
                pl.BlockSpec((slots, 1, depth, tok), lambda u, o: (0, u, 0, 0)),
                pl.BlockSpec((1, 1, length), lambda u, o: (u, 0, 0)),
            ],
            scratch_shapes=held,
        ),
        out_shape=[
            jax.ShapeDtypeStruct((slots, units, depth, tok), bf16),
            jax.ShapeDtypeStruct((units, 1, length), jnp.float32),
        ],
        compiler_params=pltpu.CompilerParams(vmem_limit_bytes=40 * 2**20),
        name="attend",
    )(order, x, seg_k, seg_q)


def attend_back_kernel(
    scale, order, x, g, seg_k, seg_q, lse, out, q_t, k_t, v_t, g_t, dq_t, dk_t, dv_t
):
    unit = pl.program_id(0)
    slots = x.shape[0]
    tok = x.shape[3]
    depth = q_t.shape[0]
    for b in range(slots):
        at = order[unit, b]
        for n, held in enumerate((q_t, k_t, v_t)):
            held[:, b * tok : (b + 1) * tok] = x[at, 0, n * depth : (n + 1) * depth]
        g_t[:, b * tok : (b + 1) * tok] = g[at, 0]
    keys = flip(k_t[...])
    values = flip(v_t[...])
    length = slots * tok
    for start in reversed(range(0, length, QUERY_BLOCK)):
        count = start + QUERY_BLOCK
        cols = slice(start, count)
        queries, grads = q_t[:, cols], g_t[:, cols]
        scores = masked_scores(
            keys[:count], queries, seg_k[0, :count], seg_q[0, :, cols], start, scale
        )
        probs = jnp.exp(scores - lse[0, :, cols])
        grad_probs = dot(values[:count], grads)
        row_dot = jnp.sum(probs * grad_probs, 0, keepdims=True)
        grad_scores = (probs * (grad_probs - row_dot)).astype(jnp.bfloat16)
        probs_low = probs.astype(jnp.bfloat16)
        dq_t[:, cols] = dot(k_t[:, :count], grad_scores) * scale
        dk = dot_right_t(queries, grad_scores)
        dv = dot_right_t(grads, probs_low)
        if count == length:
            dk_t[...] = dk
            dv_t[...] = dv
        else:
            dk_t[:, :count] += dk
            dv_t[:, :count] += dv
    for b in range(slots):
        at = order[unit, b]
        cols = slice(b * tok, (b + 1) * tok)
        out[at, 0, :depth] = dq_t[:, cols].astype(jnp.bfloat16)
        out[at, 0, depth : 2 * depth] = (dk_t[:, cols] * scale).astype(jnp.bfloat16)
        out[at, 0, 2 * depth :] = dv_t[:, cols].astype(jnp.bfloat16)


def attend_back(x, g, order, seg_k, seg_q, lse, scale):
    slots, units, depth3, tok = x.shape
    depth, length = depth3 // 3, slots * tok
    bf16 = jnp.bfloat16
    held = [pltpu.VMEM((depth, length), bf16)] * 4 + [pltpu.VMEM((depth, length), jnp.float32)] * 3
    return pl.pallas_call(
        functools.partial(attend_back_kernel, scale),
        grid_spec=pltpu.PrefetchScalarGridSpec(
            num_scalar_prefetch=1,
            grid=(units,),
            in_specs=[
                pl.BlockSpec((slots, 1, depth3, tok), lambda u, o: (0, u, 0, 0)),
                pl.BlockSpec((slots, 1, depth, tok), lambda u, o: (0, u, 0, 0)),
                pl.BlockSpec((1, length, 1), lambda u, o: (u, 0, 0)),
                pl.BlockSpec((1, 1, length), lambda u, o: (u, 0, 0)),
                pl.BlockSpec((1, 1, length), lambda u, o: (u, 0, 0)),
            ],
            out_specs=pl.BlockSpec((slots, 1, depth3, tok), lambda u, o: (0, u, 0, 0)),
            scratch_shapes=held,
        ),
        out_shape=jax.ShapeDtypeStruct(x.shape, bf16),
        compiler_params=pltpu.CompilerParams(vmem_limit_bytes=48 * 2**20),
        name="attend_back",
    )(order, x, g, seg_k, seg_q, lse)


def to_units(flat, micro_count, kinds):
    tok = flat.shape[1] // micro_count
    units = flat.reshape(kinds, HEADS, -1, micro_count, tok).transpose(3, 1, 0, 2, 4)
    units = units.reshape(micro_count * HEADS, -1, tok)
    units = jnp.pad(units, ((0, 8 * UNITS - units.shape[0]), (0, 0), (0, 0)))
    return units.reshape(8, UNITS, -1, tok)


def from_units(units, micro_count, kinds):
    tok = units.shape[3]
    held = units.reshape(8 * UNITS, -1, tok)[: micro_count * HEADS]
    held = held.reshape(micro_count, HEADS, kinds, -1, tok).transpose(0, 4, 2, 1, 3)
    return held.reshape(micro_count * tok, -1)


def shards_fast(
    tokens,
    cotangent,
    w_qkv,
    w_out,
    w_up,
    w_down,
    gain_one,
    bias_one,
    gain_two,
    bias_two,
    lengths,
    slot_order,
):
    micro_count, tok_dev, width = tokens.shape
    rows = micro_count * tok_dev
    scale = (width // HEADS) ** (-0.5)
    bf16, f32 = jnp.bfloat16, jnp.float32
    part = w_qkv.shape[0]
    my_slot = lax.axis_index("seq")

    downs = [w_down[i * part : (i + 1) * part] for i in range(4)]
    norms = jnp.stack([gain_one, bias_one, gain_two, bias_two], 1)
    rem = jnp.concatenate(
        [w_up[:, 512:], w_qkv[:, 384:], w_out[:, 128:]]
        + [down[:, 128:] for down in downs]
        + [norms, jnp.zeros((part, 28), bf16)],
        1,
    )
    gathered = gather_weights(
        [
            w_qkv[:, :384],
            jnp.concatenate([w_out[:, :128], rem, w_up[:, :128]], 1),
            w_up[:, 128:512],
            jnp.concatenate([down[:, :128] for down in downs], 1),
        ]
    )
    full_qkv, full_out, full_up, full_down, full_norms = unpack_weights(gathered)
    full_qkv = full_qkv.reshape(width, -1)
    full_out = full_out.reshape(width, width)
    full_up = full_up.reshape(width, -1)
    full_down = full_down.reshape(-1, width)
    norm_rows = full_norms[:, :, REM_NORM : REM_NORM + 4].reshape(width, 4).T.astype(f32)
    g_one, b_one, g_two, b_two = norm_rows[0], norm_rows[1], norm_rows[2], norm_rows[3]

    unit_ids = my_slot * UNITS + jnp.arange(UNITS, dtype=jnp.int32)
    second = (unit_ids >= HEADS)[:, None]
    doc_ends = jax.vmap(running_total)(lengths[:, 0])
    places = jnp.arange(8 * tok_dev, dtype=jnp.int32)
    segments = jax.vmap(segment_of, (None, 0))(places, doc_ends)
    unit_segments = jnp.where(second, segments[1][None], segments[0][None])
    seg_k, seg_q = unit_segments[:, :, None], unit_segments[:, None, :]
    slots = jnp.arange(8, dtype=jnp.int32)
    holders = jnp.sum(
        jnp.where(slot_order[:, 0][:, None, :] == slots[None, :, None], slots[None, None, :], 0), 2
    )
    order = jnp.where(second, holders[1][None], holders[0][None])

    residual = tokens.astype(f32).reshape(rows, width)
    scaled_one, inv_one = normalize(residual)
    normed_one = (scaled_one * g_one + b_one).astype(bf16)
    qkv_t = lax.dot_general(
        full_qkv, normed_one, (((0,), (1,)), ((), ())), preferred_element_type=f32
    ).astype(bf16)
    unit_qkv = exchange(to_units(qkv_t, micro_count, 3), 0)
    unit_out, lse = attend(unit_qkv, order, seg_k, seg_q, scale)
    attn_flat = from_units(exchange(unit_out, 1), micro_count, 1)
    middle = residual + dot(attn_flat, full_out)
    scaled_two, inv_two = normalize(middle)
    normed_two = (scaled_two * g_two + b_two).astype(bf16)
    hidden = dot(normed_two, full_up)
    activated_full, gelu_back = jax.vjp(gelu_tanh, hidden)
    activated = activated_full.astype(bf16)

    grad_rows = cotangent.reshape(rows, width)
    block_out = (middle + dot(activated, full_down)).astype(bf16)
    grad_hidden = gelu_back(dot_right_t(grad_rows, full_down))[0].astype(bf16)
    sum_down = outer(activated, grad_rows)
    sum_up = dot_left_t(normed_two, grad_hidden).astype(bf16)
    grad_normed_two = dot_right_t(grad_hidden, full_up)
    grad_middle = grad_rows.astype(f32) + norm_back(grad_normed_two, scaled_two, inv_two, g_two)
    grad_branch = grad_middle.astype(bf16)
    sum_proj = dot_left_t(attn_flat, grad_branch).astype(bf16)
    grad_heads_t = dot_right_t(full_out, grad_branch).astype(bf16)
    unit_grad = exchange(to_units(grad_heads_t, micro_count, 1), 2)
    unit_back = attend_back(unit_qkv, unit_grad, order, seg_k, seg_q, lse, scale)
    grad_qkv_rows = from_units(exchange(unit_back, 3), micro_count, 3)
    sum_qkv = dot_left_t(normed_one, grad_qkv_rows).astype(bf16)
    grad_normed_one = dot_right_t(grad_qkv_rows, full_qkv)
    grad_input = (
        grad_middle + norm_back(grad_normed_one, scaled_one, inv_one, g_one)
    ).astype(bf16)

    norm_sums = jnp.stack(
        [
            jnp.sum(grad_normed_one * scaled_one, 0),
            jnp.sum(grad_normed_one, 0),
            jnp.sum(grad_normed_two * scaled_two, 0),
            jnp.sum(grad_normed_two, 0),
        ]
    )
    norm_cols = jnp.pad(norm_sums.T.astype(bf16), ((0, 0), (REM_NORM, 28)))
    sum0, sum1, sum2, sum3 = (
        total.astype(f32)
        for total in scatter_grads(
            pack_grads(
                sum_qkv.reshape(4, part, -1),
                sum_proj.reshape(4, part, -1),
                sum_up.reshape(4, part, -1),
                sum_down.reshape(16, part, -1),
                norm_cols.reshape(4, part, -1),
            )
        )
    )
    rest = sum1[:, TILE : 2 * TILE]
    out_qkv = jnp.concatenate([sum0, rest[:, REM_QKV : REM_QKV + 24]], 1)
    out_proj = jnp.concatenate([sum1[:, :TILE], rest[:, REM_OUT : REM_OUT + 8]], 1)
    out_up = jnp.concatenate([sum1[:, 2 * TILE :], sum2, rest[:, REM_UP : REM_UP + 32]], 1)
    out_down = jnp.concatenate(
        [
            jnp.concatenate(
                [
                    sum3[:, i * TILE : (i + 1) * TILE],
                    rest[:, REM_DOWN + 8 * i : REM_DOWN + 8 * i + 8],
                ],
                1,
            )
            for i in range(4)
        ],
        0,
    )
    norm_mine = rest[:, REM_NORM : REM_NORM + 4].T
    return (
        block_out.reshape(tokens.shape),
        grad_input.reshape(tokens.shape),
        out_qkv,
        out_proj,
        out_up,
        out_down,
        norm_mine[0],
        norm_mine[1],
        norm_mine[2],
        norm_mine[3],
    )


def solution(mesh):
    grid = (mesh.shape["dp"], mesh.shape["seq"])
    return jax.shard_map(
        shards_fast if grid == (4, 8) else shards_plain,
        mesh=mesh,
        in_specs=(
            P(None, ("dp", "seq"), None),
            P(None, ("dp", "seq"), None),
            P("dp", "seq"),
            P("dp", "seq"),
            P("dp", "seq"),
            P("dp", "seq"),
            P("dp"),
            P("dp"),
            P("dp"),
            P("dp"),
            P(None, "dp", None),
            P(None, "dp", None),
        ),
        out_specs=(
            P(None, ("dp", "seq"), None),
            P(None, ("dp", "seq"), None),
            P("dp", "seq"),
            P("dp", "seq"),
            P("dp", "seq"),
            P("dp", "seq"),
            P("dp"),
            P("dp"),
            P("dp"),
            P("dp"),
        ),
        check_vma=False,
    )
```
